32 devices in a mesh: dp: 8 (over z, core), fsdp: 4 (over y, x).
Axes of the slice: x: 2, y: 2, z: 4, core: 2. Of those that a mesh axis runs over, the one named last changes fastest.
Arguments:
- layer_input: bfloat16 [8192, 2048], P(('dp', 'fsdp')), may hold values from -6 to 6
- first_gain: bfloat16 [2048], P(('dp', 'fsdp')), may hold values from 0.099609375 to 1.8984375
- first_shift: bfloat16 [2048], P(('dp', 'fsdp')), may hold values from -1.75 to 1.75
- query_weight: bfloat16 [2048, 2048], P(('dp', 'fsdp')), may hold values from -0.125 to 0.125
- key_weight: bfloat16 [2048, 2048], P(('dp', 'fsdp')), may hold values from -0.125 to 0.125
- value_weight: bfloat16 [2048, 2048], P(('dp', 'fsdp')), may hold values from -0.125 to 0.125
- output_weight: bfloat16 [2048, 2048], P(('dp', 'fsdp')), may hold values from -1.5 to 1.5
- query_bias: bfloat16 [2048], P(('dp', 'fsdp')), may hold values from -1.75 to 1.75
- value_bias: bfloat16 [2048], P(('dp', 'fsdp')), may hold values from -0.3125 to 0.3125
- output_bias: bfloat16 [2048], P(('dp', 'fsdp')), may hold values from -1.75 to 1.75
- second_gain: bfloat16 [2048], P(('dp', 'fsdp')), may hold values from 0.099609375 to 1.8984375
- second_shift: bfloat16 [2048], P(('dp', 'fsdp')), may hold values from -1.75 to 1.75
- up_weight: bfloat16 [2048, 8192], P(('dp', 'fsdp')), may hold values from -0.125 to 0.125
- up_bias: bfloat16 [8192], P(('dp', 'fsdp')), may hold values from -3 to 3
- down_weight: bfloat16 [8192, 2048], P(('dp', 'fsdp')), may hold values from -0.0625 to 0.0625
- down_bias: bfloat16 [2048], P(('dp', 'fsdp')), may hold values from -1.75 to 1.75
- segment_counts: int32 [2], replicated, may hold values from 1 to 4, as said below
- out_grad: bfloat16 [8192, 2048], P(('dp', 'fsdp')), may hold values from -6 to 6
Outputs:
- layer_output: bfloat16 [8192, 2048], P(('dp', 'fsdp'))
- input_grad: float32 [8192, 2048], P(('dp', 'fsdp'))
- grad_first_gain: float32 [2048], P(('dp', 'fsdp'))
- grad_first_shift: float32 [2048], P(('dp', 'fsdp'))
- grad_query_weight: float32 [2048, 2048], P(('dp', 'fsdp'))
- grad_key_weight: float32 [2048, 2048], P(('dp', 'fsdp'))
- grad_value_weight: float32 [2048, 2048], P(('dp', 'fsdp'))
- grad_output_weight: float32 [2048, 2048], P(('dp', 'fsdp'))
- grad_query_bias: float32 [2048], P(('dp', 'fsdp'))
- grad_value_bias: float32 [2048], P(('dp', 'fsdp'))
- grad_output_bias: float32 [2048], P(('dp', 'fsdp'))
- grad_second_gain: float32 [2048], P(('dp', 'fsdp'))
- grad_second_shift: float32 [2048], P(('dp', 'fsdp'))
- grad_up_weight: float32 [2048, 8192], P(('dp', 'fsdp'))
- grad_up_bias: float32 [8192], P(('dp', 'fsdp'))
- grad_down_weight: float32 [8192, 2048], P(('dp', 'fsdp'))
- grad_down_bias: float32 [2048], P(('dp', 'fsdp'))
The draws below stay inside these ranges and needn't reach their ends.
Inputs may be any that keep to these rules, and one draw needn't show every extreme that they name: `segment_counts`: every document has 1 to 4 segments; in every draw some document has 4.
All inputs are finite; a program needn't handle non-finite values.
Results may differ from the reference program's by a relative error of at most 0.02.
Values may be sent and summed in bfloat16 or wider, within the bound.
A program may use at most 384 MiB of HBM per device.

```python
from functools import partial
import jax
import jax.numpy as jnp
from jax import lax

D = 2048
HEADS = 32
HEAD = 64
FF = 8192
SUMM = 50
PREV = 3
MAXSEG = 4
TOK_DEV = 256
SEG = 1024
PRE = 150
SEGS = 8
DOCS = 2
TOKENS = 8192
N_FSDP = 4


def draw_segment_counts(key, part):
    key_counts, key_order = jax.random.split(jax.random.fold_in(key, 7))
    doc_counts = jax.random.randint(key_counts, (DOCS,), 1, MAXSEG + 1)
    fullest = jax.random.randint(key_order, (), 0, DOCS)
    doc_counts = doc_counts.at[fullest].set(MAXSEG)
    return doc_counts.astype(jnp.int32)


def with_spikes(array, key, source, target, parts, factor):
    owner, partner = [(jnp.arange(array.shape[axis_at]) // (array.shape[axis_at] // parts)).reshape([-1 if axis == axis_at else 1 for axis in range(array.ndim)]) for axis_at in (source, target)]
    chosen = jax.random.permutation(key, parts)[partner]
    strong = (owner == chosen) | (owner == (partner + parts // 2) % parts)
    return jnp.where(strong, factor * array, array)


def levels(key, shape, shards, least, largest):
    level, own = 1.0, jax.random.fold_in(key, 6)
    for dim, blocks in shards:
        draws = jnp.exp(jax.random.uniform(jax.random.fold_in(own, dim), (blocks,), jnp.float32, least / len(shards), largest / len(shards)))
        level = level * jnp.repeat(draws, shape[dim] // blocks).reshape([-1 if axis == dim else 1 for axis in range(len(shape))])
    return level


def bell_draw(stream_key, shape, deviation, bound, cuts=(), kind=jnp.bfloat16):
    array = deviation * jax.random.normal(stream_key, shape, jnp.float32)
    if cuts:
        array = array * levels(stream_key, shape, cuts, -0.22, 0.18)
    return jnp.clip(array, -bound, bound).astype(kind)


def noise_with(key, shape, spread, reach, cuts, heavy, held_as=jnp.bfloat16):
    drawn = spread * jax.random.normal(key, shape, jnp.float32)
    if cuts:
        drawn = drawn * levels(key, shape, cuts, -0.22, 0.18)
    return jnp.clip(with_spikes(drawn, jax.random.fold_in(key, 3), *heavy), -reach, reach).astype(held_as)


def setup_inputs(seed: int = 0) -> dict:
    key_list = jax.random.split(jax.random.key(seed), 19)
    layer_input = bell_draw(key_list[0], (TOKENS, D), 1.0, 6.0, ((0, 32),))
    first_gain = jnp.clip(1.0 + 0.18 * jax.random.normal(key_list[1], (D,), jnp.float32), 0.099609375, 1.8984375).astype(jnp.bfloat16)
    first_shift = bell_draw(key_list[2], (D,), 0.3, 1.75, ((0, 32),))
    query_weight = bell_draw(key_list[3], (D, D), D ** -0.5, 0.125, ((0, 32),))
    key_weight = bell_draw(key_list[4], (D, D), D ** -0.5, 0.125, ((0, 32),))
    value_weight = bell_draw(key_list[5], (D, D), D ** -0.5, 0.125, ((0, 32),))
    output_weight = bell_draw(key_list[6], (D, D), (max(1, 8 * D // (TOK_DEV * N_FSDP))) ** -0.5, 1.5, ((0, 32),))
    query_bias = bell_draw(key_list[7], (D,), 0.3, 1.75, ((0, 32),))
    value_bias = bell_draw(key_list[8], (D,), 0.05, 0.3125, ((0, 32),))
    output_bias = bell_draw(key_list[9], (D,), 0.3, 1.75, ((0, 32),))
    second_gain = jnp.clip(1.0 + 0.18 * jax.random.normal(key_list[10], (D,), jnp.float32), 0.099609375, 1.8984375).astype(jnp.bfloat16)
    second_shift = bell_draw(key_list[11], (D,), 0.3, 1.75, ((0, 32),))
    up_weight = bell_draw(key_list[12], (D, FF), D ** -0.5, 0.125, ((0, 32),))
    up_bias = bell_draw(key_list[13], (FF,), 0.5, 3.0, ((0, 32),))
    down_weight = bell_draw(key_list[14], (FF, D), FF ** -0.5, 0.0625, ((0, 32),))
    down_bias = bell_draw(key_list[15], (D,), 0.3, 1.75, ((0, 32),))
    segment_counts = draw_segment_counts(jax.random.fold_in(key_list[18], 71), 0)
    out_grad = noise_with(key_list[17], (TOKENS, D), 1.0, 6.0, ((0, 32),), (0, 1, 32, 2.75))
    return dict(layer_input=layer_input, first_gain=first_gain, first_shift=first_shift, query_weight=query_weight, key_weight=key_weight, value_weight=value_weight, output_weight=output_weight, query_bias=query_bias, value_bias=value_bias, output_bias=output_bias, second_gain=second_gain, second_shift=second_shift, up_weight=up_weight, up_bias=up_bias, down_weight=down_weight, down_bias=down_bias, segment_counts=segment_counts, out_grad=out_grad)


highest = lax.Precision.HIGHEST
epsilon = 1e-05
masked = -1e+30

@jax.custom_vjp
def low(v):
    return lax.optimization_barrier(v.astype(jnp.bfloat16)).astype(jnp.float32)

@jax.custom_vjp
def low_back(v):
    return v

def low_keep(v):
    return (low(v), None)

def low_pass(kept, grad):
    return (grad,)

def back_keep(v):
    return (v, None)

def back_low(kept, grad):
    return (low(grad),)
low.defvjp(low_keep, low_pass)
low_back.defvjp(back_keep, back_low)

def matmul(left_side, right_side):
    return jnp.dot(left_side, right_side, precision=highest, preferred_element_type=jnp.float32)

def round_both(value):
    return low(low_back(value))

def gelu_exact(value):
    return value * 0.5 * (1.0 + jax.scipy.special.erf(value * 0.7071067811865476))

def normalize(values, norm_gain, norm_shift):
    center = values - lax.optimization_barrier(jnp.mean(values, axis=-1, keepdims=True))
    inverse_std = lax.rsqrt(lax.optimization_barrier(jnp.mean(center * center, axis=-1, keepdims=True)) + epsilon)
    return center * inverse_std * norm_gain + norm_shift

def live_rows(segment_counts):
    segment = jnp.arange(SEGS, dtype=jnp.int32)
    place_in_doc = segment % MAXSEG
    present = place_in_doc < segment_counts[segment // MAXSEG]
    position = jnp.arange(SEG, dtype=jnp.int32)
    slot_live = (position >= PRE)[None, :] | (place_in_doc[:, None] >= (PREV - position // SUMM)[None, :])
    return present[:, None] & slot_live

def head_attention(inputs, key_live):
    query_head, key_head, value_head = inputs
    scores = matmul(query_head, key_head.T) * HEAD ** (-0.5)
    position = jnp.arange(SEG, dtype=jnp.int32)
    same_row = position[None, :] == position[:, None]
    allowed = (position[None, :] <= position[:, None]) & (key_live[None, :] | same_row)
    scores = low_back(jnp.where(allowed, scores, masked))
    probabilities = jax.nn.softmax(scores, axis=-1)
    return matmul(low(probabilities), value_head)

def split_heads(value):
    return value.reshape(SEG, HEADS, HEAD).transpose(1, 0, 2)

def segment_layer(segment_rows, key_live, weights):
    first_gain, first_shift, query_weight, key_weight, value_weight, output_weight, query_bias, value_bias, output_bias, second_gain, second_shift, up_weight, up_bias, down_weight, down_bias = weights
    normed = low(normalize(segment_rows, first_gain, first_shift))
    query_rows = round_both(matmul(normed, query_weight) + query_bias)
    key_rows = round_both(matmul(normed, key_weight))
    value_rows = round_both(matmul(normed, value_weight) + value_bias)
    attend = jax.checkpoint(partial(head_attention, key_live=key_live))
    mixed_heads = lax.map(attend, (split_heads(query_rows), split_heads(key_rows), split_heads(value_rows)))
    mixed_rows = round_both(mixed_heads.transpose(1, 0, 2).reshape(SEG, D))
    after_attention = segment_rows + low_back(matmul(mixed_rows, output_weight) + output_bias)
    second_normed = low(normalize(after_attention, second_gain, second_shift))
    pre_act = low_back(matmul(second_normed, up_weight) + up_bias)
    activated = low(gelu_exact(pre_act))
    return after_attention + low_back(matmul(activated, down_weight) + down_bias)

def forward(layer_rows, weights, live_mask):

    def visit_segment(state_carry, segment_item):
        segment_rows, key_live = segment_item
        return (state_carry, jax.checkpoint(segment_layer)(segment_rows, key_live, weights))
    _, results = lax.scan(visit_segment, jnp.zeros((), jnp.float32), (layer_rows.reshape(SEGS, SEG, D), live_mask))
    return results.reshape(TOKENS, D)

def reference(layer_input, first_gain, first_shift, query_weight, key_weight, value_weight, output_weight, query_bias, value_bias, output_bias, second_gain, second_shift, up_weight, up_bias, down_weight, down_bias, segment_counts, out_grad):
    weights = tuple((tensor.astype(jnp.float32) for tensor in (first_gain, first_shift, query_weight, key_weight, value_weight, output_weight, query_bias, value_bias, output_bias, second_gain, second_shift, up_weight, up_bias, down_weight, down_bias)))
    live_mask = live_rows(segment_counts)
    layer_rows = layer_input.astype(jnp.float32)
    outputs, pullback = jax.vjp(lambda row_values, params: forward(row_values, params, live_mask), layer_rows, weights)
    row_live = live_mask.reshape(TOKENS).astype(jnp.float32)
    cotangent = out_grad.astype(jnp.float32) * row_live[:, None]
    input_grad, grads = pullback(cotangent)
    keep_rows = (jnp.arange(TOKENS, dtype=jnp.int32) % SEG >= SUMM).astype(jnp.float32)
    input_grad = input_grad * keep_rows[:, None]
    grad_first_gain, grad_first_shift, grad_query_weight, grad_key_weight, grad_value_weight, grad_output_weight, grad_query_bias, grad_value_bias, grad_output_bias, grad_second_gain, grad_second_shift, grad_up_weight, grad_up_bias, grad_down_weight, grad_down_bias = grads
    return (outputs.astype(jnp.bfloat16), input_grad, grad_first_gain, grad_first_shift, grad_query_weight, grad_key_weight, grad_value_weight, grad_output_weight, grad_query_bias, grad_value_bias, grad_output_bias, grad_second_gain, grad_second_shift, grad_up_weight, grad_up_bias, grad_down_weight, grad_down_bias)
```

```python
import jax
import jax.numpy as jnp
from jax import lax
from jax.sharding import Mesh, PartitionSpec as P

HEADS = 32
HEAD = 64
SUMM = 50
PREV = 3
MAXSEG = 4
PRE = 150

epsilon = 1e-05
masked = -1e30

ALL = ("z", "core", "fsdp")
PLANE = ("core", "fsdp")
bf16 = jnp.bfloat16
f32 = jnp.float32


def dot(a, b, ca, cb):
    return lax.dot_general(a, b, (((ca,), (cb,)), ((), ())), preferred_element_type=f32)


def plane_gather(rows):
    return lax.all_gather(rows, PLANE, axis=0, tiled=True)


def plane_sum(partial):
    return lax.psum_scatter(partial.astype(bf16), PLANE, scatter_dimension=0, tiled=True).astype(f32)


def z_gather(rows):
    return lax.all_gather(rows, "z", axis=0, tiled=True)


def z_sum(partial):
    return lax.psum_scatter(partial.astype(bf16), "z", scatter_dimension=0, tiled=True)


def plane_exchange(blocks):
    return lax.all_to_all(blocks, PLANE, 0, 0, tiled=True)


def gauss_cdf(value):
    return 0.5 * (1.0 + lax.erf(value * 0.7071067811865476))


def gelu_slope(value, cdf_value):
    return cdf_value + value * jnp.exp(-0.5 * value * value) * 0.3989422804014327


def unit_norm(values):
    center = values - jnp.mean(values, axis=-1, keepdims=True)
    inverse_std = lax.rsqrt(jnp.mean(center * center, axis=-1, keepdims=True) + epsilon)
    return center * inverse_std, inverse_std


def normalize_back(grad_rows, unit_rows, inverse_std, norm_gain):
    scaled = grad_rows * norm_gain
    centered = scaled - jnp.mean(scaled, axis=-1, keepdims=True)
    centered = centered - unit_rows * jnp.mean(scaled * unit_rows, axis=-1, keepdims=True)
    return (
        centered * inverse_std,
        jnp.sum(grad_rows * unit_rows, axis=0),
        jnp.sum(grad_rows, axis=0),
    )


def attend(q, k, v, live):
    rows = q.shape[1]
    pos = jnp.arange(rows, dtype=jnp.int32)
    scores = jnp.einsum("sqhd,skhd->shqk", q, k, preferred_element_type=f32) * HEAD**-0.5
    diagonal = pos[None, :] == pos[:, None]
    allowed = (pos[None, :] <= pos[:, None]) & (live[:, None, :] | diagonal)
    scores = jnp.where(allowed[:, None], scores, masked)
    top = jnp.max(scores, axis=-1, keepdims=True)
    powers = jnp.exp(scores - top)
    probs = powers / jnp.sum(powers, axis=-1, keepdims=True)
    mixed = jnp.einsum("shqk,skhd->sqhd", probs.astype(bf16), v, preferred_element_type=f32)
    return probs, mixed


def attend_back(q, k, v, probs, mixed, grad):
    delta = jnp.sum(grad.astype(f32) * mixed, axis=-1).transpose(0, 2, 1)
    grad_probs = jnp.einsum("sqhd,skhd->shqk", grad, v, preferred_element_type=f32)
    grad_scores = (probs * (grad_probs - delta[..., None])).astype(bf16)
    grad_q = jnp.einsum("shqk,skhd->sqhd", grad_scores, k, preferred_element_type=f32)
    grad_k = jnp.einsum("shqk,sqhd->skhd", grad_scores, q, preferred_element_type=f32)
    grad_v = jnp.einsum("shqk,sqhd->skhd", probs.astype(bf16), grad, preferred_element_type=f32)
    scale = HEAD**-0.5
    return (grad_q * scale).astype(bf16), (grad_k * scale).astype(bf16), grad_v.astype(bf16)


def body(
    layer_input,
    first_gain,
    first_shift,
    query_weight,
    key_weight,
    value_weight,
    output_weight,
    query_bias,
    value_bias,
    output_bias,
    second_gain,
    second_shift,
    up_weight,
    up_bias,
    down_weight,
    down_bias,
    segment_counts,
    out_grad,
):
    here, width = layer_input.shape
    wide = up_weight.shape[1]
    planes = lax.axis_size("z")
    group = lax.axis_size("fsdp")
    team = 2 * group
    z_at, core_at, inner_at = (lax.axis_index(name) for name in ALL)
    plane_at = core_at * group + inner_at
    seg_rows = here * group
    own_rows = query_weight.shape[0]
    own_wide = down_weight.shape[0]
    cols = width // team
    heads_here = cols // HEAD
    whole_heads = own_rows % HEAD == 0

    def to_columns(weight, unit):
        cut = weight.reshape(weight.shape[0], planes, team, unit)
        return cut.transpose(2, 0, 1, 3).reshape(team, weight.shape[0], planes * unit)

    def from_columns(blocks, unit):
        rows = blocks.shape[1]
        return blocks.reshape(team, rows, planes, unit).transpose(1, 2, 0, 3).reshape(rows, planes * team * unit)

    def head_columns(weight):
        if whole_heads:
            return to_columns(weight, own_rows)
        return weight.reshape(own_rows, team, cols).transpose(1, 0, 2)

    def head_rows(blocks):
        if whole_heads:
            return from_columns(blocks, own_rows)
        return blocks.transpose(1, 0, 2).reshape(own_rows, width)

    attn_blocks = jnp.concatenate([head_columns(w) for w in (query_weight, key_weight, value_weight)], axis=2)
    attn_cols = plane_exchange(attn_blocks).reshape(team * own_rows, 3 * cols)
    up_cols = plane_exchange(to_columns(up_weight, own_wide)).reshape(team * own_rows, wide // team)
    attn_full = z_gather(attn_cols)
    small = jnp.concatenate(
        [first_gain, first_shift, query_bias, value_bias, output_bias, second_gain, second_shift, down_bias, up_bias]
    )
    small_all = lax.all_gather(small, ALL, axis=0, tiled=False).astype(f32)
    gain_one, shift_one, bias_q, bias_v, bias_o, gain_two, shift_two, bias_down = (
        small_all[:, i * own_rows : (i + 1) * own_rows].reshape(width) for i in range(8)
    )
    bias_up = small_all[:, 8 * own_rows :].reshape(planes, team, own_wide)[:, plane_at].reshape(wide // team)

    def own_columns(bias):
        if whole_heads:
            return bias.reshape(planes, team, own_rows)[:, plane_at].reshape(cols)
        return lax.dynamic_slice_in_dim(bias, plane_at * cols, cols)

    bias_q, bias_v = own_columns(bias_q), own_columns(bias_v)
    if whole_heads:
        out_full = z_gather(output_weight)
    else:
        out_full = lax.dynamic_slice_in_dim(
            lax.all_gather(output_weight, ALL, axis=0, tiled=True), plane_at * cols, cols
        )
    up_full = z_gather(up_cols)
    down_full = z_gather(down_weight)

    segment = 2 * z_at + jnp.arange(2, dtype=jnp.int32)
    place = segment % MAXSEG
    present = place < segment_counts[segment // MAXSEG]
    pos = jnp.arange(seg_rows, dtype=jnp.int32)
    live = present[:, None] & ((pos >= PRE)[None] | (place[:, None] >= PREV - pos[None] // SUMM))
    own_pos = inner_at * here + jnp.arange(here, dtype=jnp.int32)
    live_own = lax.dynamic_slice(live, (core_at, inner_at * here), (1, here))[0]

    all_rows = plane_gather(layer_input).astype(f32)
    normed_low = (unit_norm(all_rows)[0] * gain_one + shift_one).astype(bf16)
    rows_own = layer_input.astype(f32)
    unit_one, inverse_one = unit_norm(rows_own)
    heads = lambda a: a.reshape(2, seg_rows, heads_here, HEAD)
    qkv = dot(normed_low, attn_full, 1, 0)
    qkv = (qkv + jnp.concatenate([bias_q, jnp.zeros_like(bias_q), bias_v])).astype(bf16)
    q, k, v = (heads(qkv[:, i * cols : (i + 1) * cols]) for i in range(3))
    probs, mixed = attend(q, k, v, live)
    mixed_low = mixed.astype(bf16).reshape(2 * seg_rows, cols)
    after = rows_own + plane_sum(dot(mixed_low, out_full, 1, 0)) + bias_o
    unit_two, inverse_two = unit_norm(after)
    second_low = plane_gather((unit_two * gain_two + shift_two).astype(bf16))
    pre_act = dot(second_low, up_full, 1, 0) + bias_up
    cdf = gauss_cdf(pre_act)
    activated = (pre_act * cdf).astype(bf16)
    layer_output = (after + plane_sum(dot(activated, down_full, 1, 0)) + bias_down).astype(bf16)

    out_own = jnp.where(live_own[:, None], out_grad, jnp.zeros_like(out_grad))
    out_live = plane_gather(out_own)
    out_own = out_own.astype(f32)
    grad_down = z_sum(dot(activated, out_live, 0, 0)).astype(f32)
    grad_pre = (dot(out_live, down_full, 1, 1) * gelu_slope(pre_act, cdf)).astype(bf16)
    grad_up = z_sum(dot(second_low, grad_pre, 0, 0)).reshape(team, own_rows, wide // team)
    grad_up = from_columns(plane_exchange(grad_up), own_wide).astype(f32)
    grad_up_bias = jnp.sum(grad_pre.astype(f32), axis=0)
    grad_norm, grad_second_gain, grad_second_shift = normalize_back(
        plane_sum(dot(grad_pre, up_full, 1, 1)), unit_two, inverse_two, gain_two
    )
    grad_after = out_own + grad_norm
    after_low_own = grad_after.astype(bf16)
    grad_output_bias = jnp.sum(after_low_own.astype(f32), axis=0)
    after_low = plane_gather(after_low_own)
    grad_output = dot(mixed_low, after_low, 0, 0)
    if whole_heads:
        grad_output = z_sum(grad_output).astype(f32)
    else:
        spread = jnp.zeros((width, width), bf16)
        spread = lax.dynamic_update_slice_in_dim(spread, grad_output.astype(bf16), plane_at * cols, 0)
        grad_output = lax.psum_scatter(spread, ALL, scatter_dimension=0, tiled=True).astype(f32)
    grad_mixed = heads(dot(after_low, out_full, 1, 1).astype(bf16))
    grad_q, grad_k, grad_v = attend_back(q, k, v, probs, mixed, grad_mixed)
    grad_qkv = jnp.concatenate([a.reshape(2 * seg_rows, cols) for a in (grad_q, grad_k, grad_v)], axis=1)
    grad_attn = z_sum(dot(normed_low, grad_qkv, 0, 0)).reshape(team, own_rows, 3 * cols)
    grad_attn = plane_exchange(grad_attn)
    grad_weights = [head_rows(grad_attn[:, :, i * cols : (i + 1) * cols]).astype(f32) for i in range(3)]
    grad_bias = jnp.sum(grad_qkv.astype(f32), axis=0)
    grad_norm, grad_first_gain, grad_first_shift = normalize_back(
        plane_sum(dot(grad_qkv, attn_full, 1, 1)), unit_one, inverse_one, gain_one
    )
    input_grad = jnp.where((own_pos >= SUMM)[:, None], grad_after + grad_norm, 0.0)

    def spread_columns(bias):
        if whole_heads:
            full = jnp.zeros((planes, team, own_rows), f32)
            return lax.dynamic_update_slice(full, bias.reshape(planes, 1, own_rows), (0, plane_at, 0)).reshape(width)
        return lax.dynamic_update_slice(jnp.zeros((width,), f32), bias, (plane_at * cols,))

    sums = [
        grad_first_gain,
        grad_first_shift,
        spread_columns(grad_bias[:cols]),
        spread_columns(grad_bias[2 * cols :]),
        grad_output_bias,
        grad_second_gain,
        grad_second_shift,
        jnp.sum(out_own, axis=0),
    ]
    up_spread = jnp.zeros((planes, team, own_wide), f32)
    up_spread = lax.dynamic_update_slice(up_spread, grad_up_bias.reshape(planes, 1, own_wide), (0, plane_at, 0))
    packed = jnp.concatenate(
        [a.reshape(planes * team, own_rows) for a in sums] + [up_spread.reshape(planes * team, own_wide)], axis=1
    )
    packed = lax.psum_scatter(packed, ALL, scatter_dimension=0, tiled=False)
    small_grads = [packed[i * own_rows : (i + 1) * own_rows] for i in range(8)]
    return (
        layer_output,
        input_grad,
        small_grads[0],
        small_grads[1],
        *grad_weights,
        grad_output,
        small_grads[2],
        small_grads[3],
        small_grads[4],
        small_grads[5],
        small_grads[6],
        grad_up,
        packed[8 * own_rows :],
        grad_down,
        small_grads[7],
    )


def solution(mesh):
    outer, inner = mesh.devices.shape
    fine = Mesh(mesh.devices.reshape(outer // 2, 2, inner), ALL)
    rows, vector = P(ALL, None), P(ALL)
    return jax.shard_map(
        body,
        mesh=fine,
        in_specs=(
            rows, vector, vector, rows, rows, rows, rows, vector, vector, vector, vector, vector,
            rows, vector, rows, vector, P(), rows,
        ),
        out_specs=(
            rows, rows, vector, vector, rows, rows, rows, rows, vector, vector, vector, vector, vector,
            rows, vector, rows, vector,
        ),
        check_vma=False,
    )
```

```python
import functools

import jax
import jax.numpy as jnp
from jax import lax
from jax.experimental import pallas as pl
from jax.experimental.pallas import tpu as pltpu
from jax.sharding import Mesh, PartitionSpec as P

HEADS = 32
HEAD = 64
SUMM = 50
PREV = 3
MAXSEG = 4
PRE = 150

epsilon = 1e-05
masked = -1e30

ALL = ("z", "core", "fsdp")
PLANE = ("core", "fsdp")
bf16 = jnp.bfloat16
f32 = jnp.float32
MESH = pl.DeviceIdType.MESH


def dot(a, b, ca, cb):
    return lax.dot_general(a, b, (((ca,), (cb,)), ((), ())), preferred_element_type=f32)


def z_gather(rows):
    return lax.all_gather(rows, "z", axis=0, tiled=True)


def z_sum(partial):
    return lax.psum_scatter(partial.astype(bf16), "z", scatter_dimension=0, tiled=True)


def after(value, *earlier):
    return lax.optimization_barrier((value, *earlier))[0]


def gauss_cdf(value):
    return 0.5 * (1.0 + lax.erf(value * 0.7071067811865476))


def gelu_slope(value, cdf_value):
    return cdf_value + value * jnp.exp(-0.5 * value * value) * 0.3989422804014327


def unit_norm(values):
    center = values - jnp.mean(values, axis=-1, keepdims=True)
    inverse_std = lax.rsqrt(jnp.mean(center * center, axis=-1, keepdims=True) + epsilon)
    return center * inverse_std, inverse_std


def normalize_back(grad_rows, unit_rows, inverse_std, norm_gain):
    scaled = grad_rows * norm_gain
    centered = scaled - jnp.mean(scaled, axis=-1, keepdims=True)
    centered = centered - unit_rows * jnp.mean(scaled * unit_rows, axis=-1, keepdims=True)
    return (
        centered * inverse_std,
        jnp.sum(grad_rows * unit_rows, axis=0),
        jnp.sum(grad_rows, axis=0),
    )


def head_mask(rows, cols, head):
    lane = lax.broadcasted_iota(jnp.int32, (rows, cols), 1)
    return lane // HEAD == head


def attend_segment(block, heads, seg_rows, seg, qkv_ref, live_ref, mixed_ref, total_ref, bias_ref):
    cols = heads * HEAD
    base = seg * seg_rows
    lane = lax.broadcasted_iota(jnp.int32, (block, 128), 1)
    for at in range(seg_rows // block):
        wide = (at + 1) * block
        rows = pl.ds(pl.multiple_of(base + at * block, block), block)
        keys = pl.ds(pl.multiple_of(base, seg_rows), wide)
        query_pos = at * block + lax.broadcasted_iota(jnp.int32, (block, wide), 0)
        key_pos = lax.broadcasted_iota(jnp.int32, (block, wide), 1)
        open_key = (live_ref[seg, :, :wide] > 0.0) & (key_pos < query_pos) | (key_pos == query_pos)
        bias_ref[:, :wide] = jnp.where(open_key, 0.0, masked)
        query = qkv_ref[rows, :cols] * jnp.asarray(HEAD**-0.5, bf16)
        result = jnp.zeros((block, cols), f32)
        totals = jnp.zeros((block, 128), f32)
        for head in range(heads):
            chosen = head_mask(block, cols, head)
            scores = dot(jnp.where(chosen, query, jnp.zeros_like(query)), qkv_ref[keys, cols : 2 * cols], 1, 1)
            scores = scores + bias_ref[:, :wide]
            top = jnp.max(scores, axis=1, keepdims=True)
            powers = jnp.exp(scores - top)
            total = jnp.sum(powers, axis=1, keepdims=True)
            probs = (powers * (1.0 / total)).astype(bf16)
            value = dot(probs, qkv_ref[keys, 2 * cols :], 1, 0)
            result = jnp.where(chosen, value, result)
            totals = jnp.where(lane == head, top + jnp.log(total), totals)
        mixed_ref[rows, :] = result.astype(bf16)
        total_ref[seg, :, at * block : (at + 1) * block] = totals.T[:8]


def attend_back_rows(
    block, heads, seg_rows, seg, at, qkv_ref, grad_ref, live_ref, total_ref, out_ref, bias_ref, sums_ref
):
    cols = heads * HEAD
    base = seg * seg_rows
    wide = (at + 1) * block
    rows = pl.ds(pl.multiple_of(base + at * block, block), block)
    keys = pl.ds(pl.multiple_of(base, seg_rows), wide)
    key_pos = lax.broadcasted_iota(jnp.int32, (wide, block), 0)
    query_pos = at * block + lax.broadcasted_iota(jnp.int32, (wide, block), 1)
    open_key = (live_ref[keys, :] > 0.0) & (key_pos < query_pos) | (key_pos == query_pos)
    bias_ref[:wide, :] = jnp.where(open_key, 0.0, masked)
    query = qkv_ref[rows, :cols] * jnp.asarray(HEAD**-0.5, bf16)
    grad = grad_ref[rows, :]
    grad_query = jnp.zeros((block, cols), f32)
    for head in range(heads):
        chosen = head_mask(block, cols, head)
        query_one = jnp.where(chosen, query, jnp.zeros_like(query))
        grad_one = jnp.where(chosen, grad, jnp.zeros_like(grad))
        scores = dot(qkv_ref[keys, cols : 2 * cols], query_one, 1, 1)
        total = total_ref[seg, head : head + 1, at * block : (at + 1) * block]
        probs = jnp.exp(scores + bias_ref[:wide, :] - total)
        terms = probs * dot(qkv_ref[keys, 2 * cols :], grad_one, 1, 1)
        delta = jnp.sum(terms, axis=0, keepdims=True)
        grad_scores = (terms - probs * delta).astype(bf16)
        sums_ref[:wide, :cols] += dot(grad_scores, query_one, 1, 0)
        sums_ref[:wide, cols:] += dot(probs.astype(bf16), grad_one, 1, 0)
        value = dot(grad_scores, qkv_ref[keys, cols : 2 * cols], 0, 0)
        grad_query = jnp.where(chosen, value, grad_query)
    out_ref[rows, :cols] = (grad_query * HEAD**-0.5).astype(bf16)


def greet(core_at, inner_at, group):
    barrier = pltpu.get_barrier_semaphore()
    pl.semaphore_signal(barrier, inc=1, device_id={"core": 1 - core_at, "fsdp": inner_at}, device_id_type=MESH)
    for step in range(1, group):
        pl.semaphore_signal(
            barrier,
            inc=1,
            device_id={"core": core_at, "fsdp": lax.rem(inner_at + step, group)},
            device_id_type=MESH,
        )
    pl.semaphore_wait(barrier, group)


def send(source, target, send_sem, recv_sem, core, inner):
    return pltpu.make_async_remote_copy(
        src_ref=source,
        dst_ref=target,
        send_sem=send_sem,
        recv_sem=recv_sem,
        device_id={"core": core, "fsdp": inner},
        device_id_type=MESH,
    )


def beside(inner_at):
    at_x = inner_at + 1 - 2 * lax.rem(inner_at, 2)
    at_y = lax.rem(inner_at + 2, 4)
    return at_x, at_y, lax.rem(at_x + 2, 4)


class PlaneGather:

    @staticmethod
    def scratch(group):
        return [pltpu.SemaphoreType.DMA((2, 2 * group)), pltpu.SemaphoreType.DMA((2, 2 * group)), pltpu.SemaphoreType.DMA]

    def __init__(self, group, source, target, chip_sems, core_sems, own_sem):
        self.group, self.source, self.target = group, source, target
        self.chip_sems, self.core_sems = chip_sems, core_sems
        self.core, self.inner = lax.axis_index("core"), lax.axis_index("fsdp")
        self.mine = self.core * group + self.inner
        self.own = pltpu.make_async_copy(source, target.at[self.mine], own_sem)
        half = source.shape[0] // 2
        self.low, self.high = pl.ds(0, half), pl.ds(half, half)
        self.sent = []

    def to_chip(self, at, source, target, inner):
        return send(source, target, self.chip_sems.at[0, at], self.chip_sems.at[1, at], self.core, inner)

    def to_core(self, at, source, target):
        return send(source, target, self.core_sems.at[0, at], self.core_sems.at[1, at], 1 - self.core, self.inner)

    def block(self, core, inner, part=None):
        at = core * self.group + inner
        return self.target.at[at] if part is None else self.target.at[at, part]

    def go(self, copy):
        copy.start()
        self.sent.append(copy)

    def start(self):
        own = self.target.at[self.mine]
        if self.group == 4:
            at_x, at_y, _ = beside(self.inner)
            self.go(self.to_chip(0, self.source, own, at_x))
            self.go(self.to_chip(1, self.source, own, at_y))
        else:
            for step in range(1, self.group):
                self.go(self.to_chip(step, self.source, own, lax.rem(self.inner + step, self.group)))
        self.go(self.to_core(0, self.source, own))
        self.own.start()

    def relay(self):
        if self.group == 4:
            at_x, at_y, _ = beside(self.inner)
            block = self.block(self.core, at_x)
            self.to_chip(0, block, block, at_x).wait_recv()
            part = self.block(self.core, at_x, self.low)
            self.go(self.to_chip(2, part, part, at_y))
            self.go(self.to_core(1, block, block))
            block = self.block(self.core, at_y)
            self.to_chip(1, block, block, at_y).wait_recv()
            part = self.block(self.core, at_y, self.high)
            self.go(self.to_chip(3, part, part, at_x))
            self.go(self.to_core(2, block, block))
        else:
            for step in range(1, self.group):
                inner = lax.rem(self.inner - step + self.group, self.group)
                block = self.block(self.core, inner)
                self.to_chip(step, block, block, inner).wait_recv()
                self.go(self.to_core(step, block, block))

    def finish(self):
        other = 1 - self.core
        if self.group == 4:
            at_x, at_y, across = beside(self.inner)
            for at, part in ((2, self.low), (3, self.high)):
                block = self.block(self.core, across, part)
                self.to_chip(at, block, block, at_x).wait_recv()
                self.go(self.to_core(at + 1, block, block))
            arriving = [
                self.block(other, self.inner),
                self.block(other, at_x),
                self.block(other, at_y),
                self.block(other, across, self.low),
                self.block(other, across, self.high),
            ]
        else:
            arriving = [
                self.block(other, lax.rem(self.inner - step + self.group, self.group)) for step in range(self.group)
            ]
        for at, block in enumerate(arriving):
            self.to_core(at, block, block).wait_recv()
        for copy in self.sent:
            copy.wait_send()
        self.own.wait()


class PlaneSum:

    @staticmethod
    def scratch(group, here, width):
        blocks = pltpu.VMEM((group, here, width), bf16)
        return [blocks, blocks, blocks, blocks, pltpu.SemaphoreType.DMA((2, 2 * group)), pltpu.SemaphoreType.DMA((2, group))]

    def __init__(self, group, product, out_ref, to_core, from_core, pair, land, chip_sems, core_sems):
        self.group, self.product, self.out_ref = group, product, out_ref
        self.to_core_ref, self.from_core_ref, self.pair, self.land = to_core, from_core, pair, land
        self.chip_sems, self.core_sems = chip_sems, core_sems
        self.core, self.inner = lax.axis_index("core"), lax.axis_index("fsdp")
        self.here, self.width = out_ref.shape
        half = self.here // 2
        self.low, self.high = pl.ds(0, half), pl.ds(half, half)
        self.tile = 512
        if group == 4:
            self.across_x, self.across_y, across = beside(self.inner)
            self.targets = [across, self.across_x, self.across_y, self.inner]
        else:
            self.targets = [lax.rem(self.inner + step, group) for step in range(1, group)] + [self.inner]
        self.sent = []

    def to_chip(self, at, source, target, inner):
        return send(source, target, self.chip_sems.at[0, at], self.chip_sems.at[1, at], self.core, inner)

    def go(self, copy):
        copy.start()
        self.sent.append(copy)

    def core_copy(self, i):
        return send(
            self.to_core_ref.at[i],
            self.from_core_ref.at[i],
            self.core_sems.at[0, i],
            self.core_sems.at[1, i],
            1 - self.core,
            self.inner,
        )

    def part_core(self, i):
        @pl.loop(0, self.width // self.tile)
        def _(at):
            columns = pl.ds(pl.multiple_of(at * self.tile, self.tile), self.tile)
            self.to_core_ref[i, :, columns] = self.product(1 - self.core, self.targets[i], columns).astype(bf16)

        self.go(self.core_copy(i))

    def part_chip(self, i):
        self.core_copy(i).wait_recv()
        last = i == self.group - 1

        @pl.loop(0, self.width // self.tile)
        def _(at):
            columns = pl.ds(pl.multiple_of(at * self.tile, self.tile), self.tile)
            value = self.product(self.core, self.targets[i], columns) + self.from_core_ref[i, :, columns].astype(f32)
            if last:
                self.out_ref[:, columns] = value
            else:
                self.pair[i, :, columns] = value.astype(bf16)

        if last:
            return
        pair, land = self.pair, self.land
        if self.group != 4:
            self.go(self.to_chip(i, pair.at[i], land.at[i], self.targets[i]))
        elif i == 0:
            self.go(self.to_chip(0, pair.at[0, self.low], land.at[0, self.low], self.across_x))
            self.go(self.to_chip(1, pair.at[0, self.high], land.at[1, self.low], self.across_y))
        elif i == 1:
            self.go(self.to_chip(2, pair.at[1, self.low], land.at[0, self.high], self.across_x))
        else:
            self.go(self.to_chip(3, pair.at[2, self.high], land.at[1, self.high], self.across_y))

    def arrive(self, at, place, part):
        self.to_chip(at, self.pair.at[0, part], self.land.at[place, part], self.across_x).wait_recv()
        return self.land[place, part, :].astype(f32)

    def relay(self):
        if self.group != 4:
            return
        pair, land = self.pair, self.land
        value = self.arrive(0, 0, self.low) + pair[2, self.low, :].astype(f32)
        pair[3, self.low, :] = value.astype(bf16)
        self.go(self.to_chip(4, pair.at[3, self.low], land.at[2, self.low], self.across_y))
        value = self.arrive(1, 1, self.low) + pair[1, self.high, :].astype(f32)
        pair[3, self.high, :] = value.astype(bf16)
        self.go(self.to_chip(5, pair.at[3, self.high], land.at[2, self.high], self.across_x))

    def finish(self):
        out_ref = self.out_ref
        if self.group == 4:
            out_ref[self.low, :] += self.arrive(2, 0, self.high)
            out_ref[self.high, :] += self.arrive(3, 1, self.high)
            out_ref[self.low, :] += self.arrive(4, 2, self.low)
            out_ref[self.high, :] += self.arrive(5, 2, self.high)
        else:
            for i in range(self.group - 1):
                self.to_chip(i, self.pair.at[i], self.land.at[i], self.inner).wait_recv()
                out_ref[...] += self.land[i].astype(f32)
        for copy in self.sent:
            copy.wait_send()

    def run(self):
        self.part_core(0)
        for i in range(self.group):
            if i + 1 < self.group:
                self.part_core(i + 1)
            self.part_chip(i)
        self.relay()
        self.finish()


def row_product(group, here, flip, a_ref, w_ref):
    def product(core, inner, columns):
        rows = a_ref[pl.ds(pl.multiple_of((core * group + inner) * here, here), here), :]
        if flip:
            return dot(rows, w_ref[columns, :], 1, 1)
        return dot(rows, w_ref[:, columns], 1, 0)

    return product


def other_device(core_at, inner_at, group, step):
    return lax.rem(core_at + step // group, 2), lax.rem(inner_at + step % group, group)


def gather_kernel(planes, group, *refs):
    gather_refs = 3
    if not planes:
        source, target = refs[:2]
        gather = PlaneGather(group, source, target, *refs[2:])
        greet(gather.core, gather.inner, group)
        gather.start()
        gather.relay()
        gather.finish()
        return
    source, small_ref, target, all_ref = refs[:4]
    gather = PlaneGather(group, source, target, *refs[4 : 4 + gather_refs])
    line_sems, face_sems = refs[4 + gather_refs :]
    z_at, core_at, inner_at = lax.axis_index("z"), gather.core, gather.inner
    mine, team = gather.mine, 2 * group
    barrier = pltpu.get_barrier_semaphore()
    for step in range(1, team):
        core, inner = other_device(core_at, inner_at, group, step)
        pl.semaphore_signal(barrier, inc=1, device_id={"core": core, "fsdp": inner}, device_id_type=MESH)
    for step in range(1, planes):
        to = lax.rem(z_at + step, planes)
        pl.semaphore_signal(barrier, inc=1, device_id={"z": to}, device_id_type=MESH)
    pl.semaphore_wait(barrier, team + planes - 2)
    lines, faces = [], []
    for step in range(1, planes):
        copy = pltpu.make_async_remote_copy(
            src_ref=small_ref,
            dst_ref=all_ref.at[mine, z_at],
            send_sem=line_sems.at[0, step],
            recv_sem=line_sems.at[1, step],
            device_id={"z": lax.rem(z_at + step, planes)},
            device_id_type=MESH,
        )
        copy.start()
        lines.append(copy)
    gather.start()
    all_ref[mine, z_at] = small_ref[...]
    for copy in lines:
        copy.wait()
    face = all_ref.at[mine]
    for step in range(1, team):
        copy = send(
            face, face, face_sems.at[0, step], face_sems.at[1, step], *other_device(core_at, inner_at, group, step)
        )
        copy.start()
        faces.append(copy)
    gather.relay()
    gather.finish()
    for step in range(1, team):
        core = lax.rem(core_at + step // group, 2)
        face = all_ref.at[core * group + lax.rem(inner_at - step % group + group, group)]
        send(face, face, face_sems.at[0, step], face_sems.at[1, step], core_at, inner_at).wait_recv()
    for copy in faces:
        copy.wait_send()


def plane_gather(array, group, collective_id, planes=0, small=None):
    anywhere = pl.BlockSpec(memory_space=pl.ANY)
    local = pl.BlockSpec(memory_space=pltpu.VMEM)
    shapes = [jax.ShapeDtypeStruct((2 * group, *array.shape), array.dtype)]
    scratch = PlaneGather.scratch(group)
    extra = []
    if planes:
        extra = [small]
        shapes.append(jax.ShapeDtypeStruct((2 * group, planes, *small.shape), small.dtype))
        scratch += [pltpu.SemaphoreType.DMA((2, planes)), pltpu.SemaphoreType.DMA((2, 2 * group))]
    results = pl.pallas_call(
        functools.partial(gather_kernel, planes, group),
        out_shape=shapes,
        in_specs=[anywhere] + [local] * len(extra),
        out_specs=[anywhere] + [local] * len(extra),
        scratch_shapes=scratch,
        compiler_params=pltpu.CompilerParams(collective_id=collective_id, has_side_effects=True),
        cost_estimate=pl.CostEstimate(flops=0, bytes_accessed=100 * array.size * 2, transcendentals=0),
    )(array, *extra)
    return [results[0].reshape(-1, array.shape[-1]), *results[1:]]


def product_sum_kernel(group, flip, a_ref, w_ref, out_ref, *refs):
    total = PlaneSum(group, row_product(group, out_ref.shape[0], flip, a_ref, w_ref), out_ref, *refs)
    greet(total.core, total.inner, group)
    total.run()


def product_sum(a, w, flip, group, collective_id):
    here = a.shape[0] // (2 * group)
    width = w.shape[0 if flip else 1]
    local = pl.BlockSpec(memory_space=pltpu.VMEM)
    return pl.pallas_call(
        functools.partial(product_sum_kernel, group, flip),
        out_shape=jax.ShapeDtypeStruct((here, width), f32),
        in_specs=[local, local],
        out_specs=local,
        scratch_shapes=PlaneSum.scratch(group, here, width),
        compiler_params=pltpu.CompilerParams(
            collective_id=collective_id, has_side_effects=True, vmem_limit_bytes=60 * 2**20
        ),
        cost_estimate=pl.CostEstimate(
            flops=2 * a.shape[0] * a.shape[1] * width, bytes_accessed=100 * a.shape[0] * width, transcendentals=0
        ),
    )(a, w)


def attend_kernel(
    block, group, x_ref, w_ref, gain_ref, shift_ref, qkv_bias_ref, live_ref, source,
    normed_ref, qkv_ref, mixed_ref, total_ref, target, bias_ref, *refs,
):
    seg_rows, heads = x_ref.shape[0] // 2, mixed_ref.shape[1] // HEAD
    gather = PlaneGather(group, source, target, *refs)
    greet(gather.core, gather.inner, group)
    gather.start()

    @pl.loop(0, 2 * seg_rows // block)
    def _(at):
        rows = pl.ds(pl.multiple_of(at * block, block), block)
        normed = (unit_norm(x_ref[rows, :].astype(f32))[0] * gain_ref[...] + shift_ref[...]).astype(bf16)
        normed_ref[rows, :] = normed
        qkv_ref[rows, :] = (dot(normed, w_ref[...], 1, 0) + qkv_bias_ref[...]).astype(bf16)

    for seg in range(2):
        attend_segment(block, heads, seg_rows, seg, qkv_ref, live_ref, mixed_ref, total_ref, bias_ref)
        if seg == 0:
            gather.relay()
    gather.finish()


def attend(x, w, gain, shift, qkv_bias, live, array, group, collective_id):
    rows, width = x.shape
    cols = w.shape[1] // 3
    block = 256
    local = pl.BlockSpec(memory_space=pltpu.VMEM)
    anywhere = pl.BlockSpec(memory_space=pl.ANY)
    results = pl.pallas_call(
        functools.partial(attend_kernel, block, group),
        out_shape=[
            jax.ShapeDtypeStruct((rows, width), bf16),
            jax.ShapeDtypeStruct((rows, 3 * cols), bf16),
            jax.ShapeDtypeStruct((rows, cols), bf16),
            jax.ShapeDtypeStruct((2, 8, rows // 2), f32),
            jax.ShapeDtypeStruct((2 * group, *array.shape), array.dtype),
        ],
        in_specs=[local] * 6 + [anywhere],
        out_specs=[local] * 4 + [anywhere],
        scratch_shapes=[pltpu.VMEM((block, rows // 2), f32), *PlaneGather.scratch(group)],
        compiler_params=pltpu.CompilerParams(
            collective_id=collective_id, has_side_effects=True, vmem_limit_bytes=60 * 2**20
        ),
        cost_estimate=pl.CostEstimate(
            flops=rows * rows * cols + 6 * rows * width * cols, bytes_accessed=10**8, transcendentals=0
        ),
    )(x, w, gain[None], shift[None], qkv_bias[None], live.astype(f32)[:, None], array)
    return [*results[:4], results[4].reshape(-1, array.shape[-1])]


def attend_back_kernel(
    block, group, qkv_ref, grad_ref, live_ref, total_ref, a_ref, w_ref, out_ref, own_ref, bias_ref, sums_ref, *refs
):
    seg_rows, heads = qkv_ref.shape[0] // 2, grad_ref.shape[1] // HEAD
    cols = heads * HEAD
    total = PlaneSum(group, row_product(group, own_ref.shape[0], False, a_ref, w_ref), own_ref, *refs)
    greet(total.core, total.inner, group)
    blocks = seg_rows // block
    for seg in range(2):
        sums_ref[...] = jnp.zeros_like(sums_ref)
        for at in range(blocks):
            step, late = divmod(seg * blocks + at, 2)
            if late:
                total.part_chip(step)
            else:
                total.part_core(step)
            if seg and at == blocks - 1:
                total.relay()
            attend_back_rows(
                block, heads, seg_rows, seg, at, qkv_ref, grad_ref, live_ref, total_ref, out_ref, bias_ref, sums_ref
            )
        out_ref[pl.ds(seg * seg_rows, seg_rows), cols:] = sums_ref[...].astype(bf16)
    total.finish()


def attend_back(qkv, grad, live, totals, a, w, group, collective_id):
    rows, cols = qkv.shape[0], qkv.shape[1] // 3
    here, width = rows // (2 * group), w.shape[1]
    local = pl.BlockSpec(memory_space=pltpu.VMEM)
    block = here
    return pl.pallas_call(
        functools.partial(attend_back_kernel, block, group),
        out_shape=[jax.ShapeDtypeStruct((rows, 3 * cols), bf16), jax.ShapeDtypeStruct((here, width), f32)],
        in_specs=[local] * 6,
        out_specs=[local] * 2,
        scratch_shapes=[
            pltpu.VMEM((rows // 2, block), f32),
            pltpu.VMEM((rows // 2, 2 * cols), f32),
            *PlaneSum.scratch(group, here, width),
        ],
        compiler_params=pltpu.CompilerParams(
            collective_id=collective_id, has_side_effects=True, vmem_limit_bytes=62 * 2**20
        ),
        cost_estimate=pl.CostEstimate(
            flops=2 * rows * rows * cols + 2 * rows * a.shape[1] * width, bytes_accessed=10**8, transcendentals=0
        ),
    )(qkv, grad, live.astype(f32).reshape(rows, 1), totals, a, w)


def exchange_kernel(group, count, *refs):
    ins, outs = refs[:count], refs[count : 2 * count]
    own_sem, out_sem, in_sem = refs[2 * count :]
    team = 2 * group
    core_at, inner_at = lax.axis_index("core"), lax.axis_index("fsdp")
    mine = core_at * group + inner_at

    def other(step):
        return lax.rem(core_at + step // group, 2), lax.rem(inner_at + step % group, group)

    def before(step):
        return lax.rem(core_at + step // group, 2), lax.rem(inner_at - step % group + group, group)

    barrier = pltpu.get_barrier_semaphore()
    for step in range(1, team):
        core, inner = other(step)
        pl.semaphore_signal(barrier, inc=1, device_id={"core": core, "fsdp": inner}, device_id_type=MESH)
    pl.semaphore_wait(barrier, team - 1)
    copies = []
    for i in range(count):
        for step in range(1, team):
            core, inner = other(step)
            copy = send(
                ins[i].at[core * group + inner], outs[i].at[mine], out_sem.at[i, step], in_sem.at[i, step], core, inner
            )
            copy.start()
            copies.append(copy)
        pltpu.make_async_copy(ins[i].at[mine], outs[i].at[mine], own_sem.at[i]).start()
    for i in range(count):
        pltpu.make_async_copy(ins[i].at[mine], outs[i].at[mine], own_sem.at[i]).wait()
        for step in range(1, team):
            core, inner = before(step)
            block = outs[i].at[core * group + inner]
            send(block, block, out_sem.at[i, step], in_sem.at[i, step], core, inner).wait_recv()
    for copy in copies:
        copy.wait_send()


def plane_exchange(arrays, group, collective_id):
    count = len(arrays)
    sems = pltpu.SemaphoreType.DMA((count, 2 * group))
    anywhere = pl.BlockSpec(memory_space=pl.ANY)
    size = sum(a.size * a.dtype.itemsize for a in arrays)
    return pl.pallas_call(
        functools.partial(exchange_kernel, group, count),
        out_shape=[jax.ShapeDtypeStruct(a.shape, a.dtype) for a in arrays],
        in_specs=[anywhere] * count,
        out_specs=[anywhere] * count,
        scratch_shapes=[pltpu.SemaphoreType.DMA((count,)), sems, sems],
        compiler_params=pltpu.CompilerParams(collective_id=collective_id, has_side_effects=True),
        cost_estimate=pl.CostEstimate(flops=0, bytes_accessed=40 * size, transcendentals=0),
    )(*arrays)


def small_sum_kernel(planes, group, in_ref, out_ref, from_plane, summed, from_z, plane_sems, z_sems):
    team = 2 * group
    z_at, core_at, inner_at = (lax.axis_index(name) for name in ALL)
    mine = core_at * group + inner_at

    def other(step):
        return lax.rem(core_at + step // group, 2), lax.rem(inner_at + step % group, group)

    barrier = pltpu.get_barrier_semaphore()
    for step in range(1, team):
        core, inner = other(step)
        pl.semaphore_signal(barrier, inc=1, device_id={"core": core, "fsdp": inner}, device_id_type=MESH)
    for step in range(1, planes):
        pl.semaphore_signal(
            barrier, inc=1, device_id={"z": lax.rem(z_at + step, planes)}, device_id_type=MESH
        )
    pl.semaphore_wait(barrier, team + planes - 2)
    copies = []
    for step in range(1, team):
        core, inner = other(step)
        copy = send(
            in_ref.at[core * group + inner],
            from_plane.at[step],
            plane_sems.at[0, step],
            plane_sems.at[1, step],
            core,
            inner,
        )
        copy.start()
        copies.append(copy)
    summed[...] = in_ref[mine]
    for copy in copies:
        copy.wait_recv()
    for step in range(1, team):
        summed[...] += from_plane[step]
    more = []
    for step in range(1, planes):
        to = lax.rem(z_at + step, planes)
        copy = pltpu.make_async_remote_copy(
            src_ref=summed.at[to],
            dst_ref=from_z.at[step],
            send_sem=z_sems.at[0, step],
            recv_sem=z_sems.at[1, step],
            device_id={"z": to},
            device_id_type=MESH,
        )
        copy.start()
        more.append(copy)
    out_ref[...] = summed[z_at]
    for step, copy in enumerate(more, 1):
        copy.wait_recv()
        out_ref[...] += from_z[step]
    for copy in copies + more:
        copy.wait_send()


def small_sum(terms, planes, group, collective_id):
    lines = terms.shape[2]
    local = pl.BlockSpec(memory_space=pltpu.VMEM)
    return pl.pallas_call(
        functools.partial(small_sum_kernel, planes, group),
        out_shape=jax.ShapeDtypeStruct((lines, 128), f32),
        in_specs=[local],
        out_specs=local,
        scratch_shapes=[
            pltpu.VMEM((2 * group, planes, lines, 128), f32),
            pltpu.VMEM((planes, lines, 128), f32),
            pltpu.VMEM((planes, lines, 128), f32),
            pltpu.SemaphoreType.DMA((2, 2 * group)),
            pltpu.SemaphoreType.DMA((2, planes)),
        ],
        compiler_params=pltpu.CompilerParams(collective_id=collective_id, has_side_effects=True),
        cost_estimate=pl.CostEstimate(flops=0, bytes_accessed=10**7, transcendentals=0),
    )(terms)


def body(
    layer_input,
    first_gain,
    first_shift,
    query_weight,
    key_weight,
    value_weight,
    output_weight,
    query_bias,
    value_bias,
    output_bias,
    second_gain,
    second_shift,
    up_weight,
    up_bias,
    down_weight,
    down_bias,
    segment_counts,
    out_grad,
):
    here, width = layer_input.shape
    wide = up_weight.shape[1]
    planes = lax.axis_size("z")
    group = lax.axis_size("fsdp")
    team = 2 * group
    z_at, core_at, inner_at = (lax.axis_index(name) for name in ALL)
    plane_at = core_at * group + inner_at
    seg_rows = here * group
    own_rows = query_weight.shape[0]
    own_wide = down_weight.shape[0]
    cols = width // team
    heads_here = cols // HEAD
    whole_heads = own_rows % HEAD == 0

    def to_columns(weight, unit):
        cut = weight.reshape(weight.shape[0], planes, team, unit)
        return cut.transpose(2, 0, 1, 3).reshape(team, weight.shape[0], planes * unit)

    def from_columns(blocks, unit):
        rows = blocks.shape[1]
        return blocks.reshape(team, rows, planes, unit).transpose(1, 2, 0, 3).reshape(rows, planes * team * unit)

    def head_columns(weight):
        if whole_heads:
            return to_columns(weight, own_rows)
        return weight.reshape(own_rows, team, cols).transpose(1, 0, 2)

    def head_rows(blocks):
        if whole_heads:
            return from_columns(blocks, own_rows)
        return blocks.transpose(1, 0, 2).reshape(own_rows, width)

    attn_blocks = jnp.concatenate([head_columns(w) for w in (query_weight, key_weight, value_weight)], axis=2)
    (attn_cols,) = plane_exchange([attn_blocks], group, 0)
    attn_cols = attn_cols.reshape(team * own_rows, 3 * cols)
    attn_full = z_gather(attn_cols)
    small = jnp.concatenate(
        [first_gain, first_shift, query_bias, value_bias, output_bias, second_gain, second_shift, down_bias, up_bias]
    )
    length = small.shape[0]
    small = jnp.pad(small.astype(f32), (0, -length % 1024)).reshape(-1, 128)
    all_rows, small_all = plane_gather(after(layer_input, attn_cols), group, 1, planes, small)
    small_all = small_all.swapaxes(0, 1).reshape(planes * team, -1)
    (up_cols,) = plane_exchange([after(to_columns(up_weight, own_wide), all_rows)], group, 10)
    up_cols = up_cols.reshape(team * own_rows, wide // team)
    gain_one, shift_one, bias_q, bias_v, bias_o, gain_two, shift_two, bias_down = (
        small_all[:, i * own_rows : (i + 1) * own_rows].reshape(width) for i in range(8)
    )
    bias_up = small_all[:, 8 * own_rows : length].reshape(planes, team, own_wide)[:, plane_at].reshape(wide // team)

    def own_columns(bias):
        if whole_heads:
            return bias.reshape(planes, team, own_rows)[:, plane_at].reshape(cols)
        return lax.dynamic_slice_in_dim(bias, plane_at * cols, cols)

    bias_q, bias_v = own_columns(bias_q), own_columns(bias_v)
    if whole_heads:
        out_full = z_gather(output_weight)
    else:
        out_full = lax.dynamic_slice_in_dim(
            lax.all_gather(output_weight, ALL, axis=0, tiled=True), plane_at * cols, cols
        )
    up_full = z_gather(up_cols)
    down_full = z_gather(down_weight)

    segment = 2 * z_at + jnp.arange(2, dtype=jnp.int32)
    place = segment % MAXSEG
    present = place < segment_counts[segment // MAXSEG]
    pos = jnp.arange(seg_rows, dtype=jnp.int32)
    live = present[:, None] & ((pos >= PRE)[None] | (place[:, None] >= PREV - pos[None] // SUMM))
    own_pos = inner_at * here + jnp.arange(here, dtype=jnp.int32)
    live_own = lax.dynamic_slice(live, (core_at, inner_at * here), (1, here))[0]

    out_own = jnp.where(live_own[:, None], out_grad, jnp.zeros_like(out_grad))
    rows_own = layer_input.astype(f32)
    unit_one, inverse_one = unit_norm(rows_own)
    normed_low, qkv, mixed_low, totals, out_live = attend(
        all_rows,
        attn_full,
        gain_one,
        shift_one,
        jnp.concatenate([bias_q, jnp.zeros_like(bias_q), bias_v]),
        live,
        out_own,
        group,
        11,
    )
    attended = rows_own + product_sum(mixed_low, out_full, False, group, 2) + bias_o
    unit_two, inverse_two = unit_norm(attended)
    (second_low,) = plane_gather((unit_two * gain_two + shift_two).astype(bf16), group, 3)
    pre_act = dot(second_low, up_full, 1, 0) + bias_up
    cdf = gauss_cdf(pre_act)
    activated = (pre_act * cdf).astype(bf16)

    out_own = out_own.astype(f32)
    grad_down = dot(activated, out_live, 0, 0).astype(bf16)
    out_live = after(out_live, grad_down)
    grad_down = z_sum(grad_down).astype(f32)
    grad_pre = (dot(out_live, down_full, 1, 1) * gelu_slope(pre_act, cdf)).astype(bf16)
    grad_up = dot(second_low, grad_pre, 0, 0).astype(bf16)
    grad_pre = after(grad_pre, grad_up)
    grad_up_bias = jnp.sum(grad_pre.astype(f32), axis=0)
    grad_second_in = product_sum(grad_pre, up_full, True, group, 5)
    grad_up = z_sum(after(grad_up, grad_down, grad_second_in)).reshape(team, own_rows, wide // team)
    grad_norm, grad_second_gain, grad_second_shift = normalize_back(
        grad_second_in, unit_two, inverse_two, gain_two
    )
    grad_after = out_own + grad_norm
    after_low_own = grad_after.astype(bf16)
    grad_output_bias = jnp.sum(after_low_own.astype(f32), axis=0)
    (after_low,) = plane_gather(after_low_own, group, 6)
    grad_output = dot(mixed_low, after_low, 0, 0).astype(bf16)
    after_low = after(after_low, grad_output)
    grad_mixed = dot(after_low, out_full, 1, 1).astype(bf16)
    grad_qkv, added = attend_back(qkv, grad_mixed, live, totals, activated, down_full, group, 4)
    layer_output = (attended + added + bias_down).astype(bf16)
    if whole_heads:
        grad_output = z_sum(after(grad_output, grad_up, grad_qkv)).astype(f32)
    else:
        spread = jnp.zeros((width, width), bf16)
        spread = lax.dynamic_update_slice_in_dim(spread, grad_output.astype(bf16), plane_at * cols, 0)
        grad_output = lax.psum_scatter(spread, ALL, scatter_dimension=0, tiled=True).astype(f32)
    grad_attn = dot(normed_low, grad_qkv, 0, 0).astype(bf16)
    grad_qkv = after(grad_qkv, grad_attn)
    grad_attn = z_sum(after(grad_attn, grad_output)).reshape(team, own_rows, 3 * cols)
    grad_bias = jnp.sum(grad_qkv.astype(f32), axis=0)
    grad_norm, grad_first_gain, grad_first_shift = normalize_back(
        product_sum(grad_qkv, attn_full, True, group, 8), unit_one, inverse_one, gain_one
    )
    input_grad = jnp.where((own_pos >= SUMM)[:, None], grad_after + grad_norm, 0.0)

    def spread_columns(bias):
        if whole_heads:
            full = jnp.zeros((planes, team, own_rows), f32)
            return lax.dynamic_update_slice(full, bias.reshape(planes, 1, own_rows), (0, plane_at, 0)).reshape(width)
        return lax.dynamic_update_slice(jnp.zeros((width,), f32), bias, (plane_at * cols,))

    sums = [
        grad_first_gain,
        grad_first_shift,
        spread_columns(grad_bias[:cols]),
        spread_columns(grad_bias[2 * cols :]),
        grad_output_bias,
        grad_second_gain,
        grad_second_shift,
        jnp.sum(out_own, axis=0),
    ]
    up_spread = jnp.zeros((planes, team, own_wide), f32)
    up_spread = lax.dynamic_update_slice(up_spread, grad_up_bias.reshape(planes, 1, own_wide), (0, plane_at, 0))
    packed = jnp.concatenate(
        [a.reshape(planes * team, own_rows) for a in sums] + [up_spread.reshape(planes * team, own_wide)], axis=1
    )
    packed = jnp.pad(packed, ((0, 0), (0, -length % 1024))).reshape(planes, team, -1, 128).swapaxes(0, 1)
    packed = small_sum(packed, planes, group, 9).reshape(-1)
    (grad_up,) = plane_exchange([after(grad_up, packed)], group, 12)
    grad_up = from_columns(grad_up, own_wide).astype(f32)
    (grad_attn,) = plane_exchange([after(grad_attn, grad_up)], group, 7)
    grad_weights = [head_rows(grad_attn[:, :, i * cols : (i + 1) * cols]).astype(f32) for i in range(3)]
    small_grads = [packed[i * own_rows : (i + 1) * own_rows] for i in range(8)]
    return (
        layer_output,
        input_grad,
        small_grads[0],
        small_grads[1],
        *grad_weights,
        grad_output,
        small_grads[2],
        small_grads[3],
        small_grads[4],
        small_grads[5],
        small_grads[6],
        grad_up,
        packed[8 * own_rows : length],
        grad_down,
        small_grads[7],
    )


def solution(mesh):
    outer, inner = mesh.devices.shape
    fine = Mesh(mesh.devices.reshape(outer // 2, 2, inner), ALL)
    rows, vector = P(ALL, None), P(ALL)
    return jax.shard_map(
        body,
        mesh=fine,
        in_specs=(
            rows, vector, vector, rows, rows, rows, rows, vector, vector, vector, vector, vector,
            rows, vector, rows, vector, P(), rows,
        ),
        out_specs=(
            rows, rows, vector, vector, rows, rows, rows, rows, vector, vector, vector, vector, vector,
            rows, vector, rows, vector,
        ),
        check_vma=False,
    )
```

```python
import functools
import math

import jax
import jax.numpy as jnp
from jax import lax
from jax.experimental import pallas as pl
from jax.experimental.pallas import tpu as pltpu
from jax.sharding import Mesh, PartitionSpec as P

HEADS = 32
HEAD = 64
SUMM = 50
PREV = 3
MAXSEG = 4
PRE = 150

epsilon = 1e-05
masked = -1e30

ALL = ("z", "core", "fsdp")
PLANE = ("core", "fsdp")
bf16 = jnp.bfloat16
f32 = jnp.float32
MESH = pl.DeviceIdType.MESH


def dot(a, b, ca, cb):
    return lax.dot_general(a, b, (((ca,), (cb,)), ((), ())), preferred_element_type=f32)


def z_gather(rows):
    return lax.all_gather(rows, "z", axis=0, tiled=True)


def z_sum(partial):
    return lax.psum_scatter(partial.astype(bf16), "z", scatter_dimension=0, tiled=True)


def after(value, *earlier):
    return lax.optimization_barrier((value, *earlier))[0]


def unit_norm(values):
    center = values - jnp.mean(values, axis=-1, keepdims=True)
    inverse_std = lax.rsqrt(jnp.mean(center * center, axis=-1, keepdims=True) + epsilon)
    return center * inverse_std, inverse_std


def normalize_back(grad_rows, unit_rows, inverse_std, norm_gain):
    scaled = grad_rows * norm_gain
    centered = scaled - jnp.mean(scaled, axis=-1, keepdims=True)
    centered = centered - unit_rows * jnp.mean(scaled * unit_rows, axis=-1, keepdims=True)
    return centered * inverse_std


def head_mask(rows, cols, head):
    lane = lax.broadcasted_iota(jnp.int32, (rows, cols), 1)
    return lane // HEAD == head


def attend_segment(block, heads, seg_rows, seg, qkv_ref, live_ref, mixed_ref, total_ref, bias_ref):
    cols = heads * HEAD
    base = seg * seg_rows
    lane = lax.broadcasted_iota(jnp.int32, (block, 128), 1)
    for at in range(seg_rows // block):
        wide = (at + 1) * block
        rows = pl.ds(pl.multiple_of(base + at * block, block), block)
        keys = pl.ds(pl.multiple_of(base, seg_rows), wide)
        query_pos = at * block + lax.broadcasted_iota(jnp.int32, (block, wide), 0)
        key_pos = lax.broadcasted_iota(jnp.int32, (block, wide), 1)
        open_key = (live_ref[seg, :, :wide] > 0.0) & (key_pos < query_pos) | (key_pos == query_pos)
        bias_ref[:, :wide] = jnp.where(open_key, 0.0, masked)
        query = qkv_ref[rows, :cols] * jnp.asarray(HEAD**-0.5, bf16)
        result = jnp.zeros((block, cols), f32)
        totals = jnp.zeros((block, 128), f32)
        for head in range(heads):
            chosen = head_mask(block, cols, head)
            scores = dot(jnp.where(chosen, query, jnp.zeros_like(query)), qkv_ref[keys, cols : 2 * cols], 1, 1)
            scores = scores + bias_ref[:, :wide]
            top = jnp.max(scores, axis=1, keepdims=True)
            powers = jnp.exp(scores - top)
            total = jnp.sum(powers, axis=1, keepdims=True)
            probs = (powers * (1.0 / total)).astype(bf16)
            value = dot(probs, qkv_ref[keys, 2 * cols :], 1, 0)
            result = jnp.where(chosen, value, result)
            totals = jnp.where(lane == head, top + jnp.log(total), totals)
        mixed_ref[rows, :] = result.astype(bf16)
        total_ref[seg, :, at * block : (at + 1) * block] = totals.T[:8]


def attend_back_rows(
    block, heads, seg_rows, seg, at, qkv_ref, grad_ref, live_ref, total_ref, out_ref, bias_ref, sums_ref
):
    cols = heads * HEAD
    base = seg * seg_rows
    wide = (at + 1) * block
    rows = pl.ds(pl.multiple_of(base + at * block, block), block)
    keys = pl.ds(pl.multiple_of(base, seg_rows), wide)
    key_pos = lax.broadcasted_iota(jnp.int32, (wide, block), 0)
    query_pos = at * block + lax.broadcasted_iota(jnp.int32, (wide, block), 1)
    open_key = (live_ref[keys, :] > 0.0) & (key_pos < query_pos) | (key_pos == query_pos)
    bias_ref[:wide, :] = jnp.where(open_key, 0.0, masked)
    query = qkv_ref[rows, :cols] * jnp.asarray(HEAD**-0.5, bf16)
    half = block // 2
    part = pl.ds(pl.multiple_of((base + at * block) // 2, half), half)
    grad = jnp.concatenate([one[part, :] for one in grad_ref], axis=0)
    grad_query = jnp.zeros((block, cols), f32)
    for head in range(heads):
        chosen = head_mask(block, cols, head)
        query_one = jnp.where(chosen, query, jnp.zeros_like(query))
        grad_one = jnp.where(chosen, grad, jnp.zeros_like(grad))
        scores = dot(qkv_ref[keys, cols : 2 * cols], query_one, 1, 1)
        total = total_ref[seg, head : head + 1, at * block : (at + 1) * block]
        probs = jnp.exp(scores + bias_ref[:wide, :] - total)
        terms = probs * dot(qkv_ref[keys, 2 * cols :], grad_one, 1, 1)
        delta = jnp.sum(terms, axis=0, keepdims=True)
        grad_scores = (terms - probs * delta).astype(bf16)
        sums_ref[:wide, :cols] += dot(grad_scores, query_one, 1, 0)
        sums_ref[:wide, cols:] += dot(probs.astype(bf16), grad_one, 1, 0)
        value = dot(grad_scores, qkv_ref[keys, cols : 2 * cols], 0, 0)
        grad_query = jnp.where(chosen, value, grad_query)
    out_ref[rows, :cols] = (grad_query * HEAD**-0.5).astype(bf16)


def other_device(core_at, inner_at, group, step):
    return lax.rem(core_at + step // group, 2), lax.rem(inner_at + step % group, group)


def signal(**place):
    pl.semaphore_signal(pltpu.get_barrier_semaphore(), inc=1, device_id=place, device_id_type=MESH)


def greet(core_at, inner_at, group):
    signal(core=1 - core_at, fsdp=inner_at)
    for step in range(1, group):
        signal(core=core_at, fsdp=lax.rem(inner_at + step, group))
    pl.semaphore_wait(pltpu.get_barrier_semaphore(), group)


def greet_all(core_at, inner_at, group, planes):
    z_at = lax.axis_index("z")
    for step in range(1, 2 * group):
        core, inner = other_device(core_at, inner_at, group, step)
        signal(core=core, fsdp=inner)
    for step in range(1, planes):
        signal(z=lax.rem(z_at + step, planes))
    pl.semaphore_wait(pltpu.get_barrier_semaphore(), 2 * group + planes - 2)


def send(source, target, send_sem, recv_sem, core, inner):
    return pltpu.make_async_remote_copy(
        src_ref=source,
        dst_ref=target,
        send_sem=send_sem,
        recv_sem=recv_sem,
        device_id={"core": core, "fsdp": inner},
        device_id_type=MESH,
    )


def beside(inner_at):
    at_x = inner_at + 1 - 2 * lax.rem(inner_at, 2)
    at_y = lax.rem(inner_at + 2, 4)
    return at_x, at_y, lax.rem(at_x + 2, 4)


class PlaneGather:

    @staticmethod
    def scratch(group):
        return [pltpu.SemaphoreType.DMA((2, 2 * group)), pltpu.SemaphoreType.DMA((2, 2 * group)), pltpu.SemaphoreType.DMA]

    def __init__(self, group, source, target, chip_sems, core_sems, own_sem):
        self.group, self.source, self.target = group, source, target
        self.chip_sems, self.core_sems = chip_sems, core_sems
        self.core, self.inner = lax.axis_index("core"), lax.axis_index("fsdp")
        self.mine = self.core * group + self.inner
        self.own = pltpu.make_async_copy(source, target.at[self.mine], own_sem)
        half = source.shape[0] // 2
        self.low, self.high = pl.ds(0, half), pl.ds(half, half)
        self.sent = []

    def to_chip(self, at, source, target, inner):
        return send(source, target, self.chip_sems.at[0, at], self.chip_sems.at[1, at], self.core, inner)

    def to_core(self, at, source, target):
        return send(source, target, self.core_sems.at[0, at], self.core_sems.at[1, at], 1 - self.core, self.inner)

    def block(self, core, inner, part=None):
        at = core * self.group + inner
        return self.target.at[at] if part is None else self.target.at[at, part]

    def go(self, copy):
        copy.start()
        self.sent.append(copy)

    def start(self):
        own = self.target.at[self.mine]
        if self.group == 4:
            at_x, at_y, _ = beside(self.inner)
            self.go(self.to_chip(0, self.source, own, at_x))
            self.go(self.to_chip(1, self.source, own, at_y))
        else:
            for step in range(1, self.group):
                self.go(self.to_chip(step, self.source, own, lax.rem(self.inner + step, self.group)))
        self.go(self.to_core(0, self.source, own))
        self.own.start()

    def wait_core(self, at):
        other, low, high = 1 - self.core, self.low, self.high
        if self.group == 4:
            at_x, at_y, across = beside(self.inner)
            inner, part = ((self.inner, None), (at_x, None), (at_y, None), (across, low), (across, high))[at]
        else:
            inner, part = lax.rem(self.inner - at + self.group, self.group), None
        block = self.block(other, inner, part)
        self.to_core(at, block, block).wait_recv()

    def across(self):
        if self.group == 4:
            at_x, at_y, across = beside(self.inner)
            for at, part in ((2, self.low), (3, self.high)):
                block = self.block(self.core, across, part)
                self.to_chip(at, block, block, at_x).wait_recv()
                self.go(self.to_core(at + 1, block, block))

    def run(self, use):
        core, inner, other = self.core, self.inner, 1 - self.core
        self.start()
        self.own.wait()
        use(core, inner)
        self.wait_core(0)
        use(other, inner)
        self.relay()
        if self.group == 4:
            at_x, at_y, across = beside(inner)
            use(core, at_x)
            use(core, at_y)
            self.wait_core(1)
            use(other, at_x)
            self.wait_core(2)
            use(other, at_y)
            self.across()
            use(core, across)
            self.wait_core(3)
            self.wait_core(4)
            use(other, across)
        else:
            for step in range(1, self.group):
                use(core, lax.rem(inner - step + self.group, self.group))
            for step in range(1, self.group):
                self.wait_core(step)
                use(other, lax.rem(inner - step + self.group, self.group))
        for copy in self.sent:
            copy.wait_send()

    def relay(self):
        if self.group == 4:
            at_x, at_y, _ = beside(self.inner)
            block = self.block(self.core, at_x)
            self.to_chip(0, block, block, at_x).wait_recv()
            part = self.block(self.core, at_x, self.low)
            self.go(self.to_chip(2, part, part, at_y))
            self.go(self.to_core(1, block, block))
            block = self.block(self.core, at_y)
            self.to_chip(1, block, block, at_y).wait_recv()
            part = self.block(self.core, at_y, self.high)
            self.go(self.to_chip(3, part, part, at_x))
            self.go(self.to_core(2, block, block))
        else:
            for step in range(1, self.group):
                inner = lax.rem(self.inner - step + self.group, self.group)
                block = self.block(self.core, inner)
                self.to_chip(step, block, block, inner).wait_recv()
                self.go(self.to_core(step, block, block))

    def finish(self):
        self.across()
        for at in range(5 if self.group == 4 else self.group):
            self.wait_core(at)
        for copy in self.sent:
            copy.wait_send()
        self.own.wait()


class PlaneSum:

    @staticmethod
    def scratch(group, here, width):
        blocks, fewer = (pltpu.VMEM((count, here, width), bf16) for count in (group, group - 1))
        sems = [pltpu.SemaphoreType.DMA((2, 2 * group)), pltpu.SemaphoreType.DMA((2, group))]
        return [blocks, blocks, blocks if group == 4 else fewer, fewer, *sems]

    def __init__(self, group, product, out_ref, to_core, from_core, pair, land, chip_sems, core_sems, prepare=None):
        self.group, self.product, self.out_ref, self.prepare = group, product, out_ref, prepare
        self.to_core_ref, self.from_core_ref, self.pair, self.land = to_core, from_core, pair, land
        self.chip_sems, self.core_sems = chip_sems, core_sems
        self.core, self.inner = lax.axis_index("core"), lax.axis_index("fsdp")
        self.here, self.width = out_ref.shape
        half = self.here // 2
        self.low, self.high = pl.ds(0, half), pl.ds(half, half)
        self.tile = math.gcd(self.width, 8192 // group)
        if group == 4:
            self.across_x, self.across_y, across = beside(self.inner)
            self.targets = [across, self.across_x, self.across_y, self.inner]
        else:
            self.targets = [lax.rem(self.inner + step, group) for step in range(1, group)] + [self.inner]
        self.sent = []

    def to_chip(self, at, source, target, inner):
        return send(source, target, self.chip_sems.at[0, at], self.chip_sems.at[1, at], self.core, inner)

    def go(self, copy):
        copy.start()
        self.sent.append(copy)

    def core_copy(self, i):
        return send(
            self.to_core_ref.at[i],
            self.from_core_ref.at[i],
            self.core_sems.at[0, i],
            self.core_sems.at[1, i],
            1 - self.core,
            self.inner,
        )

    def part_core(self, i):
        if self.prepare:
            self.prepare(1 - self.core, self.targets[i], 2 * i)

        @pl.loop(0, self.width // self.tile)
        def _(at):
            columns = pl.ds(pl.multiple_of(at * self.tile, self.tile), self.tile)
            self.to_core_ref[i, :, columns] = self.product(1 - self.core, self.targets[i], columns).astype(bf16)

        self.go(self.core_copy(i))

    def part_chip(self, i):
        if self.prepare:
            self.prepare(self.core, self.targets[i], 2 * i + 1)
        self.core_copy(i).wait_recv()
        last = i == self.group - 1

        @pl.loop(0, self.width // self.tile)
        def _(at):
            columns = pl.ds(pl.multiple_of(at * self.tile, self.tile), self.tile)
            value = self.product(self.core, self.targets[i], columns) + self.from_core_ref[i, :, columns].astype(f32)
            if last:
                self.out_ref[:, columns] = value
            else:
                self.pair[i, :, columns] = value.astype(bf16)

        if last:
            return
        pair, land = self.pair, self.land
        if self.group != 4:
            self.go(self.to_chip(i, pair.at[i], land.at[i], self.targets[i]))
        elif i == 0:
            self.go(self.to_chip(0, pair.at[0, self.low], land.at[0, self.low], self.across_x))
            self.go(self.to_chip(1, pair.at[0, self.high], land.at[1, self.low], self.across_y))
        elif i == 1:
            self.go(self.to_chip(2, pair.at[1, self.low], land.at[0, self.high], self.across_x))
        else:
            self.go(self.to_chip(3, pair.at[2, self.high], land.at[1, self.high], self.across_y))

    def arrive(self, at, place, part):
        self.to_chip(at, self.pair.at[0, part], self.land.at[place, part], self.across_x).wait_recv()
        return self.land[place, part, :].astype(f32)

    def relay(self):
        if self.group != 4:
            return
        pair, land = self.pair, self.land
        value = self.arrive(0, 0, self.low) + pair[2, self.low, :].astype(f32)
        pair[3, self.low, :] = value.astype(bf16)
        self.go(self.to_chip(4, pair.at[3, self.low], land.at[2, self.low], self.across_y))
        value = self.arrive(1, 1, self.low) + pair[1, self.high, :].astype(f32)
        pair[3, self.high, :] = value.astype(bf16)
        self.go(self.to_chip(5, pair.at[3, self.high], land.at[2, self.high], self.across_x))

    def finish(self):
        out_ref = self.out_ref
        if self.group == 4:
            out_ref[self.low, :] += self.arrive(2, 0, self.high)
            out_ref[self.high, :] += self.arrive(3, 1, self.high)
            out_ref[self.low, :] += self.arrive(4, 2, self.low)
            out_ref[self.high, :] += self.arrive(5, 2, self.high)
        else:
            for i in range(self.group - 1):
                self.to_chip(i, self.pair.at[i], self.land.at[i], self.inner).wait_recv()
                out_ref[...] += self.land[i].astype(f32)
        for copy in self.sent:
            copy.wait_send()

    @staticmethod
    def order(group, eager=False):
        if eager:
            return list(range(2 * group))
        parts = [0]
        for i in range(group):
            parts += ([2 * i + 2] if i + 1 < group else []) + [2 * i + 1]
        return parts

    def part(self, at):
        (self.part_chip if at % 2 else self.part_core)(at // 2)

    def run(self, eager=False, meanwhile=None):
        for at in self.order(self.group, eager):
            self.part(at)
        self.relay()
        if meanwhile:
            meanwhile()
        self.finish()


class PlanesSum:

    @staticmethod
    def scratch(planes, rows, width):
        return [pltpu.VMEM((planes, rows, width), bf16), pltpu.SemaphoreType.DMA((2, planes))]

    def __init__(self, planes, source, out_ref, land, sems):
        self.planes, self.source, self.out_ref, self.land, self.sems = planes, source, out_ref, land, sems
        self.z = lax.axis_index("z")
        self.sent = []

    def rows(self, z):
        count = self.out_ref.shape[0]
        return pl.ds(pl.multiple_of(z * count, count), count)

    def start(self):
        for step in range(1, self.planes):
            to = lax.rem(self.z + step, self.planes)
            copy = pltpu.make_async_remote_copy(
                src_ref=self.source.at[self.rows(to)],
                dst_ref=self.land.at[step],
                send_sem=self.sems.at[0, step],
                recv_sem=self.sems.at[1, step],
                device_id={"z": to},
                device_id_type=MESH,
            )
            copy.start()
            self.sent.append(copy)

    def finish(self):
        self.out_ref[...] = self.source[self.rows(self.z), :].astype(f32)
        for step, copy in enumerate(self.sent, 1):
            copy.wait()
            self.out_ref[...] += self.land[step].astype(f32)


def place_columns(out_ref, blocks, base, unit, planes, team):
    several = max(1, 128 // unit)
    for z in range(planes):
        for p in range(0, team, several):
            parts = [blocks[p + i, :, base + z * unit : base + (z + 1) * unit] for i in range(several)]
            value = parts[0] if several == 1 else jnp.concatenate(parts, axis=1)
            start = (z * team + p) * unit
            out_ref[:, start : start + unit * several] = value


def row_product(group, here, flip, a_ref, w_ref):
    def product(core, inner, columns):
        rows = a_ref[pl.ds(pl.multiple_of((core * group + inner) * here, here), here), :]
        if flip:
            return dot(rows, w_ref[columns, :], 1, 1)
        return dot(rows, w_ref[:, columns], 1, 0)

    return product


class PlaneExchange:

    @staticmethod
    def scratch(group):
        return [pltpu.SemaphoreType.DMA((2, 2 * group)), pltpu.SemaphoreType.DMA]

    def __init__(self, group, source, target, sems, own_sem):
        self.group, self.source, self.target, self.sems = group, source, target, sems
        self.core, self.inner = lax.axis_index("core"), lax.axis_index("fsdp")
        self.mine = self.core * group + self.inner
        self.own = pltpu.make_async_copy(source.at[self.mine], target.at[self.mine], own_sem)
        self.sent = []

    def start(self):
        for step in range(1, 2 * self.group):
            core, inner = other_device(self.core, self.inner, self.group, step)
            copy = send(
                self.source.at[core * self.group + inner],
                self.target.at[self.mine],
                self.sems.at[0, step],
                self.sems.at[1, step],
                core,
                inner,
            )
            copy.start()
            self.sent.append(copy)
        self.own.start()

    def start_cut(self, whole, unit, repeats):
        team = 2 * self.group
        for p in range(team):
            for r in range(repeats):
                start = (r * team + p) * unit
                self.source[p, :, r * unit : (r + 1) * unit] = whole[:, start : start + unit]
        self.start()

    def finish(self):
        group = self.group
        for step in range(1, 2 * group):
            core = lax.rem(self.core + step // group, 2)
            inner = lax.rem(self.inner - step % group + group, group)
            block = self.target.at[core * group + inner]
            send(block, block, self.sems.at[0, step], self.sems.at[1, step], core, inner).wait_recv()
        for copy in self.sent:
            copy.wait_send()
        self.own.wait()


ANY = pl.BlockSpec(memory_space=pl.ANY)
LOCAL = pl.BlockSpec(memory_space=pltpu.VMEM)


def talk(collective_id, megabytes):
    return pltpu.CompilerParams(
        collective_id=collective_id, has_side_effects=True, vmem_limit_bytes=megabytes * 2**20
    )


def cost(flops, bytes_accessed):
    return pl.CostEstimate(flops=flops, bytes_accessed=bytes_accessed, transcendentals=0)


def swap_kernel(group, unit, repeats, attn, up, attn_all, up_all, up_blocks, *refs):
    first = PlaneExchange(group, attn, attn_all, *refs[:2])
    second = PlaneExchange(group, up_blocks, up_all, *refs[2:])
    greet_all(first.core, first.inner, group, 1)
    first.start()
    second.start_cut(up, unit, repeats)
    first.finish()
    second.finish()


def plane_exchange(attn, up, unit, repeats, group, collective_id):
    team = 2 * group
    blocks = jax.ShapeDtypeStruct((team, up.shape[0], unit * repeats), up.dtype)
    return pl.pallas_call(
        functools.partial(swap_kernel, group, unit, repeats),
        out_shape=[jax.ShapeDtypeStruct(attn.shape, attn.dtype), blocks],
        in_specs=[ANY, LOCAL],
        out_specs=[ANY, ANY],
        scratch_shapes=[
            pltpu.VMEM(blocks.shape, blocks.dtype),
            *PlaneExchange.scratch(group),
            *PlaneExchange.scratch(group),
        ],
        compiler_params=talk(collective_id, 60),
        cost_estimate=cost(0, 80 * (attn.size + up.size)),
    )(attn, up)


def halves(ref, first):
    half = ref.shape[-2] // 2
    part = pl.ds(0 if first else half, half)
    return ref.at[part] if len(ref.shape) == 2 else ref.at[:, part]


def entry_kernel(planes, group, x_ref, small_ref, out_ref, x_all, small_all, out_all, *refs):
    rows = PlaneGather(group, x_ref, x_all, *refs[:3])
    first = PlaneGather(group, halves(out_ref, True), halves(out_all, True), *refs[3:6])
    line_sems, face_sems = refs[6:]
    z_at, core_at, inner_at, mine = lax.axis_index("z"), rows.core, rows.inner, rows.mine
    greet_all(core_at, inner_at, group, planes)
    lines, faces = [], []
    for step in range(1, planes):
        copy = pltpu.make_async_remote_copy(
            src_ref=small_ref,
            dst_ref=small_all.at[mine, z_at],
            send_sem=line_sems.at[0, step],
            recv_sem=line_sems.at[1, step],
            device_id={"z": lax.rem(z_at + step, planes)},
            device_id_type=MESH,
        )
        copy.start()
        lines.append(copy)
    rows.start()
    small_all[mine, z_at] = small_ref[...]
    for copy in lines:
        copy.wait()
    face = small_all.at[mine]
    for step in range(1, 2 * group):
        core, inner = other_device(core_at, inner_at, group, step)
        copy = send(face, face, face_sems.at[0, step], face_sems.at[1, step], core, inner)
        copy.start()
        faces.append(copy)
    rows.relay()
    first.start()
    rows.finish()
    first.relay()
    first.finish()
    for step in range(1, 2 * group):
        core = lax.rem(core_at + step // group, 2)
        face = small_all.at[core * group + lax.rem(inner_at - step % group + group, group)]
        send(face, face, face_sems.at[0, step], face_sems.at[1, step], core_at, inner_at).wait_recv()
    for copy in faces:
        copy.wait_send()


def entry(x, small, out_own, planes, group, collective_id):
    team = 2 * group
    return pl.pallas_call(
        functools.partial(entry_kernel, planes, group),
        out_shape=[
            jax.ShapeDtypeStruct((team, *x.shape), x.dtype),
            jax.ShapeDtypeStruct((team, planes, *small.shape), small.dtype),
            jax.ShapeDtypeStruct((team, *out_own.shape), out_own.dtype),
        ],
        in_specs=[ANY, LOCAL, ANY],
        out_specs=[ANY, LOCAL, ANY],
        scratch_shapes=[
            *PlaneGather.scratch(group),
            *PlaneGather.scratch(group),
            pltpu.SemaphoreType.DMA((2, planes)),
            pltpu.SemaphoreType.DMA((2, team)),
        ],
        compiler_params=talk(collective_id, 60),
        cost_estimate=cost(0, 400 * x.size),
    )(x, small, out_own)


def chunks(ref, do):
    rows = math.gcd(ref.shape[0], 64)

    @pl.loop(0, ref.shape[0] // rows)
    def _(at):
        do(pl.ds(pl.multiple_of(at * rows, rows), rows))


GAIN_ONE, SHIFT_ONE, BIAS_Q, BIAS_V, BIAS_O, GAIN_TWO, SHIFT_TWO, BIAS_DOWN = range(8)


def line(params_ref, at):
    return params_ref[at : at + 1, :]


def close_attention(inner_at, own_ref, ins, outs):
    x_ref, params_ref = ins
    attended_ref, low_ref = outs

    def do(rows):
        value = x_ref[rows, :].astype(f32) + own_ref[rows, :] + line(params_ref, BIAS_O)
        attended_ref[rows, :] = value
        normed = unit_norm(value)[0] * line(params_ref, GAIN_TWO) + line(params_ref, SHIFT_TWO)
        low_ref[rows, :] = normed.astype(bf16)

    chunks(own_ref, do)


def add_sums(sums_ref, *terms):
    for i, term in enumerate(terms):
        sums_ref[i : i + 1, :] += jnp.sum(term, axis=0, keepdims=True)


def close_second(inner_at, own_ref, ins, outs):
    attended_ref, out_ref, params_ref = ins
    after_ref, low_ref, sums_ref = outs
    sums_ref[...] = jnp.zeros_like(sums_ref)

    def do(rows):
        unit, inverse = unit_norm(attended_ref[rows, :])
        grad = own_ref[rows, :]
        value = out_ref[rows, :].astype(f32) + normalize_back(
            grad, unit, inverse, line(params_ref, GAIN_TWO)
        )
        low = value.astype(bf16)
        after_ref[rows, :] = value
        low_ref[rows, :] = low
        add_sums(sums_ref, grad * unit, grad, low.astype(f32), out_ref[rows, :].astype(f32))

    chunks(own_ref, do)


def close_first(inner_at, own_ref, ins, outs):
    x_ref, params_ref, after_ref = ins
    grad_ref, sums_ref = outs
    sums_ref[...] = jnp.zeros_like(sums_ref)

    def do(rows):
        unit, inverse = unit_norm(x_ref[rows, :].astype(f32))
        grad = own_ref[rows, :]
        grad_ref[rows, :] = after_ref[rows, :] + normalize_back(grad, unit, inverse, line(params_ref, GAIN_ONE))
        add_sums(sums_ref, grad * unit, grad)

    chunks(own_ref, do)


def product_sum_kernel(group, planes, flip, close, ins, outs, swap, extra, a_ref, w_ref, *refs):
    in_refs, refs = refs[:ins], refs[ins:]
    ahead, refs = refs[: swap + extra], refs[swap + extra :]
    out_refs, refs = refs[:outs], refs[outs:]
    placed, refs = refs[: swap + extra], refs[swap + extra :]
    own_ref, *refs = refs
    sums, refs = refs[:6], refs[6:]
    total = PlaneSum(group, row_product(group, own_ref.shape[0], flip, a_ref, w_ref), own_ref, *sums)
    if swap:
        arrived, *refs = refs
        exchange = PlaneExchange(group, ahead[0], arrived, *refs[:2])
        lines = PlanesSum(planes, ahead[1], placed[1], *refs[2:]) if extra else None
        greet_all(total.core, total.inner, group, planes)
        if extra:
            lines.start()
        exchange.start()
    else:
        greet(total.core, total.inner, group)
    total.run()
    close(total.inner, own_ref, in_refs, out_refs)
    if swap:
        exchange.finish()
        place_columns(placed[0], arrived, 0, arrived.shape[2] // planes, planes, 2 * group)
        if extra:
            lines.finish()


def product_sum(a, w, flip, close, ins, outs, group, collective_id, planes=1, swap=None, terms=None):
    here = a.shape[0] // (2 * group)
    width = w.shape[0 if flip else 1]
    shapes = [jax.ShapeDtypeStruct((rows, width), kind) for rows, kind in outs]
    scratch = [pltpu.VMEM((here, width), f32), *PlaneSum.scratch(group, here, width)]
    ahead, places = [], []
    if swap is not None:
        ahead, places = [swap], [ANY]
        shapes.append(jax.ShapeDtypeStruct((swap.shape[1], swap.shape[0] * swap.shape[2]), swap.dtype))
        scratch += [pltpu.VMEM(swap.shape, swap.dtype), *PlaneExchange.scratch(group)]
    if terms is not None:
        ahead, places = ahead + [terms], places + [LOCAL]
        rows = terms.shape[0] // planes
        shapes.append(jax.ShapeDtypeStruct((rows, width), f32))
        scratch += PlanesSum.scratch(planes, rows, width)
    extra = terms is not None
    return pl.pallas_call(
        functools.partial(
            product_sum_kernel, group, planes, flip, close, len(ins), len(outs), len(ahead) - extra, int(extra)
        ),
        out_shape=shapes,
        in_specs=[LOCAL] * (2 + len(ins)) + places,
        out_specs=[LOCAL] * len(shapes),
        scratch_shapes=scratch,
        compiler_params=talk(collective_id, 60),
        cost_estimate=cost(2 * a.shape[0] * a.shape[1] * width, 100 * a.shape[0] * width),
    )(a, w, *ins, *ahead)


def attend_kernel(
    block, group, x_ref, w_ref, params_ref, qkv_bias_ref, live_ref, source, _,
    normed_ref, qkv_ref, mixed_ref, total_ref, target, bias_ref, *refs,
):
    seg_rows, heads = x_ref.shape[0] // 2, mixed_ref.shape[1] // HEAD
    gather = PlaneGather(group, halves(source, False), halves(target, False), *refs)
    greet(gather.core, gather.inner, group)
    gather.start()

    @pl.loop(0, 2 * seg_rows // block)
    def _(at):
        rows = pl.ds(pl.multiple_of(at * block, block), block)
        normed = unit_norm(x_ref[rows, :].astype(f32))[0] * line(params_ref, GAIN_ONE)
        normed = (normed + line(params_ref, SHIFT_ONE)).astype(bf16)
        normed_ref[rows, :] = normed
        qkv_ref[rows, :] = (dot(normed, w_ref[...], 1, 0) + qkv_bias_ref[...]).astype(bf16)

    for seg in range(2):
        attend_segment(block, heads, seg_rows, seg, qkv_ref, live_ref, mixed_ref, total_ref, bias_ref)
        if seg == 0:
            gather.relay()
    gather.finish()


def attend(x, w, params, qkv_bias, live, array, gathered, group, collective_id):
    rows, width = x.shape
    cols = w.shape[1] // 3
    block = 256
    local = pl.BlockSpec(memory_space=pltpu.VMEM)
    anywhere = pl.BlockSpec(memory_space=pl.ANY)
    results = pl.pallas_call(
        functools.partial(attend_kernel, block, group),
        out_shape=[
            jax.ShapeDtypeStruct((rows, width), bf16),
            jax.ShapeDtypeStruct((rows, 3 * cols), bf16),
            jax.ShapeDtypeStruct((rows, cols), bf16),
            jax.ShapeDtypeStruct((2, 8, rows // 2), f32),
            jax.ShapeDtypeStruct((2 * group, *array.shape), array.dtype),
        ],
        in_specs=[local] * 5 + [anywhere] * 2,
        out_specs=[local] * 4 + [anywhere],
        input_output_aliases={6: 4},
        scratch_shapes=[pltpu.VMEM((block, rows // 2), f32), *PlaneGather.scratch(group)],
        compiler_params=pltpu.CompilerParams(
            collective_id=collective_id, has_side_effects=True, vmem_limit_bytes=60 * 2**20
        ),
        cost_estimate=pl.CostEstimate(
            flops=rows * rows * cols + 6 * rows * width * cols, bytes_accessed=10**8, transcendentals=0
        ),
    )(x, w, params, qkv_bias[None], live.astype(f32)[:, None], array, gathered)
    return [*results[:4], results[4].reshape(-1, array.shape[-1])]


def attend_back_kernel(
    block, group, qkv_ref, first_ref, second_ref, live_ref, total_ref, params_ref, a, w, attended, normed, *refs
):
    out_ref, layer_ref, column_ref, grad_w, *refs = refs
    own_ref, a_ref, w_ref, attended_ref, load_sems, bias_ref, sums_ref, *refs = refs
    grad_ref = first_ref, second_ref
    seg_rows, heads = qkv_ref.shape[0] // 2, first_ref.shape[1] // HEAD
    cols = heads * HEAD
    loads = [
        pltpu.make_async_copy(whole, held, load_sems.at[i])
        for i, (whole, held) in enumerate(((a, a_ref), (w, w_ref), (attended, attended_ref)))
    ]
    for load in loads:
        load.start()
    strips = Strips(normed, out_ref, grad_w, *refs[:3])
    strips.start()
    total = PlaneSum(group, row_product(group, own_ref.shape[0], False, a_ref, w_ref), own_ref, *refs[3:])
    greet(total.core, total.inner, group)
    column_ref[...] = jnp.zeros_like(column_ref)
    blocks = seg_rows // block
    parts, relayed = total.order(group), False
    for seg in range(2):
        sums_ref[...] = jnp.zeros_like(sums_ref)
        for at in range(blocks):
            turn = seg * blocks + at
            if turn == 0:
                for load in loads:
                    load.wait()
            for part in parts[:2]:
                total.part(part)
            if not parts and not relayed and turn >= group + 1:
                total.relay()
                relayed = True
            parts = parts[2:]
            attend_back_rows(
                block, heads, seg_rows, seg, at, qkv_ref, grad_ref, live_ref, total_ref, out_ref, bias_ref, sums_ref
            )
        low = sums_ref[...].astype(bf16)
        out_ref[pl.ds(seg * seg_rows, seg_rows), cols:] = low
        column_ref[:, cols:] += jnp.sum(low.astype(f32), axis=0, keepdims=True)
    column_ref[:, :cols] = jnp.sum(out_ref[:, :cols].astype(f32), axis=0, keepdims=True)
    strips.run()
    total.finish()

    def do(rows):
        layer_ref[rows, :] = (
            attended_ref[rows, :] + own_ref[rows, :] + line(params_ref, BIAS_DOWN)
        ).astype(bf16)

    chunks(own_ref, do)
    strips.finish()


def attend_back(qkv, grads, live, totals, params, a, w, attended, normed, group, collective_id):
    rows, cols = qkv.shape[0], qkv.shape[1] // 3
    here, width = rows // (2 * group), w.shape[1]
    block = here
    shapes = [
        jax.ShapeDtypeStruct((rows, 3 * cols), bf16),
        jax.ShapeDtypeStruct((here, width), bf16),
        jax.ShapeDtypeStruct((1, 3 * cols), f32),
        jax.ShapeDtypeStruct((width, 3 * cols), bf16),
    ]
    scratch = [
        pltpu.VMEM((here, width), f32),
        pltpu.VMEM(a.shape, bf16),
        pltpu.VMEM(w.shape, bf16),
        pltpu.VMEM(attended.shape, f32),
        pltpu.SemaphoreType.DMA((3,)),
        pltpu.VMEM((rows // 2, block), f32),
        pltpu.VMEM((rows // 2, 2 * cols), f32),
        *Strips.scratch(rows, 3 * cols, 1024 // group),
        *PlaneSum.scratch(group, here, width),
    ]
    return pl.pallas_call(
        functools.partial(attend_back_kernel, block, group),
        out_shape=shapes,
        in_specs=[LOCAL] * 6 + [ANY] * 4,
        out_specs=[LOCAL] * 3 + [ANY],
        scratch_shapes=scratch,
        compiler_params=talk(collective_id, 63),
        cost_estimate=cost(2 * rows * rows * cols + 2 * rows * a.shape[1] * width, 10**8),
    )(qkv, *grads, live.astype(f32).reshape(rows, 1), totals, params, a, w, attended, normed)


def gelu_parts(value):
    cdf = 0.5 * (1.0 + lax.erf(value * 0.7071067811865476))
    return value * cdf, cdf + value * jnp.exp(-0.5 * value * value) * 0.3989422804014327


def gather_up_kernel(group, source, up_ref, bias_ref, all_out, act_ref, slope_ref, all_ref, out_sems, *refs):
    gather = PlaneGather(group, source, all_ref, *refs)
    greet(gather.core, gather.inner, group)
    here = source.shape[0]
    tile = math.gcd(1024, up_ref.shape[1])

    def out_copy(core, inner):
        at = core * group + inner
        return pltpu.make_async_copy(all_ref.at[at], all_out.at[at], out_sems.at[at])

    def use(core, inner):
        at = core * group + inner
        out_copy(core, inner).start()
        rows = pl.ds(pl.multiple_of(at * here, here), here)

        @pl.loop(0, up_ref.shape[1] // tile)
        def _(i):
            columns = pl.ds(pl.multiple_of(i * tile, tile), tile)
            value, slope = gelu_parts(dot(all_ref[at], up_ref[:, columns], 1, 0) + bias_ref[:, columns])
            act_ref[rows, columns] = value.astype(bf16)
            slope_ref[rows, columns] = slope.astype(bf16)

    gather.run(use)
    for at in range(2 * group):
        pltpu.make_async_copy(all_ref.at[at], all_out.at[at], out_sems.at[at]).wait()


def gather_up(array, up, bias, group, collective_id):
    here, width = array.shape
    rows, wide = 2 * group * here, up.shape[1]
    local = pl.BlockSpec(memory_space=pltpu.VMEM)
    anywhere = pl.BlockSpec(memory_space=pl.ANY)
    all_rows, act, slope = pl.pallas_call(
        functools.partial(gather_up_kernel, group),
        out_shape=[
            jax.ShapeDtypeStruct((2 * group, here, width), bf16),
            jax.ShapeDtypeStruct((rows, wide), bf16),
            jax.ShapeDtypeStruct((rows, wide), bf16),
        ],
        in_specs=[anywhere, local, local],
        out_specs=[anywhere, local, local],
        scratch_shapes=[
            pltpu.VMEM((2 * group, here, width), bf16),
            pltpu.SemaphoreType.DMA((2 * group,)),
            *PlaneGather.scratch(group),
        ],
        compiler_params=pltpu.CompilerParams(
            collective_id=collective_id, has_side_effects=True, vmem_limit_bytes=60 * 2**20
        ),
        cost_estimate=pl.CostEstimate(
            flops=2 * rows * width * wide, bytes_accessed=50 * rows * width, transcendentals=0
        ),
    )(array, up, bias[None])
    return all_rows.reshape(rows, width), act, slope


def gather_mixed_kernel(group, last, array, w_ref, mixed_ref, *refs):
    sum_in, refs = (refs[0], refs[1:]) if last else (None, refs)
    grad_mixed_ref, grad_w_ref, all_ref, sum_ref = refs[:4]
    source = halves(array, not last)
    gather = PlaneGather(group, source, all_ref, *refs[4:])
    greet(gather.core, gather.inner, group)
    rows_here = source.shape[0]
    sum_ref[...] = sum_in[...] if last else jnp.zeros_like(sum_ref)

    def use(core, inner):
        at = core * group + inner
        rows = pl.ds(pl.multiple_of(at * rows_here, rows_here), rows_here)
        grad_mixed_ref[rows, :] = dot(all_ref[at], w_ref[...], 1, 1).astype(bf16)
        start = at * 2 * rows_here + last * rows_here
        mixed = mixed_ref[pl.ds(pl.multiple_of(start, rows_here), rows_here), :]
        sum_ref[...] += dot(mixed, all_ref[at], 0, 0)

    gather.run(use)
    grad_w_ref[...] = sum_ref[...].astype(grad_w_ref.dtype)


def gather_mixed(array, w, mixed, group, collective_id, before=None):
    here, width = array.shape
    rows, cols = mixed.shape
    extra = [] if before is None else [before]
    return pl.pallas_call(
        functools.partial(gather_mixed_kernel, group, len(extra)),
        out_shape=[
            jax.ShapeDtypeStruct((rows // 2, cols), bf16),
            jax.ShapeDtypeStruct((cols, width), bf16 if extra else f32),
        ],
        in_specs=[ANY] + [LOCAL] * (2 + len(extra)),
        out_specs=[LOCAL] * 2,
        scratch_shapes=[
            pltpu.VMEM((2 * group, here // 2, width), bf16),
            pltpu.VMEM((cols, width), f32),
            *PlaneGather.scratch(group),
        ],
        compiler_params=talk(collective_id, 60),
        cost_estimate=cost(2 * rows * width * cols, 25 * rows * width),
    )(array, w, mixed, *extra)


class Strips:

    @staticmethod
    def scratch(rows, right, depth):
        return [
            pltpu.VMEM((2, rows, depth), bf16),
            pltpu.VMEM((2, depth, right), bf16),
            pltpu.SemaphoreType.DMA((2, 2)),
        ]

    def __init__(self, whole, right_ref, target, held, done, sems):
        self.whole, self.right_ref, self.target = whole, right_ref, target
        self.held, self.done, self.sems = held, done, sems
        self.depth = held.shape[2]
        self.count = whole.shape[1] // self.depth

    def strip(self, at):
        return pl.ds(pl.multiple_of(at * self.depth, self.depth), self.depth)

    def load(self, at):
        slot = lax.rem(at, 2)
        return pltpu.make_async_copy(self.whole.at[:, self.strip(at)], self.held.at[slot], self.sems.at[0, slot])

    def store(self, at):
        slot = lax.rem(at, 2)
        return pltpu.make_async_copy(self.done.at[slot], self.target.at[self.strip(at)], self.sems.at[1, slot])

    def start(self):
        for at in range(2):
            self.load(at).start()

    def run(self):
        @pl.loop(0, self.count)
        def _(at):
            slot = lax.rem(at, 2)
            self.load(at).wait()

            @pl.when(at >= 2)
            def _():
                self.store(at - 2).wait()

            self.done[slot] = dot(self.held[slot], self.right_ref[...], 0, 0).astype(bf16)
            self.store(at).start()

            @pl.when(at + 2 < self.count)
            def _():
                self.load(at + 2).start()

    def finish(self):
        for at in range(self.count - 2, self.count):
            self.store(at).wait()


def back_sum_kernel(
    group, out_live, slope, down, up, second, attended_ref, out_ref, params_ref, bias_ref,
    after_ref, low_ref, sums_ref, grad_up, grad_pre_ref, own_ref, live_v, slope_v, down_v, up_v, sems, *refs,
):
    here = own_ref.shape[0]
    wide = down.shape[0]
    tile = math.gcd(1024, wide)
    order = PlaneSum.order(group, True)

    def rows_of(core, inner):
        return pl.ds(pl.multiple_of((core * group + inner) * here, here), here)

    slots = live_v.shape[0]

    def loads(turn):
        core = total.core if order[turn] % 2 else 1 - total.core
        rows, slot = rows_of(core, total.targets[order[turn] // 2]), turn % slots
        return (
            pltpu.make_async_copy(out_live.at[rows, :], live_v.at[slot], sems.at[0, slot]),
            pltpu.make_async_copy(slope.at[rows, :], slope_v.at[slot], sems.at[1, slot]),
        )

    def start_loads(turn):
        if turn < 2 * group:
            for load in loads(turn):
                load.start()

    down_load = pltpu.make_async_copy(down, down_v, sems.at[0, slots])
    up_load = pltpu.make_async_copy(up, up_v, sems.at[1, slots])

    def prepare(core, inner, at):
        turn = order.index(at)
        slot = turn % slots
        for load in loads(turn):
            load.wait()
        if turn == 0:
            down_load.wait()
        else:
            start_loads(turn + slots - 1)
        rows = rows_of(core, inner)

        @pl.loop(0, wide // tile)
        def _(i):
            columns = pl.ds(pl.multiple_of(i * tile, tile), tile)
            value = dot(live_v[slot], down_v[columns, :], 1, 1) * slope_v[slot, :, columns].astype(f32)
            value = value.astype(bf16)
            grad_pre_ref[rows, columns] = value
            bias_ref[:, columns] += jnp.sum(value.astype(f32), axis=0, keepdims=True)

        if turn == 0:
            up_load.wait()

    strips = Strips(second, grad_pre_ref, grad_up, *refs[:3])
    total = PlaneSum(group, row_product(group, here, True, grad_pre_ref, up_v), own_ref, *refs[3:], prepare=prepare)
    down_load.start()
    for turn in range(slots):
        start_loads(turn)
        if turn == 0:
            up_load.start()
    bias_ref[...] = jnp.zeros_like(bias_ref)
    strips.start()
    greet(total.core, total.inner, group)
    total.run(True, strips.run)
    close_second(total.inner, own_ref, (attended_ref, out_ref, params_ref), (after_ref, low_ref, sums_ref))
    strips.finish()


def back_sum(out_live, slope, down, up, second, attended, out_own, params, group, collective_id):
    rows, width = out_live.shape
    here, wide = rows // (2 * group), down.shape[0]
    local = pl.BlockSpec(memory_space=pltpu.VMEM)
    anywhere = pl.BlockSpec(memory_space=pl.ANY)
    bias, grad_after, low, sums, grad_up = pl.pallas_call(
        functools.partial(back_sum_kernel, group),
        out_shape=[
            jax.ShapeDtypeStruct((1, wide), f32),
            jax.ShapeDtypeStruct((here, width), f32),
            jax.ShapeDtypeStruct((here, width), bf16),
            jax.ShapeDtypeStruct((8, width), f32),
            jax.ShapeDtypeStruct((width, wide), bf16),
        ],
        in_specs=[anywhere] * 5 + [local] * 3,
        out_specs=[local] * 4 + [anywhere],
        scratch_shapes=[
            pltpu.VMEM((rows, wide), bf16),
            pltpu.VMEM((here, width), f32),
            pltpu.VMEM((4, here, width), bf16),
            pltpu.VMEM((4, here, wide), bf16),
            pltpu.VMEM(down.shape, bf16),
            pltpu.VMEM(up.shape, bf16),
            pltpu.SemaphoreType.DMA((2, 5)),
            *Strips.scratch(rows, wide, 1024 // group),
            *PlaneSum.scratch(group, here, width),
        ],
        compiler_params=pltpu.CompilerParams(
            collective_id=collective_id, has_side_effects=True, vmem_limit_bytes=63 * 2**20
        ),
        cost_estimate=pl.CostEstimate(
            flops=4 * rows * width * wide, bytes_accessed=50 * rows * width, transcendentals=0
        ),
    )(out_live, slope, down, up, second, attended, out_own, params)
    return bias[0], grad_after, low, sums, grad_up


def closing_kernel(
    planes, group, unit, repeats, terms, attn, out_ref, *refs
):
    weight_refs, refs = refs[:3], refs[3:]
    attn_all, from_plane, summed, from_z, plane_sems, z_sems = refs[:6]
    exchange = PlaneExchange(group, attn, attn_all, *refs[6:])
    team = 2 * group
    z_at, core_at, inner_at, mine = lax.axis_index("z"), exchange.core, exchange.inner, exchange.mine
    greet_all(core_at, inner_at, group, planes)
    copies = []
    for step in range(1, team):
        core, inner = other_device(core_at, inner_at, group, step)
        copy = send(
            terms.at[core * group + inner],
            from_plane.at[step],
            plane_sems.at[0, step],
            plane_sems.at[1, step],
            core,
            inner,
        )
        copy.start()
        copies.append(copy)
    exchange.start()
    summed[...] = terms[mine]
    for copy in copies:
        copy.wait_recv()
    for step in range(1, team):
        summed[...] += from_plane[step]
    more = []
    for step in range(1, planes):
        to = lax.rem(z_at + step, planes)
        copy = pltpu.make_async_remote_copy(
            src_ref=summed.at[to],
            dst_ref=from_z.at[step],
            send_sem=z_sems.at[0, step],
            recv_sem=z_sems.at[1, step],
            device_id={"z": to},
            device_id_type=MESH,
        )
        copy.start()
        more.append(copy)
    exchange.finish()
    cols = unit * repeats
    for i in range(3):
        place_columns(weight_refs[i], attn_all, i * cols, unit, repeats, team)
    out_ref[...] = summed[z_at]
    for step, copy in enumerate(more, 1):
        copy.wait_recv()
        out_ref[...] += from_z[step]
    for copy in copies + more:
        copy.wait_send()


def closing(terms, attn, planes, group, unit, collective_id):
    team, _, lines, _ = terms.shape
    rows, cols = attn.shape[1], attn.shape[2] // 3
    weight = jax.ShapeDtypeStruct((rows, cols * team), bf16)
    return pl.pallas_call(
        functools.partial(closing_kernel, planes, group, unit, cols // unit),
        out_shape=[
            jax.ShapeDtypeStruct((lines, 128), f32),
            weight,
            weight,
            weight,
        ],
        in_specs=[LOCAL, ANY],
        out_specs=[LOCAL] * 4,
        scratch_shapes=[
            pltpu.VMEM(attn.shape, bf16),
            pltpu.VMEM((team, planes, lines, 128), f32),
            pltpu.VMEM((planes, lines, 128), f32),
            pltpu.VMEM((planes, lines, 128), f32),
            pltpu.SemaphoreType.DMA((2, team)),
            pltpu.SemaphoreType.DMA((2, planes)),
            *PlaneExchange.scratch(group),
        ],
        compiler_params=talk(collective_id, 40),
        cost_estimate=cost(0, 10**8),
    )(terms, attn)


def body(
    layer_input,
    first_gain,
    first_shift,
    query_weight,
    key_weight,
    value_weight,
    output_weight,
    query_bias,
    value_bias,
    output_bias,
    second_gain,
    second_shift,
    up_weight,
    up_bias,
    down_weight,
    down_bias,
    segment_counts,
    out_grad,
):
    here, width = layer_input.shape
    wide = up_weight.shape[1]
    planes = lax.axis_size("z")
    group = lax.axis_size("fsdp")
    team = 2 * group
    z_at, core_at, inner_at = (lax.axis_index(name) for name in ALL)
    plane_at = core_at * group + inner_at
    seg_rows = here * group
    own_rows = query_weight.shape[0]
    own_wide = down_weight.shape[0]
    cols = width // team
    heads_here = cols // HEAD
    whole_heads = own_rows % HEAD == 0

    def to_columns(weight, unit):
        cut = weight.reshape(weight.shape[0], planes, team, unit)
        return cut.transpose(2, 0, 1, 3).reshape(team, weight.shape[0], planes * unit)

    def head_columns(weight):
        if whole_heads:
            return to_columns(weight, own_rows)
        return weight.reshape(own_rows, team, cols).transpose(1, 0, 2)

    attn_blocks = jnp.concatenate([head_columns(w) for w in (query_weight, key_weight, value_weight)], axis=2)
    out_here = z_gather(output_weight) if whole_heads else lax.all_gather(output_weight, ALL, axis=0, tiled=True)
    attn_cols, up_cols = plane_exchange(attn_blocks, up_weight, own_wide, planes, group, 0)
    attn_cols = attn_cols.reshape(team * own_rows, 3 * cols)
    up_cols = up_cols.reshape(team * own_rows, wide // team)
    attn_full = z_gather(after(attn_cols, out_here))
    small = jnp.concatenate(
        [first_gain, first_shift, query_bias, value_bias, output_bias, second_gain, second_shift, down_bias, up_bias]
    )
    length = small.shape[0]
    small = jnp.pad(small.astype(f32), (0, -length % 1024)).reshape(-1, 128)
    segment = 2 * z_at + jnp.arange(2, dtype=jnp.int32)
    place = segment % MAXSEG
    present = place < segment_counts[segment // MAXSEG]
    pos = jnp.arange(seg_rows, dtype=jnp.int32)
    live = present[:, None] & ((pos >= PRE)[None] | (place[:, None] >= PREV - pos[None] // SUMM))
    live_own = lax.dynamic_slice(live, (core_at, inner_at * here), (1, here))[0]
    out_own = jnp.where(live_own[:, None], out_grad, jnp.zeros_like(out_grad))
    all_rows, small_all, out_live = entry(after(layer_input, up_cols), small, out_own, planes, group, 1)
    all_rows = all_rows.reshape(-1, width)
    small_all = small_all.swapaxes(0, 1).reshape(planes * team, -1)
    params = small_all[:, : 8 * own_rows].reshape(planes * team, 8, own_rows).swapaxes(0, 1).reshape(8, width)
    bias_up = small_all[:, 8 * own_rows : length].reshape(planes, team, own_wide)[:, plane_at].reshape(wide // team)

    def own_columns(bias):
        if whole_heads:
            return bias.reshape(planes, team, own_rows)[:, plane_at].reshape(cols)
        return lax.dynamic_slice_in_dim(bias, plane_at * cols, cols)

    bias_q, bias_v = own_columns(params[BIAS_Q]), own_columns(params[BIAS_V])
    out_full = out_here if whole_heads else lax.dynamic_slice_in_dim(out_here, plane_at * cols, cols)
    up_full = z_gather(up_cols)
    down_full = z_gather(after(down_weight, up_cols))
    normed_low, qkv, mixed_low, totals, out_live = attend(
        all_rows,
        attn_full,
        params,
        jnp.concatenate([bias_q, jnp.zeros_like(bias_q), bias_v]),
        live,
        out_own,
        out_live,
        group,
        11,
    )
    out_live = out_live.reshape(-1, width)
    attended, second_own = product_sum(
        mixed_low,
        out_full,
        False,
        close_attention,
        [layer_input, params],
        [(here, f32), (here, bf16)],
        group,
        2,
    )
    second_low, activated, slope = gather_up(second_own, up_full, bias_up, group, 3)
    grad_down = dot(activated, out_live, 0, 0).astype(bf16)
    out_live = after(out_live, grad_down)
    grad_down = z_sum(grad_down)
    grad_up_bias, grad_after, after_low_own, second_sums, grad_up = back_sum(
        out_live, slope, down_full, up_full, second_low, attended, out_own, params, group, 5
    )
    first_mixed, first_output = gather_mixed(after_low_own, out_full, mixed_low, group, 6)
    grad_up = z_sum(after(grad_up, grad_down, first_mixed)).reshape(team, own_rows, wide // team)
    second_mixed, grad_output = gather_mixed(after_low_own, out_full, mixed_low, group, 7, first_output)
    grad_qkv, layer_output, grad_bias, grad_attn = attend_back(
        qkv, (first_mixed, second_mixed), live, totals, params, activated, down_full, attended, normed_low, group, 4
    )
    grad_bias = grad_bias[0]
    grad_attn = z_sum(after(grad_attn, grad_up)).reshape(team, own_rows, 3 * cols)
    input_grad, first_sums, grad_up, *summed = product_sum(
        grad_qkv,
        attn_full,
        True,
        close_first,
        [layer_input, params, grad_after],
        [(here, f32), (8, f32)],
        group,
        8,
        planes,
        grad_up,
        grad_output if whole_heads else None,
    )
    own_pos = inner_at * here + jnp.arange(here, dtype=jnp.int32)
    input_grad = jnp.where((own_pos >= SUMM)[:, None], input_grad, 0.0)

    if not whole_heads:
        spread = jnp.zeros((width, width), bf16)
        spread = lax.dynamic_update_slice_in_dim(spread, grad_output.astype(bf16), plane_at * cols, 0)
        grad_output = lax.psum_scatter(spread, ALL, scatter_dimension=0, tiled=True)
    else:
        (grad_output,) = summed

    def spread_columns(bias):
        if whole_heads:
            full = jnp.zeros((planes, team, own_rows), f32)
            return lax.dynamic_update_slice(full, bias.reshape(planes, 1, own_rows), (0, plane_at, 0)).reshape(width)
        return lax.dynamic_update_slice(jnp.zeros((width,), f32), bias, (plane_at * cols,))

    sums = [
        first_sums[0],
        first_sums[1],
        spread_columns(grad_bias[:cols]),
        spread_columns(grad_bias[2 * cols :]),
        second_sums[2],
        second_sums[0],
        second_sums[1],
        second_sums[3],
    ]
    up_spread = jnp.zeros((planes, team, own_wide), f32)
    up_spread = lax.dynamic_update_slice(up_spread, grad_up_bias.reshape(planes, 1, own_wide), (0, plane_at, 0))
    packed = jnp.concatenate(
        [a.reshape(planes * team, own_rows) for a in sums] + [up_spread.reshape(planes * team, own_wide)], axis=1
    )
    packed = jnp.pad(packed, ((0, 0), (0, -length % 1024))).reshape(planes, team, -1, 128).swapaxes(0, 1)
    packed, *grad_weights = closing(
        packed, grad_attn, planes, group, own_rows if whole_heads else cols, 9
    )
    packed = packed.reshape(-1)
    small_grads = [packed[i * own_rows : (i + 1) * own_rows] for i in range(8)]
    return (
        layer_output,
        input_grad,
        small_grads[0],
        small_grads[1],
        *[weight.astype(f32) for weight in grad_weights],
        grad_output.astype(f32),
        small_grads[2],
        small_grads[3],
        small_grads[4],
        small_grads[5],
        small_grads[6],
        grad_up.astype(f32),
        packed[8 * own_rows : length],
        grad_down.astype(f32),
        small_grads[7],
    )


def solution(mesh):
    outer, inner = mesh.devices.shape
    fine = Mesh(mesh.devices.reshape(outer // 2, 2, inner), ALL)
    rows, vector = P(ALL, None), P(ALL)
    return jax.shard_map(
        body,
        mesh=fine,
        in_specs=(
            rows, vector, vector, rows, rows, rows, rows, vector, vector, vector, vector, vector,
            rows, vector, rows, vector, P(), rows,
        ),
        out_specs=(
            rows, rows, vector, vector, rows, rows, rows, rows, vector, vector, vector, vector, vector,
            rows, vector, rows, vector,
        ),
        check_vma=False,
    )
```

```python
import functools
import math

import jax
import jax.numpy as jnp
from jax import lax
from jax.experimental import pallas as pl
from jax.experimental.pallas import tpu as pltpu
from jax.sharding import Mesh, PartitionSpec as P

HEADS = 32
HEAD = 64
SUMM = 50
PREV = 3
MAXSEG = 4
PRE = 150

epsilon = 1e-05
masked = -1e30

ALL = ("z", "core", "fsdp")
PLANE = ("core", "fsdp")
bf16 = jnp.bfloat16
f32 = jnp.float32
MESH = pl.DeviceIdType.MESH


def dot(a, b, ca, cb):
    return lax.dot_general(a, b, (((ca,), (cb,)), ((), ())), preferred_element_type=f32)


def z_gather(rows):
    return lax.all_gather(rows, "z", axis=0, tiled=True)


def z_sum(partial):
    return lax.psum_scatter(partial.astype(bf16), "z", scatter_dimension=0, tiled=True)


def after(value, *earlier):
    return lax.optimization_barrier((value, *earlier))[0]


def unit_norm(values):
    center = values - jnp.mean(values, axis=-1, keepdims=True)
    inverse_std = lax.rsqrt(jnp.mean(center * center, axis=-1, keepdims=True) + epsilon)
    return center * inverse_std, inverse_std


def normalize_back(grad_rows, unit_rows, inverse_std, norm_gain):
    scaled = grad_rows * norm_gain
    centered = scaled - jnp.mean(scaled, axis=-1, keepdims=True)
    centered = centered - unit_rows * jnp.mean(scaled * unit_rows, axis=-1, keepdims=True)
    return centered * inverse_std


def head_mask(rows, cols, head):
    lane = lax.broadcasted_iota(jnp.int32, (rows, cols), 1)
    return lane // HEAD == head


def attend_segment(block, heads, seg_rows, seg, qkv_ref, live_ref, mixed_ref, total_ref, bias_ref):
    cols = heads * HEAD
    base = seg * seg_rows
    lane = lax.broadcasted_iota(jnp.int32, (block, 128), 1)
    for at in range(seg_rows // block):
        wide = (at + 1) * block
        rows = pl.ds(pl.multiple_of(base + at * block, block), block)
        keys = pl.ds(pl.multiple_of(base, seg_rows), wide)
        query_pos = at * block + lax.broadcasted_iota(jnp.int32, (block, wide), 0)
        key_pos = lax.broadcasted_iota(jnp.int32, (block, wide), 1)
        open_key = (live_ref[seg, :, :wide] > 0.0) & (key_pos < query_pos) | (key_pos == query_pos)
        bias_ref[:, :wide] = jnp.where(open_key, 0.0, masked)
        query = qkv_ref[rows, :cols] * jnp.asarray(HEAD**-0.5, bf16)
        result = jnp.zeros((block, cols), f32)
        totals = jnp.zeros((block, 128), f32)
        for head in range(heads):
            chosen = head_mask(block, cols, head)
            scores = dot(jnp.where(chosen, query, jnp.zeros_like(query)), qkv_ref[keys, cols : 2 * cols], 1, 1)
            scores = scores + bias_ref[:, :wide]
            top = jnp.max(scores, axis=1, keepdims=True)
            powers = jnp.exp(scores - top)
            total = jnp.sum(powers, axis=1, keepdims=True)
            probs = (powers * (1.0 / total)).astype(bf16)
            value = dot(probs, qkv_ref[keys, 2 * cols :], 1, 0)
            result = jnp.where(chosen, value, result)
            totals = jnp.where(lane == head, top + jnp.log(total), totals)
        mixed_ref[rows, :] = result.astype(bf16)
        total_ref[seg, :, at * block : (at + 1) * block] = totals.T[:8]


def attend_back_rows(
    block, heads, seg_rows, seg, at, qkv_ref, grad_ref, live_ref, total_ref, out_ref, bias_ref, sums_ref
):
    cols = heads * HEAD
    base = seg * seg_rows
    wide = (at + 1) * block
    rows = pl.ds(pl.multiple_of(base + at * block, block), block)
    keys = pl.ds(pl.multiple_of(base, seg_rows), wide)
    key_pos = lax.broadcasted_iota(jnp.int32, (wide, block), 0)
    query_pos = at * block + lax.broadcasted_iota(jnp.int32, (wide, block), 1)
    open_key = (live_ref[keys, :] > 0.0) & (key_pos < query_pos) | (key_pos == query_pos)
    bias_ref[:wide, :] = jnp.where(open_key, 0.0, masked)
    query = qkv_ref[rows, :cols] * jnp.asarray(HEAD**-0.5, bf16)
    half = block // 2
    part = pl.ds(pl.multiple_of((base + at * block) // 2, half), half)
    grad = jnp.concatenate([one[part, :] for one in grad_ref], axis=0)
    grad_query = jnp.zeros((block, cols), f32)
    for head in range(heads):
        chosen = head_mask(block, cols, head)
        query_one = jnp.where(chosen, query, jnp.zeros_like(query))
        grad_one = jnp.where(chosen, grad, jnp.zeros_like(grad))
        scores = dot(qkv_ref[keys, cols : 2 * cols], query_one, 1, 1)
        total = total_ref[seg, head : head + 1, at * block : (at + 1) * block]
        probs = jnp.exp(scores + bias_ref[:wide, :] - total)
        terms = probs * dot(qkv_ref[keys, 2 * cols :], grad_one, 1, 1)
        delta = jnp.sum(terms, axis=0, keepdims=True)
        grad_scores = (terms - probs * delta).astype(bf16)
        sums_ref[:wide, :cols] += dot(grad_scores, query_one, 1, 0)
        sums_ref[:wide, cols:] += dot(probs.astype(bf16), grad_one, 1, 0)
        value = dot(grad_scores, qkv_ref[keys, cols : 2 * cols], 0, 0)
        grad_query = jnp.where(chosen, value, grad_query)
    out_ref[rows, :cols] = (grad_query * HEAD**-0.5).astype(bf16)


def other_device(core_at, inner_at, group, step):
    return lax.rem(core_at + step // group, 2), lax.rem(inner_at + step % group, group)


def signal(**place):
    pl.semaphore_signal(pltpu.get_barrier_semaphore(), inc=1, device_id=place, device_id_type=MESH)


def greet(core_at, inner_at, group):
    signal(core=1 - core_at, fsdp=inner_at)
    for step in range(1, group):
        signal(core=core_at, fsdp=lax.rem(inner_at + step, group))
    pl.semaphore_wait(pltpu.get_barrier_semaphore(), group)


def greet_all(core_at, inner_at, group, planes):
    z_at = lax.axis_index("z")
    for step in range(1, 2 * group):
        core, inner = other_device(core_at, inner_at, group, step)
        signal(core=core, fsdp=inner)
    for step in range(1, planes):
        signal(z=lax.rem(z_at + step, planes))
    pl.semaphore_wait(pltpu.get_barrier_semaphore(), 2 * group + planes - 2)


def send(source, target, send_sem, recv_sem, core, inner):
    return pltpu.make_async_remote_copy(
        src_ref=source,
        dst_ref=target,
        send_sem=send_sem,
        recv_sem=recv_sem,
        device_id={"core": core, "fsdp": inner},
        device_id_type=MESH,
    )


def beside(inner_at):
    at_x = inner_at + 1 - 2 * lax.rem(inner_at, 2)
    at_y = lax.rem(inner_at + 2, 4)
    return at_x, at_y, lax.rem(at_x + 2, 4)


class PlaneGather:

    @staticmethod
    def scratch(group):
        return [pltpu.SemaphoreType.DMA((2, 2 * group)), pltpu.SemaphoreType.DMA((2, 2 * group)), pltpu.SemaphoreType.DMA]

    def __init__(self, group, source, target, chip_sems, core_sems, own_sem):
        self.group, self.source, self.target = group, source, target
        self.chip_sems, self.core_sems = chip_sems, core_sems
        self.core, self.inner = lax.axis_index("core"), lax.axis_index("fsdp")
        self.mine = self.core * group + self.inner
        self.own = pltpu.make_async_copy(source, target.at[self.mine], own_sem)
        half = source.shape[0] // 2
        self.low, self.high = pl.ds(0, half), pl.ds(half, half)
        self.sent = []

    def to_chip(self, at, source, target, inner):
        return send(source, target, self.chip_sems.at[0, at], self.chip_sems.at[1, at], self.core, inner)

    def to_core(self, at, source, target):
        return send(source, target, self.core_sems.at[0, at], self.core_sems.at[1, at], 1 - self.core, self.inner)

    def block(self, core, inner, part=None):
        at = core * self.group + inner
        return self.target.at[at] if part is None else self.target.at[at, part]

    def go(self, copy):
        copy.start()
        self.sent.append(copy)

    def start(self):
        own = self.target.at[self.mine]
        if self.group == 4:
            at_x, at_y, _ = beside(self.inner)
            self.go(self.to_chip(0, self.source, own, at_x))
            self.go(self.to_chip(1, self.source, own, at_y))
        else:
            for step in range(1, self.group):
                self.go(self.to_chip(step, self.source, own, lax.rem(self.inner + step, self.group)))
        self.go(self.to_core(0, self.source, own))
        self.own.start()

    def wait_core(self, at):
        other, low, high = 1 - self.core, self.low, self.high
        if self.group == 4:
            at_x, at_y, across = beside(self.inner)
            inner, part = ((self.inner, None), (at_x, None), (at_y, None), (across, low), (across, high))[at]
        else:
            inner, part = lax.rem(self.inner - at + self.group, self.group), None
        block = self.block(other, inner, part)
        self.to_core(at, block, block).wait_recv()

    def across(self):
        if self.group == 4:
            at_x, at_y, across = beside(self.inner)
            for at, part in ((2, self.low), (3, self.high)):
                block = self.block(self.core, across, part)
                self.to_chip(at, block, block, at_x).wait_recv()
                self.go(self.to_core(at + 1, block, block))

    def run(self, use):
        core, inner, other = self.core, self.inner, 1 - self.core
        self.start()
        self.own.wait()
        use(core, inner)
        self.wait_core(0)
        use(other, inner)
        self.relay()
        if self.group == 4:
            at_x, at_y, across = beside(inner)
            use(core, at_x)
            use(core, at_y)
            self.wait_core(1)
            use(other, at_x)
            self.wait_core(2)
            use(other, at_y)
            self.across()
            use(core, across)
            self.wait_core(3)
            self.wait_core(4)
            use(other, across)
        else:
            for step in range(1, self.group):
                use(core, lax.rem(inner - step + self.group, self.group))
            for step in range(1, self.group):
                self.wait_core(step)
                use(other, lax.rem(inner - step + self.group, self.group))
        for copy in self.sent:
            copy.wait_send()

    def relay(self):
        if self.group == 4:
            at_x, at_y, _ = beside(self.inner)
            block = self.block(self.core, at_x)
            self.to_chip(0, block, block, at_x).wait_recv()
            part = self.block(self.core, at_x, self.low)
            self.go(self.to_chip(2, part, part, at_y))
            self.go(self.to_core(1, block, block))
            block = self.block(self.core, at_y)
            self.to_chip(1, block, block, at_y).wait_recv()
            part = self.block(self.core, at_y, self.high)
            self.go(self.to_chip(3, part, part, at_x))
            self.go(self.to_core(2, block, block))
        else:
            for step in range(1, self.group):
                inner = lax.rem(self.inner - step + self.group, self.group)
                block = self.block(self.core, inner)
                self.to_chip(step, block, block, inner).wait_recv()
                self.go(self.to_core(step, block, block))

    def finish(self):
        self.across()
        for at in range(5 if self.group == 4 else self.group):
            self.wait_core(at)
        for copy in self.sent:
            copy.wait_send()
        self.own.wait()


class PlaneSum:

    @staticmethod
    def scratch(group, here, width):
        blocks, fewer = (pltpu.VMEM((count, here, width), bf16) for count in (group, group - 1))
        sems = [pltpu.SemaphoreType.DMA((2, 2 * group)), pltpu.SemaphoreType.DMA((2, group))]
        return [blocks, blocks, blocks if group == 4 else fewer, fewer, *sems]

    def __init__(self, group, product, out_ref, to_core, from_core, pair, land, chip_sems, core_sems, prepare=None):
        self.group, self.product, self.out_ref, self.prepare = group, product, out_ref, prepare
        self.to_core_ref, self.from_core_ref, self.pair, self.land = to_core, from_core, pair, land
        self.chip_sems, self.core_sems = chip_sems, core_sems
        self.core, self.inner = lax.axis_index("core"), lax.axis_index("fsdp")
        self.here, self.width = out_ref.shape
        half = self.here // 2
        self.low, self.high = pl.ds(0, half), pl.ds(half, half)
        self.tile = math.gcd(self.width, 8192 // group)
        if group == 4:
            self.across_x, self.across_y, across = beside(self.inner)
            self.targets = [across, self.across_x, self.across_y, self.inner]
        else:
            self.targets = [lax.rem(self.inner + step, group) for step in range(1, group)] + [self.inner]
        self.sent = []

    def to_chip(self, at, source, target, inner):
        return send(source, target, self.chip_sems.at[0, at], self.chip_sems.at[1, at], self.core, inner)

    def go(self, copy):
        copy.start()
        self.sent.append(copy)

    def core_copy(self, i):
        return send(
            self.to_core_ref.at[i],
            self.from_core_ref.at[i],
            self.core_sems.at[0, i],
            self.core_sems.at[1, i],
            1 - self.core,
            self.inner,
        )

    def part_core(self, i):
        if self.prepare:
            self.prepare(1 - self.core, self.targets[i], 2 * i)

        @pl.loop(0, self.width // self.tile)
        def _(at):
            columns = pl.ds(pl.multiple_of(at * self.tile, self.tile), self.tile)
            self.to_core_ref[i, :, columns] = self.product(1 - self.core, self.targets[i], columns).astype(bf16)

        self.go(self.core_copy(i))

    def part_chip(self, i):
        if self.prepare:
            self.prepare(self.core, self.targets[i], 2 * i + 1)
        self.core_copy(i).wait_recv()
        last = i == self.group - 1

        @pl.loop(0, self.width // self.tile)
        def _(at):
            columns = pl.ds(pl.multiple_of(at * self.tile, self.tile), self.tile)
            value = self.product(self.core, self.targets[i], columns) + self.from_core_ref[i, :, columns].astype(f32)
            if last:
                self.out_ref[:, columns] = value
            else:
                self.pair[i, :, columns] = value.astype(bf16)

        if last:
            return
        pair, land = self.pair, self.land
        if self.group != 4:
            self.go(self.to_chip(i, pair.at[i], land.at[i], self.targets[i]))
        elif i == 0:
            self.go(self.to_chip(0, pair.at[0, self.low], land.at[0, self.low], self.across_x))
            self.go(self.to_chip(1, pair.at[0, self.high], land.at[1, self.low], self.across_y))
        elif i == 1:
            self.go(self.to_chip(2, pair.at[1, self.low], land.at[0, self.high], self.across_x))
        else:
            self.go(self.to_chip(3, pair.at[2, self.high], land.at[1, self.high], self.across_y))

    def arrive(self, at, place, part):
        self.to_chip(at, self.pair.at[0, part], self.land.at[place, part], self.across_x).wait_recv()
        return self.land[place, part, :].astype(f32)

    def relay(self):
        if self.group != 4:
            return
        pair, land = self.pair, self.land
        value = self.arrive(0, 0, self.low) + pair[2, self.low, :].astype(f32)
        pair[3, self.low, :] = value.astype(bf16)
        self.go(self.to_chip(4, pair.at[3, self.low], land.at[2, self.low], self.across_y))
        value = self.arrive(1, 1, self.low) + pair[1, self.high, :].astype(f32)
        pair[3, self.high, :] = value.astype(bf16)
        self.go(self.to_chip(5, pair.at[3, self.high], land.at[2, self.high], self.across_x))

    def finish(self):
        out_ref = self.out_ref
        if self.group == 4:
            out_ref[self.low, :] += self.arrive(2, 0, self.high)
            out_ref[self.high, :] += self.arrive(3, 1, self.high)
            out_ref[self.low, :] += self.arrive(4, 2, self.low)
            out_ref[self.high, :] += self.arrive(5, 2, self.high)
        else:
            for i in range(self.group - 1):
                self.to_chip(i, self.pair.at[i], self.land.at[i], self.inner).wait_recv()
                out_ref[...] += self.land[i].astype(f32)
        for copy in self.sent:
            copy.wait_send()

    @staticmethod
    def order(group, eager=False):
        if eager:
            return list(range(2 * group))
        parts = [0]
        for i in range(group):
            parts += ([2 * i + 2] if i + 1 < group else []) + [2 * i + 1]
        return parts

    def part(self, at):
        (self.part_chip if at % 2 else self.part_core)(at // 2)

    def run(self, eager=False, meanwhile=None):
        for at in self.order(self.group, eager):
            self.part(at)
        self.relay()
        if meanwhile:
            meanwhile()
        self.finish()


class PlanesSum:

    @staticmethod
    def scratch(planes, rows, width):
        return [pltpu.VMEM((planes, rows, width), bf16), pltpu.SemaphoreType.DMA((2, planes))]

    def __init__(self, planes, part, source, out_ref, land, sems):
        self.columns = pl.ds(part * out_ref.shape[1], out_ref.shape[1])
        self.planes, self.source, self.out_ref, self.land, self.sems = planes, source, out_ref, land, sems
        self.z = lax.axis_index("z")
        self.sent = []

    def rows(self, z):
        count = self.out_ref.shape[0]
        return pl.ds(pl.multiple_of(z * count, count), count)

    def start(self):
        for step in range(1, self.planes):
            to = lax.rem(self.z + step, self.planes)
            copy = pltpu.make_async_remote_copy(
                src_ref=self.source.at[self.rows(to), self.columns],
                dst_ref=self.land.at[step],
                send_sem=self.sems.at[0, step],
                recv_sem=self.sems.at[1, step],
                device_id={"z": to},
                device_id_type=MESH,
            )
            copy.start()
            self.sent.append(copy)

    def finish(self):
        self.out_ref[...] = self.source[self.rows(self.z), self.columns].astype(f32)
        for step, copy in enumerate(self.sent, 1):
            copy.wait()
            self.out_ref[...] += self.land[step].astype(f32)


def place_columns(out_ref, blocks, base, unit, planes, team):
    several = max(1, 128 // unit)
    for z in range(planes):
        for p in range(0, team, several):
            parts = [blocks[p + i, :, base + z * unit : base + (z + 1) * unit] for i in range(several)]
            value = parts[0] if several == 1 else jnp.concatenate(parts, axis=1)
            start = (z * team + p) * unit
            out_ref[:, start : start + unit * several] = value


def row_product(group, here, flip, a_ref, w_ref):
    def product(core, inner, columns):
        rows = a_ref[pl.ds(pl.multiple_of((core * group + inner) * here, here), here), :]
        if flip:
            return dot(rows, w_ref[columns, :], 1, 1)
        return dot(rows, w_ref[:, columns], 1, 0)

    return product


class PlaneExchange:

    @staticmethod
    def scratch(group):
        return [pltpu.SemaphoreType.DMA((2, 2 * group)), pltpu.SemaphoreType.DMA]

    def __init__(self, group, source, target, sems, own_sem):
        self.group, self.source, self.target, self.sems = group, source, target, sems
        self.core, self.inner = lax.axis_index("core"), lax.axis_index("fsdp")
        self.mine = self.core * group + self.inner
        self.own = pltpu.make_async_copy(source.at[self.mine], target.at[self.mine], own_sem)
        self.sent = []

    def start(self):
        for step in range(1, 2 * self.group):
            core, inner = other_device(self.core, self.inner, self.group, step)
            copy = send(
                self.source.at[core * self.group + inner],
                self.target.at[self.mine],
                self.sems.at[0, step],
                self.sems.at[1, step],
                core,
                inner,
            )
            copy.start()
            self.sent.append(copy)
        self.own.start()

    def start_cut(self, whole, unit, repeats):
        team = 2 * self.group
        for p in range(team):
            for r in range(repeats):
                start = (r * team + p) * unit
                self.source[p, :, r * unit : (r + 1) * unit] = whole[:, start : start + unit]
        self.start()

    def finish(self):
        group = self.group
        for step in range(1, 2 * group):
            core = lax.rem(self.core + step // group, 2)
            inner = lax.rem(self.inner - step % group + group, group)
            block = self.target.at[core * group + inner]
            send(block, block, self.sems.at[0, step], self.sems.at[1, step], core, inner).wait_recv()
        for copy in self.sent:
            copy.wait_send()
        self.own.wait()


ANY = pl.BlockSpec(memory_space=pl.ANY)
LOCAL = pl.BlockSpec(memory_space=pltpu.VMEM)


def talk(collective_id, megabytes):
    return pltpu.CompilerParams(
        collective_id=collective_id, has_side_effects=True, vmem_limit_bytes=megabytes * 2**20
    )


def cost(flops, bytes_accessed):
    return pl.CostEstimate(flops=flops, bytes_accessed=bytes_accessed, transcendentals=0)


def swap_kernel(group, unit, repeats, attn, up, attn_all, up_all, up_blocks, *refs):
    first = PlaneExchange(group, attn, attn_all, *refs[:2])
    second = PlaneExchange(group, up_blocks, up_all, *refs[2:])
    greet_all(first.core, first.inner, group, 1)
    first.start()
    second.start_cut(up, unit, repeats)
    first.finish()
    second.finish()


def plane_exchange(attn, up, unit, repeats, group, collective_id):
    team = 2 * group
    blocks = jax.ShapeDtypeStruct((team, up.shape[0], unit * repeats), up.dtype)
    return pl.pallas_call(
        functools.partial(swap_kernel, group, unit, repeats),
        out_shape=[jax.ShapeDtypeStruct(attn.shape, attn.dtype), blocks],
        in_specs=[ANY, LOCAL],
        out_specs=[ANY, ANY],
        scratch_shapes=[
            pltpu.VMEM(blocks.shape, blocks.dtype),
            *PlaneExchange.scratch(group),
            *PlaneExchange.scratch(group),
        ],
        compiler_params=talk(collective_id, 60),
        cost_estimate=cost(0, 80 * (attn.size + up.size)),
    )(attn, up)


def halves(ref, first):
    half = ref.shape[-2] // 2
    part = pl.ds(0 if first else half, half)
    return ref.at[part] if len(ref.shape) == 2 else ref.at[:, part]


def entry_kernel(planes, group, x_ref, small_ref, out_ref, x_all, small_all, out_all, *refs):
    rows = PlaneGather(group, x_ref, x_all, *refs[:3])
    first = PlaneGather(group, halves(out_ref, True), halves(out_all, True), *refs[3:6])
    line_sems, face_sems = refs[6:]
    z_at, core_at, inner_at, mine = lax.axis_index("z"), rows.core, rows.inner, rows.mine
    greet_all(core_at, inner_at, group, planes)
    lines, faces = [], []
    for step in range(1, planes):
        copy = pltpu.make_async_remote_copy(
            src_ref=small_ref,
            dst_ref=small_all.at[mine, z_at],
            send_sem=line_sems.at[0, step],
            recv_sem=line_sems.at[1, step],
            device_id={"z": lax.rem(z_at + step, planes)},
            device_id_type=MESH,
        )
        copy.start()
        lines.append(copy)
    rows.start()
    small_all[mine, z_at] = small_ref[...]
    for copy in lines:
        copy.wait()
    face = small_all.at[mine]
    for step in range(1, 2 * group):
        core, inner = other_device(core_at, inner_at, group, step)
        copy = send(face, face, face_sems.at[0, step], face_sems.at[1, step], core, inner)
        copy.start()
        faces.append(copy)
    rows.relay()
    first.start()
    rows.finish()
    first.relay()
    first.finish()
    for step in range(1, 2 * group):
        core = lax.rem(core_at + step // group, 2)
        face = small_all.at[core * group + lax.rem(inner_at - step % group + group, group)]
        send(face, face, face_sems.at[0, step], face_sems.at[1, step], core_at, inner_at).wait_recv()
    for copy in faces:
        copy.wait_send()


def entry(x, small, out_own, planes, group, collective_id):
    team = 2 * group
    return pl.pallas_call(
        functools.partial(entry_kernel, planes, group),
        out_shape=[
            jax.ShapeDtypeStruct((team, *x.shape), x.dtype),
            jax.ShapeDtypeStruct((team, planes, *small.shape), small.dtype),
            jax.ShapeDtypeStruct((team, *out_own.shape), out_own.dtype),
        ],
        in_specs=[ANY, LOCAL, ANY],
        out_specs=[ANY, LOCAL, ANY],
        scratch_shapes=[
            *PlaneGather.scratch(group),
            *PlaneGather.scratch(group),
            pltpu.SemaphoreType.DMA((2, planes)),
            pltpu.SemaphoreType.DMA((2, team)),
        ],
        compiler_params=talk(collective_id, 60),
        cost_estimate=cost(0, 400 * x.size),
    )(x, small, out_own)


def chunks(ref, do):
    rows = math.gcd(ref.shape[0], 64)

    @pl.loop(0, ref.shape[0] // rows)
    def _(at):
        do(pl.ds(pl.multiple_of(at * rows, rows), rows))


GAIN_ONE, SHIFT_ONE, BIAS_Q, BIAS_V, BIAS_O, GAIN_TWO, SHIFT_TWO, BIAS_DOWN = range(8)


def line(params_ref, at):
    return params_ref[at : at + 1, :]


def close_attention(inner_at, own_ref, ins, outs):
    x_ref, params_ref = ins
    attended_ref, low_ref = outs

    def do(rows):
        value = x_ref[rows, :].astype(f32) + own_ref[rows, :] + line(params_ref, BIAS_O)
        attended_ref[rows, :] = value
        normed = unit_norm(value)[0] * line(params_ref, GAIN_TWO) + line(params_ref, SHIFT_TWO)
        low_ref[rows, :] = normed.astype(bf16)

    chunks(own_ref, do)


def add_sums(sums_ref, *terms):
    for i, term in enumerate(terms):
        sums_ref[i : i + 1, :] += jnp.sum(term, axis=0, keepdims=True)


def close_second(inner_at, own_ref, ins, outs):
    attended_ref, out_ref, params_ref = ins
    after_ref, low_ref, sums_ref = outs
    sums_ref[...] = jnp.zeros_like(sums_ref)

    def do(rows):
        unit, inverse = unit_norm(attended_ref[rows, :])
        grad = own_ref[rows, :]
        value = out_ref[rows, :].astype(f32) + normalize_back(
            grad, unit, inverse, line(params_ref, GAIN_TWO)
        )
        low = value.astype(bf16)
        after_ref[rows, :] = value
        low_ref[rows, :] = low
        add_sums(sums_ref, grad * unit, grad, low.astype(f32), out_ref[rows, :].astype(f32))

    chunks(own_ref, do)


def close_first(inner_at, own_ref, ins, outs):
    x_ref, params_ref, after_ref = ins
    grad_ref, sums_ref = outs
    sums_ref[...] = jnp.zeros_like(sums_ref)

    def do(rows):
        unit, inverse = unit_norm(x_ref[rows, :].astype(f32))
        grad = own_ref[rows, :]
        grad_ref[rows, :] = after_ref[rows, :] + normalize_back(grad, unit, inverse, line(params_ref, GAIN_ONE))
        add_sums(sums_ref, grad * unit, grad)

    chunks(own_ref, do)


def product_sum_kernel(group, planes, flip, close, ins, outs, swap, extra, a_ref, w_ref, *refs):
    in_refs, refs = refs[:ins], refs[ins:]
    ahead, refs = refs[: swap + extra], refs[swap + extra :]
    out_refs, refs = refs[:outs], refs[outs:]
    placed, refs = refs[: swap + extra], refs[swap + extra :]
    own_ref, *refs = refs
    sums, refs = refs[:6], refs[6:]
    total = PlaneSum(group, row_product(group, own_ref.shape[0], flip, a_ref, w_ref), own_ref, *sums)
    if swap:
        arrived, *refs = refs
        exchange = PlaneExchange(group, ahead[0], arrived, *refs[:2])
        lines = PlanesSum(planes, 0, ahead[1], placed[1], *refs[2:]) if extra else None
        greet_all(total.core, total.inner, group, planes)
        if extra:
            lines.start()
        exchange.start()
    else:
        greet(total.core, total.inner, group)
    total.run()
    close(total.inner, own_ref, in_refs, out_refs)
    if swap:
        exchange.finish()
        place_columns(placed[0], arrived, 0, arrived.shape[2] // planes, planes, 2 * group)
        if extra:
            lines.finish()


def product_sum(a, w, flip, close, ins, outs, group, collective_id, planes=1, swap=None, terms=None):
    here = a.shape[0] // (2 * group)
    width = w.shape[0 if flip else 1]
    shapes = [jax.ShapeDtypeStruct((rows, width), kind) for rows, kind in outs]
    scratch = [pltpu.VMEM((here, width), f32), *PlaneSum.scratch(group, here, width)]
    ahead, places = [], []
    if swap is not None:
        ahead, places = [swap], [ANY]
        shapes.append(jax.ShapeDtypeStruct((swap.shape[1], swap.shape[0] * swap.shape[2]), swap.dtype))
        scratch += [pltpu.VMEM(swap.shape, swap.dtype), *PlaneExchange.scratch(group)]
    if terms is not None:
        ahead, places = ahead + [terms], places + [LOCAL]
        rows = terms.shape[0] // planes
        shapes.append(jax.ShapeDtypeStruct((rows, width // 2), f32))
        scratch += PlanesSum.scratch(planes, rows, width // 2)
    extra = terms is not None
    return pl.pallas_call(
        functools.partial(
            product_sum_kernel, group, planes, flip, close, len(ins), len(outs), len(ahead) - extra, int(extra)
        ),
        out_shape=shapes,
        in_specs=[LOCAL] * (2 + len(ins)) + places,
        out_specs=[LOCAL] * len(shapes),
        scratch_shapes=scratch,
        compiler_params=talk(collective_id, 60),
        cost_estimate=cost(2 * a.shape[0] * a.shape[1] * width, 100 * a.shape[0] * width),
    )(a, w, *ins, *ahead)


def attend_kernel(
    block, group, x_ref, w_ref, params_ref, qkv_bias_ref, live_ref, source, _,
    normed_ref, qkv_ref, mixed_ref, total_ref, target, bias_ref, *refs,
):
    seg_rows, heads = x_ref.shape[0] // 2, mixed_ref.shape[1] // HEAD
    gather = PlaneGather(group, halves(source, False), halves(target, False), *refs)
    greet(gather.core, gather.inner, group)
    gather.start()

    @pl.loop(0, 2 * seg_rows // block)
    def _(at):
        rows = pl.ds(pl.multiple_of(at * block, block), block)
        normed = unit_norm(x_ref[rows, :].astype(f32))[0] * line(params_ref, GAIN_ONE)
        normed = (normed + line(params_ref, SHIFT_ONE)).astype(bf16)
        normed_ref[rows, :] = normed
        qkv_ref[rows, :] = (dot(normed, w_ref[...], 1, 0) + qkv_bias_ref[...]).astype(bf16)

    for seg in range(2):
        attend_segment(block, heads, seg_rows, seg, qkv_ref, live_ref, mixed_ref, total_ref, bias_ref)
        if seg == 0:
            gather.relay()
    gather.finish()


def attend(x, w, params, qkv_bias, live, array, gathered, group, collective_id):
    rows, width = x.shape
    cols = w.shape[1] // 3
    block = 256
    local = pl.BlockSpec(memory_space=pltpu.VMEM)
    anywhere = pl.BlockSpec(memory_space=pl.ANY)
    results = pl.pallas_call(
        functools.partial(attend_kernel, block, group),
        out_shape=[
            jax.ShapeDtypeStruct((rows, width), bf16),
            jax.ShapeDtypeStruct((rows, 3 * cols), bf16),
            jax.ShapeDtypeStruct((rows, cols), bf16),
            jax.ShapeDtypeStruct((2, 8, rows // 2), f32),
            jax.ShapeDtypeStruct((2 * group, *array.shape), array.dtype),
        ],
        in_specs=[local] * 5 + [anywhere] * 2,
        out_specs=[local] * 4 + [anywhere],
        input_output_aliases={6: 4},
        scratch_shapes=[pltpu.VMEM((block, rows // 2), f32), *PlaneGather.scratch(group)],
        compiler_params=pltpu.CompilerParams(
            collective_id=collective_id, has_side_effects=True, vmem_limit_bytes=60 * 2**20
        ),
        cost_estimate=pl.CostEstimate(
            flops=rows * rows * cols + 6 * rows * width * cols, bytes_accessed=10**8, transcendentals=0
        ),
    )(x, w, params, qkv_bias[None], live.astype(f32)[:, None], array, gathered)
    return [*results[:4], results[4].reshape(-1, array.shape[-1])]


def attend_back_kernel(
    block, group, qkv_ref, first_ref, second_ref, live_ref, total_ref, a, w, normed, *refs
):
    out_ref, own_ref, column_ref, grad_w, *refs = refs
    a_ref, w_ref, load_sems, bias_ref, sums_ref, *refs = refs
    grad_ref = first_ref, second_ref
    seg_rows, heads = qkv_ref.shape[0] // 2, first_ref.shape[1] // HEAD
    cols = heads * HEAD
    loads = [
        pltpu.make_async_copy(whole, held, load_sems.at[i])
        for i, (whole, held) in enumerate(((a, a_ref), (w, w_ref)))
    ]
    for load in loads:
        load.start()
    strips = Strips(normed, out_ref, grad_w, *refs[:3])
    strips.start()
    total = PlaneSum(group, row_product(group, own_ref.shape[0], False, a_ref, w_ref), own_ref, *refs[3:])
    greet(total.core, total.inner, group)
    column_ref[...] = jnp.zeros_like(column_ref)
    blocks = seg_rows // block
    parts, relayed = total.order(group), False
    for seg in range(2):
        sums_ref[...] = jnp.zeros_like(sums_ref)
        for at in range(blocks):
            turn = seg * blocks + at
            if turn == 0:
                for load in loads:
                    load.wait()
            for part in parts[:2]:
                total.part(part)
            if not parts and not relayed and turn >= group + 1:
                total.relay()
                relayed = True
            parts = parts[2:]
            attend_back_rows(
                block, heads, seg_rows, seg, at, qkv_ref, grad_ref, live_ref, total_ref, out_ref, bias_ref, sums_ref
            )
        low = sums_ref[...].astype(bf16)
        out_ref[pl.ds(seg * seg_rows, seg_rows), cols:] = low
        column_ref[:, cols:] += jnp.sum(low.astype(f32), axis=0, keepdims=True)
    column_ref[:, :cols] = jnp.sum(out_ref[:, :cols].astype(f32), axis=0, keepdims=True)
    strips.run()
    total.finish()
    strips.finish()


def attend_back(qkv, grads, live, totals, a, w, normed, group, collective_id):
    rows, cols = qkv.shape[0], qkv.shape[1] // 3
    here, width = rows // (2 * group), w.shape[1]
    block = here
    shapes = [
        jax.ShapeDtypeStruct((rows, 3 * cols), bf16),
        jax.ShapeDtypeStruct((here, width), f32),
        jax.ShapeDtypeStruct((1, 3 * cols), f32),
        jax.ShapeDtypeStruct((width, 3 * cols), bf16),
    ]
    scratch = [
        pltpu.VMEM(a.shape, bf16),
        pltpu.VMEM(w.shape, bf16),
        pltpu.SemaphoreType.DMA((2,)),
        pltpu.VMEM((rows // 2, block), f32),
        pltpu.VMEM((rows // 2, 2 * cols), f32),
        *Strips.scratch(rows, 3 * cols, 1024 // group),
        *PlaneSum.scratch(group, here, width),
    ]
    return pl.pallas_call(
        functools.partial(attend_back_kernel, block, group),
        out_shape=shapes,
        in_specs=[LOCAL] * 5 + [ANY] * 3,
        out_specs=[LOCAL] * 3 + [ANY],
        scratch_shapes=scratch,
        compiler_params=talk(collective_id, 63),
        cost_estimate=cost(2 * rows * rows * cols + 2 * rows * a.shape[1] * width, 10**8),
    )(qkv, *grads, live.astype(f32).reshape(rows, 1), totals, a, w, normed)


def gelu_parts(value):
    cdf = 0.5 * (1.0 + lax.erf(value * 0.7071067811865476))
    return value * cdf, cdf + value * jnp.exp(-0.5 * value * value) * 0.3989422804014327


def gather_up_kernel(group, source, up_ref, bias_ref, all_out, act_ref, slope_ref, all_ref, out_sems, *refs):
    gather = PlaneGather(group, source, all_ref, *refs)
    greet(gather.core, gather.inner, group)
    here = source.shape[0]
    tile = math.gcd(1024, up_ref.shape[1])

    def out_copy(core, inner):
        at = core * group + inner
        return pltpu.make_async_copy(all_ref.at[at], all_out.at[at], out_sems.at[at])

    def use(core, inner):
        at = core * group + inner
        out_copy(core, inner).start()
        rows = pl.ds(pl.multiple_of(at * here, here), here)

        @pl.loop(0, up_ref.shape[1] // tile)
        def _(i):
            columns = pl.ds(pl.multiple_of(i * tile, tile), tile)
            value, slope = gelu_parts(dot(all_ref[at], up_ref[:, columns], 1, 0) + bias_ref[:, columns])
            act_ref[rows, columns] = value.astype(bf16)
            slope_ref[rows, columns] = slope.astype(bf16)

    gather.run(use)
    for at in range(2 * group):
        pltpu.make_async_copy(all_ref.at[at], all_out.at[at], out_sems.at[at]).wait()


def gather_up(array, up, bias, group, collective_id):
    here, width = array.shape
    rows, wide = 2 * group * here, up.shape[1]
    local = pl.BlockSpec(memory_space=pltpu.VMEM)
    anywhere = pl.BlockSpec(memory_space=pl.ANY)
    all_rows, act, slope = pl.pallas_call(
        functools.partial(gather_up_kernel, group),
        out_shape=[
            jax.ShapeDtypeStruct((2 * group, here, width), bf16),
            jax.ShapeDtypeStruct((rows, wide), bf16),
            jax.ShapeDtypeStruct((rows, wide), bf16),
        ],
        in_specs=[anywhere, local, local],
        out_specs=[anywhere, local, local],
        scratch_shapes=[
            pltpu.VMEM((2 * group, here, width), bf16),
            pltpu.SemaphoreType.DMA((2 * group,)),
            *PlaneGather.scratch(group),
        ],
        compiler_params=pltpu.CompilerParams(
            collective_id=collective_id, has_side_effects=True, vmem_limit_bytes=60 * 2**20
        ),
        cost_estimate=pl.CostEstimate(
            flops=2 * rows * width * wide, bytes_accessed=50 * rows * width, transcendentals=0
        ),
    )(array, up, bias[None])
    return all_rows.reshape(rows, width), act, slope


def gather_mixed_kernel(group, last, array, w_ref, mixed_ref, *refs):
    sum_in, refs = (refs[0], refs[1:]) if last else (None, refs)
    grad_mixed_ref, grad_w_ref, all_ref, sum_ref = refs[:4]
    source = halves(array, not last)
    gather = PlaneGather(group, source, all_ref, *refs[4:])
    greet(gather.core, gather.inner, group)
    rows_here = source.shape[0]
    sum_ref[...] = sum_in[...] if last else jnp.zeros_like(sum_ref)

    def use(core, inner):
        at = core * group + inner
        rows = pl.ds(pl.multiple_of(at * rows_here, rows_here), rows_here)
        grad_mixed_ref[rows, :] = dot(all_ref[at], w_ref[...], 1, 1).astype(bf16)
        start = at * 2 * rows_here + last * rows_here
        mixed = mixed_ref[pl.ds(pl.multiple_of(start, rows_here), rows_here), :]
        sum_ref[...] += dot(mixed, all_ref[at], 0, 0)

    gather.run(use)
    grad_w_ref[...] = sum_ref[...].astype(grad_w_ref.dtype)


def gather_mixed(array, w, mixed, group, collective_id, before=None):
    here, width = array.shape
    rows, cols = mixed.shape
    extra = [] if before is None else [before]
    return pl.pallas_call(
        functools.partial(gather_mixed_kernel, group, len(extra)),
        out_shape=[
            jax.ShapeDtypeStruct((rows // 2, cols), bf16),
            jax.ShapeDtypeStruct((cols, width), bf16 if extra else f32),
        ],
        in_specs=[ANY] + [LOCAL] * (2 + len(extra)),
        out_specs=[LOCAL] * 2,
        scratch_shapes=[
            pltpu.VMEM((2 * group, here // 2, width), bf16),
            pltpu.VMEM((cols, width), f32),
            *PlaneGather.scratch(group),
        ],
        compiler_params=talk(collective_id, 60),
        cost_estimate=cost(2 * rows * width * cols, 25 * rows * width),
    )(array, w, mixed, *extra)


class Strips:

    @staticmethod
    def scratch(rows, right, depth):
        return [
            pltpu.VMEM((2, rows, depth), bf16),
            pltpu.VMEM((2, depth, right), bf16),
            pltpu.SemaphoreType.DMA((2, 2)),
        ]

    def __init__(self, whole, right_ref, target, held, done, sems):
        self.whole, self.right_ref, self.target = whole, right_ref, target
        self.held, self.done, self.sems = held, done, sems
        self.depth = held.shape[2]
        self.count = whole.shape[1] // self.depth

    def strip(self, at):
        return pl.ds(pl.multiple_of(at * self.depth, self.depth), self.depth)

    def load(self, at):
        slot = lax.rem(at, 2)
        return pltpu.make_async_copy(self.whole.at[:, self.strip(at)], self.held.at[slot], self.sems.at[0, slot])

    def store(self, at):
        slot = lax.rem(at, 2)
        return pltpu.make_async_copy(self.done.at[slot], self.target.at[self.strip(at)], self.sems.at[1, slot])

    def start(self):
        for at in range(2):
            self.load(at).start()

    def run(self):
        @pl.loop(0, self.count)
        def _(at):
            slot = lax.rem(at, 2)
            self.load(at).wait()

            @pl.when(at >= 2)
            def _():
                self.store(at - 2).wait()

            self.done[slot] = dot(self.held[slot], self.right_ref[...], 0, 0).astype(bf16)
            self.store(at).start()

            @pl.when(at + 2 < self.count)
            def _():
                self.load(at + 2).start()

    def finish(self):
        for at in range(self.count - 2, self.count):
            self.store(at).wait()


def back_sum_kernel(
    group, out_live, slope, down, up, second, attended_ref, out_ref, params_ref, bias_ref,
    after_ref, low_ref, sums_ref, grad_up, grad_pre_ref, own_ref, live_v, slope_v, down_v, up_v, sems, *refs,
):
    here = own_ref.shape[0]
    wide = down.shape[0]
    tile = math.gcd(1024, wide)
    order = PlaneSum.order(group, True)

    def rows_of(core, inner):
        return pl.ds(pl.multiple_of((core * group + inner) * here, here), here)

    slots = live_v.shape[0]

    def loads(turn):
        core = total.core if order[turn] % 2 else 1 - total.core
        rows, slot = rows_of(core, total.targets[order[turn] // 2]), turn % slots
        return (
            pltpu.make_async_copy(out_live.at[rows, :], live_v.at[slot], sems.at[0, slot]),
            pltpu.make_async_copy(slope.at[rows, :], slope_v.at[slot], sems.at[1, slot]),
        )

    def start_loads(turn):
        if turn < 2 * group:
            for load in loads(turn):
                load.start()

    down_load = pltpu.make_async_copy(down, down_v, sems.at[0, slots])
    up_load = pltpu.make_async_copy(up, up_v, sems.at[1, slots])

    def prepare(core, inner, at):
        turn = order.index(at)
        slot = turn % slots
        for load in loads(turn):
            load.wait()
        if turn == 0:
            down_load.wait()
        else:
            start_loads(turn + slots - 1)
        rows = rows_of(core, inner)

        @pl.loop(0, wide // tile)
        def _(i):
            columns = pl.ds(pl.multiple_of(i * tile, tile), tile)
            value = dot(live_v[slot], down_v[columns, :], 1, 1) * slope_v[slot, :, columns].astype(f32)
            value = value.astype(bf16)
            grad_pre_ref[rows, columns] = value
            bias_ref[:, columns] += jnp.sum(value.astype(f32), axis=0, keepdims=True)

        if turn == 0:
            up_load.wait()

    strips = Strips(second, grad_pre_ref, grad_up, *refs[:3])
    total = PlaneSum(group, row_product(group, here, True, grad_pre_ref, up_v), own_ref, *refs[3:], prepare=prepare)
    down_load.start()
    for turn in range(slots):
        start_loads(turn)
        if turn == 0:
            up_load.start()
    bias_ref[...] = jnp.zeros_like(bias_ref)
    strips.start()
    greet(total.core, total.inner, group)
    total.run(True, strips.run)
    close_second(total.inner, own_ref, (attended_ref, out_ref, params_ref), (after_ref, low_ref, sums_ref))
    strips.finish()


def back_sum(out_live, slope, down, up, second, attended, out_own, params, group, collective_id):
    rows, width = out_live.shape
    here, wide = rows // (2 * group), down.shape[0]
    local = pl.BlockSpec(memory_space=pltpu.VMEM)
    anywhere = pl.BlockSpec(memory_space=pl.ANY)
    bias, grad_after, low, sums, grad_up = pl.pallas_call(
        functools.partial(back_sum_kernel, group),
        out_shape=[
            jax.ShapeDtypeStruct((1, wide), f32),
            jax.ShapeDtypeStruct((here, width), f32),
            jax.ShapeDtypeStruct((here, width), bf16),
            jax.ShapeDtypeStruct((8, width), f32),
            jax.ShapeDtypeStruct((width, wide), bf16),
        ],
        in_specs=[anywhere] * 5 + [local] * 3,
        out_specs=[local] * 4 + [anywhere],
        scratch_shapes=[
            pltpu.VMEM((rows, wide), bf16),
            pltpu.VMEM((here, width), f32),
            pltpu.VMEM((4, here, width), bf16),
            pltpu.VMEM((4, here, wide), bf16),
            pltpu.VMEM(down.shape, bf16),
            pltpu.VMEM(up.shape, bf16),
            pltpu.SemaphoreType.DMA((2, 5)),
            *Strips.scratch(rows, wide, 1024 // group),
            *PlaneSum.scratch(group, here, width),
        ],
        compiler_params=pltpu.CompilerParams(
            collective_id=collective_id, has_side_effects=True, vmem_limit_bytes=63 * 2**20
        ),
        cost_estimate=pl.CostEstimate(
            flops=4 * rows * width * wide, bytes_accessed=50 * rows * width, transcendentals=0
        ),
    )(out_live, slope, down, up, second, attended, out_own, params)
    return bias[0], grad_after, low, sums, grad_up


def closing_kernel(planes, group, unit, repeats, extra, terms, attn, *refs):
    source, refs = refs[:extra], refs[extra:]
    out_ref, weight_refs, line_ref, refs = refs[0], refs[1:4], refs[4 : 4 + extra], refs[4 + extra :]
    attn_all, from_plane, summed, from_z, plane_sems, z_sems = refs[:6]
    exchange = PlaneExchange(group, attn, attn_all, *refs[6:8])
    sums = [PlanesSum(planes, 1, *source, *line_ref, *refs[8:])] if extra else []
    team = 2 * group
    z_at, core_at, inner_at, mine = lax.axis_index("z"), exchange.core, exchange.inner, exchange.mine
    greet_all(core_at, inner_at, group, planes)
    for one in sums:
        one.start()
    copies = []
    for step in range(1, team):
        core, inner = other_device(core_at, inner_at, group, step)
        copy = send(
            terms.at[core * group + inner],
            from_plane.at[step],
            plane_sems.at[0, step],
            plane_sems.at[1, step],
            core,
            inner,
        )
        copy.start()
        copies.append(copy)
    exchange.start()
    summed[...] = terms[mine]
    for copy in copies:
        copy.wait_recv()
    for step in range(1, team):
        summed[...] += from_plane[step]
    more = []
    for step in range(1, planes):
        to = lax.rem(z_at + step, planes)
        copy = pltpu.make_async_remote_copy(
            src_ref=summed.at[to],
            dst_ref=from_z.at[step],
            send_sem=z_sems.at[0, step],
            recv_sem=z_sems.at[1, step],
            device_id={"z": to},
            device_id_type=MESH,
        )
        copy.start()
        more.append(copy)
    exchange.finish()
    cols = unit * repeats
    for i in range(3):
        place_columns(weight_refs[i], attn_all, i * cols, unit, repeats, team)
    out_ref[...] = summed[z_at]
    for step, copy in enumerate(more, 1):
        copy.wait_recv()
        out_ref[...] += from_z[step]
    for copy in copies + more:
        copy.wait_send()
    for one in sums:
        one.finish()


def closing(terms, attn, planes, group, unit, collective_id, source=None):
    team, _, lines, _ = terms.shape
    rows, cols = attn.shape[1], attn.shape[2] // 3
    weight = jax.ShapeDtypeStruct((rows, cols * team), bf16)
    extra = [] if source is None else [source]
    sums = [(one.shape[0] // planes, one.shape[1] // 2) for one in extra]
    return pl.pallas_call(
        functools.partial(closing_kernel, planes, group, unit, cols // unit, len(extra)),
        out_shape=[
            jax.ShapeDtypeStruct((lines, 128), f32),
            weight,
            weight,
            weight,
            *[jax.ShapeDtypeStruct(shape, f32) for shape in sums],
        ],
        in_specs=[LOCAL, ANY] + [LOCAL] * len(extra),
        out_specs=[LOCAL] * (4 + len(extra)),
        scratch_shapes=[
            pltpu.VMEM(attn.shape, bf16),
            pltpu.VMEM((team, planes, lines, 128), f32),
            pltpu.VMEM((planes, lines, 128), f32),
            pltpu.VMEM((planes, lines, 128), f32),
            pltpu.SemaphoreType.DMA((2, team)),
            pltpu.SemaphoreType.DMA((2, planes)),
            *PlaneExchange.scratch(group),
            *[one for shape in sums for one in PlanesSum.scratch(planes, *shape)],
        ],
        compiler_params=talk(collective_id, 40),
        cost_estimate=cost(0, 10**8),
    )(terms, attn, *extra)


def body(
    layer_input,
    first_gain,
    first_shift,
    query_weight,
    key_weight,
    value_weight,
    output_weight,
    query_bias,
    value_bias,
    output_bias,
    second_gain,
    second_shift,
    up_weight,
    up_bias,
    down_weight,
    down_bias,
    segment_counts,
    out_grad,
):
    here, width = layer_input.shape
    wide = up_weight.shape[1]
    planes = lax.axis_size("z")
    group = lax.axis_size("fsdp")
    team = 2 * group
    z_at, core_at, inner_at = (lax.axis_index(name) for name in ALL)
    plane_at = core_at * group + inner_at
    seg_rows = here * group
    own_rows = query_weight.shape[0]
    own_wide = down_weight.shape[0]
    cols = width // team
    heads_here = cols // HEAD
    whole_heads = own_rows % HEAD == 0

    def to_columns(weight, unit):
        cut = weight.reshape(weight.shape[0], planes, team, unit)
        return cut.transpose(2, 0, 1, 3).reshape(team, weight.shape[0], planes * unit)

    def head_columns(weight):
        if whole_heads:
            return to_columns(weight, own_rows)
        return weight.reshape(own_rows, team, cols).transpose(1, 0, 2)

    attn_blocks = jnp.concatenate([head_columns(w) for w in (query_weight, key_weight, value_weight)], axis=2)
    out_here = z_gather(output_weight) if whole_heads else lax.all_gather(output_weight, ALL, axis=0, tiled=True)
    attn_cols, up_cols = plane_exchange(attn_blocks, up_weight, own_wide, planes, group, 0)
    attn_cols = attn_cols.reshape(team * own_rows, 3 * cols)
    up_cols = up_cols.reshape(team * own_rows, wide // team)
    attn_full = z_gather(after(attn_cols, out_here))
    small = jnp.concatenate(
        [first_gain, first_shift, query_bias, value_bias, output_bias, second_gain, second_shift, down_bias, up_bias]
    )
    length = small.shape[0]
    small = jnp.pad(small.astype(f32), (0, -length % 1024)).reshape(-1, 128)
    segment = 2 * z_at + jnp.arange(2, dtype=jnp.int32)
    place = segment % MAXSEG
    present = place < segment_counts[segment // MAXSEG]
    pos = jnp.arange(seg_rows, dtype=jnp.int32)
    live = present[:, None] & ((pos >= PRE)[None] | (place[:, None] >= PREV - pos[None] // SUMM))
    live_own = lax.dynamic_slice(live, (core_at, inner_at * here), (1, here))[0]
    out_own = jnp.where(live_own[:, None], out_grad, jnp.zeros_like(out_grad))
    all_rows, small_all, out_live = entry(after(layer_input, up_cols), small, out_own, planes, group, 1)
    all_rows = all_rows.reshape(-1, width)
    small_all = small_all.swapaxes(0, 1).reshape(planes * team, -1)
    params = small_all[:, : 8 * own_rows].reshape(planes * team, 8, own_rows).swapaxes(0, 1).reshape(8, width)
    bias_up = small_all[:, 8 * own_rows : length].reshape(planes, team, own_wide)[:, plane_at].reshape(wide // team)

    def own_columns(bias):
        if whole_heads:
            return bias.reshape(planes, team, own_rows)[:, plane_at].reshape(cols)
        return lax.dynamic_slice_in_dim(bias, plane_at * cols, cols)

    bias_q, bias_v = own_columns(params[BIAS_Q]), own_columns(params[BIAS_V])
    out_full = out_here if whole_heads else lax.dynamic_slice_in_dim(out_here, plane_at * cols, cols)
    up_full = z_gather(up_cols)
    down_full = z_gather(after(down_weight, up_cols))
    normed_low, qkv, mixed_low, totals, out_live = attend(
        all_rows,
        attn_full,
        params,
        jnp.concatenate([bias_q, jnp.zeros_like(bias_q), bias_v]),
        live,
        out_own,
        out_live,
        group,
        11,
    )
    out_live = out_live.reshape(-1, width)
    attended, second_own = product_sum(
        mixed_low,
        out_full,
        False,
        close_attention,
        [layer_input, params],
        [(here, f32), (here, bf16)],
        group,
        2,
    )
    second_low, activated, slope = gather_up(second_own, up_full, bias_up, group, 3)
    grad_down = dot(activated, out_live, 0, 0).astype(bf16)
    out_live = after(out_live, grad_down)
    grad_down = z_sum(grad_down)
    grad_up_bias, grad_after, after_low_own, second_sums, grad_up = back_sum(
        out_live, slope, down_full, up_full, second_low, attended, out_own, params, group, 5
    )
    first_mixed, first_output = gather_mixed(after_low_own, out_full, mixed_low, group, 6)
    grad_up = z_sum(after(grad_up, grad_down, first_mixed)).reshape(team, own_rows, wide // team)
    second_mixed, grad_output = gather_mixed(after_low_own, out_full, mixed_low, group, 7, first_output)
    grad_qkv, added, grad_bias, grad_attn = attend_back(
        qkv, (first_mixed, second_mixed), live, totals, activated, down_full, normed_low, group, 4
    )
    grad_bias = grad_bias[0]
    grad_attn = z_sum(after(grad_attn, grad_up)).reshape(team, own_rows, 3 * cols)
    input_grad, first_sums, grad_up, *summed = product_sum(
        grad_qkv,
        attn_full,
        True,
        close_first,
        [layer_input, params, grad_after],
        [(here, f32), (8, f32)],
        group,
        8,
        planes,
        grad_up,
        grad_output if whole_heads else None,
    )
    grad_down, added = after(grad_down, input_grad), after(added, input_grad)
    layer_output = (attended + added + params[BIAS_DOWN]).astype(bf16)
    own_pos = inner_at * here + jnp.arange(here, dtype=jnp.int32)
    input_grad = jnp.where((own_pos >= SUMM)[:, None], input_grad, 0.0)

    def spread_columns(bias):
        if whole_heads:
            full = jnp.zeros((planes, team, own_rows), f32)
            return lax.dynamic_update_slice(full, bias.reshape(planes, 1, own_rows), (0, plane_at, 0)).reshape(width)
        return lax.dynamic_update_slice(jnp.zeros((width,), f32), bias, (plane_at * cols,))

    sums = [
        first_sums[0],
        first_sums[1],
        spread_columns(grad_bias[:cols]),
        spread_columns(grad_bias[2 * cols :]),
        second_sums[2],
        second_sums[0],
        second_sums[1],
        second_sums[3],
    ]
    up_spread = jnp.zeros((planes, team, own_wide), f32)
    up_spread = lax.dynamic_update_slice(up_spread, grad_up_bias.reshape(planes, 1, own_wide), (0, plane_at, 0))
    packed = jnp.concatenate(
        [a.reshape(planes * team, own_rows) for a in sums] + [up_spread.reshape(planes * team, own_wide)], axis=1
    )
    packed = jnp.pad(packed, ((0, 0), (0, -length % 1024))).reshape(planes, team, -1, 128).swapaxes(0, 1)
    if not whole_heads:
        spread = jnp.zeros((width, width), bf16)
        spread = lax.dynamic_update_slice_in_dim(spread, grad_output, plane_at * cols, 0)
        last_sum = lax.psum_scatter(spread, ALL, scatter_dimension=0, tiled=True).astype(f32)
    packed, *grad_weights = closing(
        packed,
        grad_attn,
        planes,
        group,
        own_rows if whole_heads else cols,
        9,
        grad_output if whole_heads else None,
    )
    if whole_heads:
        last_sum = jnp.concatenate([*summed, grad_weights.pop()], axis=1)
    packed = packed.reshape(-1)
    small_grads = [packed[i * own_rows : (i + 1) * own_rows] for i in range(8)]
    return (
        layer_output,
        input_grad,
        small_grads[0],
        small_grads[1],
        *[weight.astype(f32) for weight in grad_weights],
        last_sum,
        small_grads[2],
        small_grads[3],
        small_grads[4],
        small_grads[5],
        small_grads[6],
        grad_up.astype(f32),
        packed[8 * own_rows : length],
        grad_down.astype(f32),
        small_grads[7],
    )


def solution(mesh):
    outer, inner = mesh.devices.shape
    fine = Mesh(mesh.devices.reshape(outer // 2, 2, inner), ALL)
    rows, vector = P(ALL, None), P(ALL)
    return jax.shard_map(
        body,
        mesh=fine,
        in_specs=(
            rows, vector, vector, rows, rows, rows, rows, vector, vector, vector, vector, vector,
            rows, vector, rows, vector, P(), rows,
        ),
        out_specs=(
            rows, rows, vector, vector, rows, rows, rows, rows, vector, vector, vector, vector, vector,
            rows, vector, rows, vector,
        ),
        check_vma=False,
    )
```

```python
import functools
import math

import jax
import jax.numpy as jnp
from jax import lax
from jax.experimental import pallas as pl
from jax.experimental.pallas import tpu as pltpu
from jax.sharding import Mesh, PartitionSpec as P

HEADS = 32
HEAD = 64
SUMM = 50
PREV = 3
MAXSEG = 4
PRE = 150

epsilon = 1e-05
masked = -1e30

ALL = ("z", "core", "fsdp")
PLANE = ("core", "fsdp")
bf16 = jnp.bfloat16
f32 = jnp.float32
MESH = pl.DeviceIdType.MESH


def dot(a, b, ca, cb):
    return lax.dot_general(a, b, (((ca,), (cb,)), ((), ())), preferred_element_type=f32)


def z_gather(rows):
    return lax.all_gather(rows, "z", axis=0, tiled=True)


def z_sum(partial):
    return lax.psum_scatter(partial.astype(bf16), "z", scatter_dimension=0, tiled=True)


def after(value, *earlier):
    return lax.optimization_barrier((value, *earlier))[0]


def unit_norm(values):
    center = values - jnp.mean(values, axis=-1, keepdims=True)
    inverse_std = lax.rsqrt(jnp.mean(center * center, axis=-1, keepdims=True) + epsilon)
    return center * inverse_std, inverse_std


def normalize_back(grad_rows, unit_rows, inverse_std, norm_gain):
    scaled = grad_rows * norm_gain
    centered = scaled - jnp.mean(scaled, axis=-1, keepdims=True)
    centered = centered - unit_rows * jnp.mean(scaled * unit_rows, axis=-1, keepdims=True)
    return centered * inverse_std


def head_mask(rows, cols, head):
    lane = lax.broadcasted_iota(jnp.int32, (rows, cols), 1)
    return lane // HEAD == head


def attend_segment(block, heads, seg_rows, seg, qkv_ref, live_ref, mixed_ref, total_ref, bias_ref):
    cols = heads * HEAD
    base = seg * seg_rows
    lane = lax.broadcasted_iota(jnp.int32, (block, 128), 1)
    for at in range(seg_rows // block):
        wide = (at + 1) * block
        rows = pl.ds(pl.multiple_of(base + at * block, block), block)
        keys = pl.ds(pl.multiple_of(base, seg_rows), wide)
        query_pos = at * block + lax.broadcasted_iota(jnp.int32, (block, wide), 0)
        key_pos = lax.broadcasted_iota(jnp.int32, (block, wide), 1)
        open_key = (live_ref[seg, :, :wide] > 0.0) & (key_pos < query_pos) | (key_pos == query_pos)
        bias_ref[:, :wide] = jnp.where(open_key, 0.0, masked)
        query = qkv_ref[rows, :cols] * jnp.asarray(HEAD**-0.5, bf16)
        result = jnp.zeros((block, cols), f32)
        totals = jnp.zeros((block, 128), f32)
        for head in range(heads):
            chosen = head_mask(block, cols, head)
            scores = dot(jnp.where(chosen, query, jnp.zeros_like(query)), qkv_ref[keys, cols : 2 * cols], 1, 1)
            scores = scores + bias_ref[:, :wide]
            top = jnp.max(scores, axis=1, keepdims=True)
            powers = jnp.exp(scores - top)
            total = jnp.sum(powers, axis=1, keepdims=True)
            probs = (powers * (1.0 / total)).astype(bf16)
            value = dot(probs, qkv_ref[keys, 2 * cols :], 1, 0)
            result = jnp.where(chosen, value, result)
            totals = jnp.where(lane == head, top + jnp.log(total), totals)
        mixed_ref[rows, :] = result.astype(bf16)
        total_ref[seg, :, at * block : (at + 1) * block] = totals.T[:8]


def attend_back_rows(
    block, heads, seg_rows, seg, at, qkv_ref, grad_ref, live_ref, total_ref, out_ref, bias_ref, sums_ref
):
    cols = heads * HEAD
    base = seg * seg_rows
    wide = (at + 1) * block
    rows = pl.ds(pl.multiple_of(base + at * block, block), block)
    keys = pl.ds(pl.multiple_of(base, seg_rows), wide)
    key_pos = lax.broadcasted_iota(jnp.int32, (wide, block), 0)
    query_pos = at * block + lax.broadcasted_iota(jnp.int32, (wide, block), 1)
    open_key = (live_ref[keys, :] > 0.0) & (key_pos < query_pos) | (key_pos == query_pos)
    bias_ref[:wide, :] = jnp.where(open_key, 0.0, masked)
    query = qkv_ref[rows, :cols] * jnp.asarray(HEAD**-0.5, bf16)
    half = block // 2
    part = pl.ds(pl.multiple_of((base + at * block) // 2, half), half)
    grad = jnp.concatenate([one[part, :] for one in grad_ref], axis=0)
    grad_query = jnp.zeros((block, cols), f32)
    for head in range(heads):
        chosen = head_mask(block, cols, head)
        query_one = jnp.where(chosen, query, jnp.zeros_like(query))
        grad_one = jnp.where(chosen, grad, jnp.zeros_like(grad))
        scores = dot(qkv_ref[keys, cols : 2 * cols], query_one, 1, 1)
        total = total_ref[seg, head : head + 1, at * block : (at + 1) * block]
        probs = jnp.exp(scores + bias_ref[:wide, :] - total)
        terms = probs * dot(qkv_ref[keys, 2 * cols :], grad_one, 1, 1)
        delta = jnp.sum(terms, axis=0, keepdims=True)
        grad_scores = (terms - probs * delta).astype(bf16)
        sums_ref[:wide, :cols] += dot(grad_scores, query_one, 1, 0)
        sums_ref[:wide, cols:] += dot(probs.astype(bf16), grad_one, 1, 0)
        value = dot(grad_scores, qkv_ref[keys, cols : 2 * cols], 0, 0)
        grad_query = jnp.where(chosen, value, grad_query)
    out_ref[rows, :cols] = (grad_query * HEAD**-0.5).astype(bf16)


def other_device(core_at, inner_at, group, step):
    return lax.rem(core_at + step // group, 2), lax.rem(inner_at + step % group, group)


def signal(**place):
    pl.semaphore_signal(pltpu.get_barrier_semaphore(), inc=1, device_id=place, device_id_type=MESH)


def greet(core_at, inner_at, group):
    signal(core=1 - core_at, fsdp=inner_at)
    for step in range(1, group):
        signal(core=core_at, fsdp=lax.rem(inner_at + step, group))
    pl.semaphore_wait(pltpu.get_barrier_semaphore(), group)


def greet_all(core_at, inner_at, group, planes):
    z_at = lax.axis_index("z")
    for step in range(1, 2 * group):
        core, inner = other_device(core_at, inner_at, group, step)
        signal(core=core, fsdp=inner)
    for step in range(1, planes):
        signal(z=lax.rem(z_at + step, planes))
    pl.semaphore_wait(pltpu.get_barrier_semaphore(), 2 * group + planes - 2)


def send(source, target, send_sem, recv_sem, core, inner):
    return pltpu.make_async_remote_copy(
        src_ref=source,
        dst_ref=target,
        send_sem=send_sem,
        recv_sem=recv_sem,
        device_id={"core": core, "fsdp": inner},
        device_id_type=MESH,
    )


def beside(inner_at):
    at_x = inner_at + 1 - 2 * lax.rem(inner_at, 2)
    at_y = lax.rem(inner_at + 2, 4)
    return at_x, at_y, lax.rem(at_x + 2, 4)


class PlaneGather:

    @staticmethod
    def scratch(group):
        return [pltpu.SemaphoreType.DMA((2, 2 * group)), pltpu.SemaphoreType.DMA((2, 2 * group)), pltpu.SemaphoreType.DMA]

    def __init__(self, group, source, target, chip_sems, core_sems, own_sem):
        self.group, self.source, self.target = group, source, target
        self.chip_sems, self.core_sems = chip_sems, core_sems
        self.core, self.inner = lax.axis_index("core"), lax.axis_index("fsdp")
        self.mine = self.core * group + self.inner
        self.own = pltpu.make_async_copy(source, target.at[self.mine], own_sem)
        half = source.shape[0] // 2
        self.low, self.high = pl.ds(0, half), pl.ds(half, half)
        self.sent = []

    def to_chip(self, at, source, target, inner):
        return send(source, target, self.chip_sems.at[0, at], self.chip_sems.at[1, at], self.core, inner)

    def to_core(self, at, source, target):
        return send(source, target, self.core_sems.at[0, at], self.core_sems.at[1, at], 1 - self.core, self.inner)

    def block(self, core, inner, part=None):
        at = core * self.group + inner
        return self.target.at[at] if part is None else self.target.at[at, part]

    def go(self, copy):
        copy.start()
        self.sent.append(copy)

    def start(self):
        own = self.target.at[self.mine]
        if self.group == 4:
            at_x, at_y, _ = beside(self.inner)
            for at, part, inner in ((0, self.low, at_x), (1, self.high, at_y), (2, self.high, at_x), (3, self.low, at_y)):
                self.go(self.to_chip(at, self.source.at[part], self.block(self.core, self.inner, part), inner))
        else:
            for step in range(1, self.group):
                self.go(self.to_chip(step, self.source, own, lax.rem(self.inner + step, self.group)))
        self.go(self.to_core(0, self.source, own))
        self.own.start()

    def wait_core(self, at):
        other, low, high = 1 - self.core, self.low, self.high
        if self.group == 4:
            at_x, at_y, across = beside(self.inner)
            inner, part = ((self.inner, None), (at_x, None), (at_y, None), (across, low), (across, high))[at]
        else:
            inner, part = lax.rem(self.inner - at + self.group, self.group), None
        block = self.block(other, inner, part)
        self.to_core(at, block, block).wait_recv()

    def across(self):
        if self.group == 4:
            at_x, at_y, across = beside(self.inner)
            for at, part in ((2, self.low), (3, self.high)):
                block = self.block(self.core, across, part)
                self.to_chip(at + 2, block, block, at_x).wait_recv()
                self.go(self.to_core(at + 1, block, block))

    def run(self, use):
        core, inner, other = self.core, self.inner, 1 - self.core
        self.start()
        self.own.wait()
        use(core, inner)
        self.wait_core(0)
        use(other, inner)
        self.relay()
        if self.group == 4:
            at_x, at_y, across = beside(inner)
            use(core, at_x)
            use(core, at_y)
            self.wait_core(1)
            use(other, at_x)
            self.wait_core(2)
            use(other, at_y)
            self.across()
            use(core, across)
            self.wait_core(3)
            self.wait_core(4)
            use(other, across)
        else:
            for step in range(1, self.group):
                use(core, lax.rem(inner - step + self.group, self.group))
            for step in range(1, self.group):
                self.wait_core(step)
                use(other, lax.rem(inner - step + self.group, self.group))
        for copy in self.sent:
            copy.wait_send()

    def relay(self):
        if self.group == 4:
            at_x, at_y, _ = beside(self.inner)
            for at, inner, part, onward in ((0, at_x, self.low, at_y), (1, at_y, self.high, at_x)):
                block = self.block(self.core, inner, part)
                self.to_chip(at, block, block, inner).wait_recv()
                self.go(self.to_chip(at + 4, block, block, onward))
            for at, inner, part in ((2, at_x, self.high), (3, at_y, self.low)):
                block = self.block(self.core, inner, part)
                self.to_chip(at, block, block, inner).wait_recv()
                block = self.block(self.core, inner)
                self.go(self.to_core(at - 1, block, block))
        else:
            for step in range(1, self.group):
                inner = lax.rem(self.inner - step + self.group, self.group)
                block = self.block(self.core, inner)
                self.to_chip(step, block, block, inner).wait_recv()
                self.go(self.to_core(step, block, block))

    def finish(self):
        self.across()
        for at in range(5 if self.group == 4 else self.group):
            self.wait_core(at)
        for copy in self.sent:
            copy.wait_send()
        self.own.wait()


class PlaneSum:

    @staticmethod
    def scratch(group, here, width):
        blocks, fewer = (pltpu.VMEM((count, here, width), bf16) for count in (group, group - 1))
        sems = [pltpu.SemaphoreType.DMA((2, 2 * group)), pltpu.SemaphoreType.DMA((2, group))]
        return [blocks, blocks, blocks if group == 4 else fewer, fewer, *sems]

    def __init__(self, group, product, out_ref, to_core, from_core, pair, land, chip_sems, core_sems, prepare=None):
        self.group, self.product, self.out_ref, self.prepare = group, product, out_ref, prepare
        self.to_core_ref, self.from_core_ref, self.pair, self.land = to_core, from_core, pair, land
        self.chip_sems, self.core_sems = chip_sems, core_sems
        self.core, self.inner = lax.axis_index("core"), lax.axis_index("fsdp")
        self.here, self.width = out_ref.shape
        half = self.here // 2
        self.low, self.high = pl.ds(0, half), pl.ds(half, half)
        self.tile = math.gcd(self.width, 8192 // group)
        if group == 4:
            self.across_x, self.across_y, across = beside(self.inner)
            self.targets = [across, self.across_x, self.across_y, self.inner]
        else:
            self.targets = [lax.rem(self.inner + step, group) for step in range(1, group)] + [self.inner]
        self.sent = []

    def to_chip(self, at, source, target, inner):
        return send(source, target, self.chip_sems.at[0, at], self.chip_sems.at[1, at], self.core, inner)

    def go(self, copy):
        copy.start()
        self.sent.append(copy)

    def core_copy(self, i):
        return send(
            self.to_core_ref.at[i],
            self.from_core_ref.at[i],
            self.core_sems.at[0, i],
            self.core_sems.at[1, i],
            1 - self.core,
            self.inner,
        )

    def part_core(self, i):
        if self.prepare:
            self.prepare(1 - self.core, self.targets[i], 2 * i)

        @pl.loop(0, self.width // self.tile)
        def _(at):
            columns = pl.ds(pl.multiple_of(at * self.tile, self.tile), self.tile)
            self.to_core_ref[i, :, columns] = self.product(1 - self.core, self.targets[i], columns).astype(bf16)

        self.go(self.core_copy(i))

    def part_chip(self, i):
        if self.prepare:
            self.prepare(self.core, self.targets[i], 2 * i + 1)
        self.core_copy(i).wait_recv()
        last = i == self.group - 1

        @pl.loop(0, self.width // self.tile)
        def _(at):
            columns = pl.ds(pl.multiple_of(at * self.tile, self.tile), self.tile)
            value = self.product(self.core, self.targets[i], columns) + self.from_core_ref[i, :, columns].astype(f32)
            if last:
                self.out_ref[:, columns] = value
            else:
                self.pair[i, :, columns] = value.astype(bf16)

        if last:
            return
        pair, land = self.pair, self.land
        if self.group != 4:
            self.go(self.to_chip(i, pair.at[i], land.at[i], self.targets[i]))
        elif i == 0:
            self.go(self.to_chip(0, pair.at[0, self.low], land.at[0, self.low], self.across_x))
            self.go(self.to_chip(1, pair.at[0, self.high], land.at[1, self.low], self.across_y))
        elif i == 1:
            self.go(self.to_chip(2, pair.at[1, self.low], land.at[0, self.high], self.across_x))
        else:
            self.go(self.to_chip(3, pair.at[2, self.high], land.at[1, self.high], self.across_y))

    def arrive(self, at, place, part):
        self.to_chip(at, self.pair.at[0, part], self.land.at[place, part], self.across_x).wait_recv()
        return self.land[place, part, :].astype(f32)

    def relay(self):
        if self.group != 4:
            return
        pair, land = self.pair, self.land
        value = self.arrive(0, 0, self.low) + pair[2, self.low, :].astype(f32)
        pair[3, self.low, :] = value.astype(bf16)
        self.go(self.to_chip(4, pair.at[3, self.low], land.at[2, self.low], self.across_y))
        value = self.arrive(1, 1, self.low) + pair[1, self.high, :].astype(f32)
        pair[3, self.high, :] = value.astype(bf16)
        self.go(self.to_chip(5, pair.at[3, self.high], land.at[2, self.high], self.across_x))

    def finish(self):
        out_ref = self.out_ref
        if self.group == 4:
            out_ref[self.low, :] += self.arrive(2, 0, self.high)
            out_ref[self.high, :] += self.arrive(3, 1, self.high)
            out_ref[self.low, :] += self.arrive(4, 2, self.low)
            out_ref[self.high, :] += self.arrive(5, 2, self.high)
        else:
            for i in range(self.group - 1):
                self.to_chip(i, self.pair.at[i], self.land.at[i], self.inner).wait_recv()
                out_ref[...] += self.land[i].astype(f32)
        for copy in self.sent:
            copy.wait_send()

    @staticmethod
    def order(group, eager=False):
        if eager:
            return list(range(2 * group))
        parts = [0]
        for i in range(group):
            parts += ([2 * i + 2] if i + 1 < group else []) + [2 * i + 1]
        return parts

    def part(self, at):
        (self.part_chip if at % 2 else self.part_core)(at // 2)

    def run(self, eager=False, meanwhile=None):
        for at in self.order(self.group, eager):
            self.part(at)
        self.relay()
        if meanwhile:
            meanwhile()
        self.finish()


class PlanesSum:

    @staticmethod
    def scratch(planes, rows, width):
        return [pltpu.VMEM((planes, rows, width), bf16), pltpu.SemaphoreType.DMA((2, planes))]

    def __init__(self, planes, part, source, out_ref, land, sems):
        self.columns = pl.ds(part * out_ref.shape[1], out_ref.shape[1])
        self.planes, self.source, self.out_ref, self.land, self.sems = planes, source, out_ref, land, sems
        self.z = lax.axis_index("z")
        self.sent = []

    def rows(self, z):
        count = self.out_ref.shape[0]
        return pl.ds(pl.multiple_of(z * count, count), count)

    def start(self):
        for step in range(1, self.planes):
            to = lax.rem(self.z + step, self.planes)
            copy = pltpu.make_async_remote_copy(
                src_ref=self.source.at[self.rows(to), self.columns],
                dst_ref=self.land.at[step],
                send_sem=self.sems.at[0, step],
                recv_sem=self.sems.at[1, step],
                device_id={"z": to},
                device_id_type=MESH,
            )
            copy.start()
            self.sent.append(copy)

    def finish(self):
        self.out_ref[...] = self.source[self.rows(self.z), self.columns].astype(f32)
        for step, copy in enumerate(self.sent, 1):
            copy.wait()
            self.out_ref[...] += self.land[step].astype(f32)


def place_columns(out_ref, blocks, base, unit, planes, team):
    several = max(1, 128 // unit)
    for z in range(planes):
        for p in range(0, team, several):
            parts = [blocks[p + i, :, base + z * unit : base + (z + 1) * unit] for i in range(several)]
            value = parts[0] if several == 1 else jnp.concatenate(parts, axis=1)
            start = (z * team + p) * unit
            out_ref[:, start : start + unit * several] = value


def row_product(group, here, flip, a_ref, w_ref):
    def product(core, inner, columns):
        rows = a_ref[pl.ds(pl.multiple_of((core * group + inner) * here, here), here), :]
        if flip:
            return dot(rows, w_ref[columns, :], 1, 1)
        return dot(rows, w_ref[:, columns], 1, 0)

    return product


class PlaneExchange:

    @staticmethod
    def scratch(group):
        return [pltpu.SemaphoreType.DMA((2, 2 * group)), pltpu.SemaphoreType.DMA]

    def __init__(self, group, source, target, sems, own_sem):
        self.group, self.source, self.target, self.sems = group, source, target, sems
        self.core, self.inner = lax.axis_index("core"), lax.axis_index("fsdp")
        self.mine = self.core * group + self.inner
        self.own = pltpu.make_async_copy(source.at[self.mine], target.at[self.mine], own_sem)
        self.sent = []

    def start(self):
        for step in range(1, 2 * self.group):
            core, inner = other_device(self.core, self.inner, self.group, step)
            copy = send(
                self.source.at[core * self.group + inner],
                self.target.at[self.mine],
                self.sems.at[0, step],
                self.sems.at[1, step],
                core,
                inner,
            )
            copy.start()
            self.sent.append(copy)
        self.own.start()

    def start_cut(self, whole, unit, repeats):
        team = 2 * self.group
        for p in range(team):
            for r in range(repeats):
                start = (r * team + p) * unit
                self.source[p, :, r * unit : (r + 1) * unit] = whole[:, start : start + unit]
        self.start()

    def finish(self):
        group = self.group
        for step in range(1, 2 * group):
            core = lax.rem(self.core + step // group, 2)
            inner = lax.rem(self.inner - step % group + group, group)
            block = self.target.at[core * group + inner]
            send(block, block, self.sems.at[0, step], self.sems.at[1, step], core, inner).wait_recv()
        for copy in self.sent:
            copy.wait_send()
        self.own.wait()


ANY = pl.BlockSpec(memory_space=pl.ANY)
LOCAL = pl.BlockSpec(memory_space=pltpu.VMEM)


def talk(collective_id, megabytes):
    return pltpu.CompilerParams(
        collective_id=collective_id, has_side_effects=True, vmem_limit_bytes=megabytes * 2**20
    )


def cost(flops, bytes_accessed):
    return pl.CostEstimate(flops=flops, bytes_accessed=bytes_accessed, transcendentals=0)


def swap_kernel(group, unit, repeats, attn, up, attn_all, up_all, up_blocks, *refs):
    first = PlaneExchange(group, attn, attn_all, *refs[:2])
    second = PlaneExchange(group, up_blocks, up_all, *refs[2:])
    greet_all(first.core, first.inner, group, 1)
    first.start()
    second.start_cut(up, unit, repeats)
    first.finish()
    second.finish()


def plane_exchange(attn, up, unit, repeats, group, collective_id):
    team = 2 * group
    blocks = jax.ShapeDtypeStruct((team, up.shape[0], unit * repeats), up.dtype)
    return pl.pallas_call(
        functools.partial(swap_kernel, group, unit, repeats),
        out_shape=[jax.ShapeDtypeStruct(attn.shape, attn.dtype), blocks],
        in_specs=[ANY, LOCAL],
        out_specs=[ANY, ANY],
        scratch_shapes=[
            pltpu.VMEM(blocks.shape, blocks.dtype),
            *PlaneExchange.scratch(group),
            *PlaneExchange.scratch(group),
        ],
        compiler_params=talk(collective_id, 60),
        cost_estimate=cost(0, 80 * (attn.size + up.size)),
    )(attn, up)


def halves(ref, first):
    half = ref.shape[-2] // 2
    part = pl.ds(0 if first else half, half)
    return ref.at[part] if len(ref.shape) == 2 else ref.at[:, part]


def entry_kernel(planes, group, x_ref, small_ref, out_ref, x_all, small_all, out_all, *refs):
    rows = PlaneGather(group, x_ref, x_all, *refs[:3])
    first = PlaneGather(group, halves(out_ref, True), halves(out_all, True), *refs[3:6])
    line_sems, face_sems = refs[6:]
    z_at, core_at, inner_at, mine = lax.axis_index("z"), rows.core, rows.inner, rows.mine
    greet_all(core_at, inner_at, group, planes)
    lines, faces = [], []
    for step in range(1, planes):
        copy = pltpu.make_async_remote_copy(
            src_ref=small_ref,
            dst_ref=small_all.at[mine, z_at],
            send_sem=line_sems.at[0, step],
            recv_sem=line_sems.at[1, step],
            device_id={"z": lax.rem(z_at + step, planes)},
            device_id_type=MESH,
        )
        copy.start()
        lines.append(copy)
    rows.start()
    small_all[mine, z_at] = small_ref[...]
    for copy in lines:
        copy.wait()
    face = small_all.at[mine]
    for step in range(1, 2 * group):
        core, inner = other_device(core_at, inner_at, group, step)
        copy = send(face, face, face_sems.at[0, step], face_sems.at[1, step], core, inner)
        copy.start()
        faces.append(copy)
    rows.relay()
    first.start()
    rows.finish()
    first.relay()
    first.finish()
    for step in range(1, 2 * group):
        core = lax.rem(core_at + step // group, 2)
        face = small_all.at[core * group + lax.rem(inner_at - step % group + group, group)]
        send(face, face, face_sems.at[0, step], face_sems.at[1, step], core_at, inner_at).wait_recv()
    for copy in faces:
        copy.wait_send()


def entry(x, small, out_own, planes, group, collective_id):
    team = 2 * group
    return pl.pallas_call(
        functools.partial(entry_kernel, planes, group),
        out_shape=[
            jax.ShapeDtypeStruct((team, *x.shape), x.dtype),
            jax.ShapeDtypeStruct((team, planes, *small.shape), small.dtype),
            jax.ShapeDtypeStruct((team, *out_own.shape), out_own.dtype),
        ],
        in_specs=[ANY, LOCAL, ANY],
        out_specs=[ANY, LOCAL, ANY],
        scratch_shapes=[
            *PlaneGather.scratch(group),
            *PlaneGather.scratch(group),
            pltpu.SemaphoreType.DMA((2, planes)),
            pltpu.SemaphoreType.DMA((2, team)),
        ],
        compiler_params=talk(collective_id, 60),
        cost_estimate=cost(0, 400 * x.size),
    )(x, small, out_own)


def chunks(ref, do):
    rows = math.gcd(ref.shape[0], 64)

    @pl.loop(0, ref.shape[0] // rows)
    def _(at):
        do(pl.ds(pl.multiple_of(at * rows, rows), rows))


GAIN_ONE, SHIFT_ONE, BIAS_Q, BIAS_V, BIAS_O, GAIN_TWO, SHIFT_TWO, BIAS_DOWN = range(8)


def line(params_ref, at):
    return params_ref[at : at + 1, :]


def close_attention(inner_at, own_ref, ins, outs):
    x_ref, params_ref = ins
    attended_ref, low_ref = outs

    def do(rows):
        value = x_ref[rows, :].astype(f32) + own_ref[rows, :] + line(params_ref, BIAS_O)
        attended_ref[rows, :] = value
        normed = unit_norm(value)[0] * line(params_ref, GAIN_TWO) + line(params_ref, SHIFT_TWO)
        low_ref[rows, :] = normed.astype(bf16)

    chunks(own_ref, do)


def add_sums(sums_ref, *terms):
    for i, term in enumerate(terms):
        sums_ref[i : i + 1, :] += jnp.sum(term, axis=0, keepdims=True)


def close_second(inner_at, own_ref, ins, outs):
    attended_ref, out_ref, params_ref = ins
    after_ref, low_ref, sums_ref = outs
    sums_ref[...] = jnp.zeros_like(sums_ref)

    def do(rows):
        unit, inverse = unit_norm(attended_ref[rows, :])
        grad = own_ref[rows, :]
        value = out_ref[rows, :].astype(f32) + normalize_back(
            grad, unit, inverse, line(params_ref, GAIN_TWO)
        )
        low = value.astype(bf16)
        after_ref[rows, :] = value
        low_ref[rows, :] = low
        add_sums(sums_ref, grad * unit, grad, low.astype(f32), out_ref[rows, :].astype(f32))

    chunks(own_ref, do)


def close_first(inner_at, own_ref, ins, outs):
    x_ref, params_ref, after_ref = ins
    grad_ref, sums_ref = outs
    sums_ref[...] = jnp.zeros_like(sums_ref)

    def do(rows):
        unit, inverse = unit_norm(x_ref[rows, :].astype(f32))
        grad = own_ref[rows, :]
        grad_ref[rows, :] = after_ref[rows, :] + normalize_back(grad, unit, inverse, line(params_ref, GAIN_ONE))
        add_sums(sums_ref, grad * unit, grad)

    chunks(own_ref, do)


def product_sum_kernel(group, planes, flip, close, ins, outs, swap, extra, a_ref, w_ref, *refs):
    in_refs, refs = refs[:ins], refs[ins:]
    ahead, refs = refs[: swap + extra], refs[swap + extra :]
    out_refs, refs = refs[:outs], refs[outs:]
    placed, refs = refs[: swap + extra], refs[swap + extra :]
    own_ref, *refs = refs
    sums, refs = refs[:6], refs[6:]
    total = PlaneSum(group, row_product(group, own_ref.shape[0], flip, a_ref, w_ref), own_ref, *sums)
    if swap:
        arrived, *refs = refs
        exchange = PlaneExchange(group, ahead[0], arrived, *refs[:2])
        lines = PlanesSum(planes, 0, ahead[1], placed[1], *refs[2:]) if extra else None
        greet_all(total.core, total.inner, group, planes)
        if extra:
            lines.start()
        exchange.start()
    else:
        greet(total.core, total.inner, group)
    total.run()
    close(total.inner, own_ref, in_refs, out_refs)
    if swap:
        exchange.finish()
        place_columns(placed[0], arrived, 0, arrived.shape[2] // planes, planes, 2 * group)
        if extra:
            lines.finish()


def product_sum(a, w, flip, close, ins, outs, group, collective_id, planes=1, swap=None, terms=None):
    here = a.shape[0] // (2 * group)
    width = w.shape[0 if flip else 1]
    shapes = [jax.ShapeDtypeStruct((rows, width), kind) for rows, kind in outs]
    scratch = [pltpu.VMEM((here, width), f32), *PlaneSum.scratch(group, here, width)]
    ahead, places = [], []
    if swap is not None:
        ahead, places = [swap], [ANY]
        shapes.append(jax.ShapeDtypeStruct((swap.shape[1], swap.shape[0] * swap.shape[2]), swap.dtype))
        scratch += [pltpu.VMEM(swap.shape, swap.dtype), *PlaneExchange.scratch(group)]
    if terms is not None:
        ahead, places = ahead + [terms], places + [LOCAL]
        rows = terms.shape[0] // planes
        shapes.append(jax.ShapeDtypeStruct((rows, width // 2), f32))
        scratch += PlanesSum.scratch(planes, rows, width // 2)
    extra = terms is not None
    return pl.pallas_call(
        functools.partial(
            product_sum_kernel, group, planes, flip, close, len(ins), len(outs), len(ahead) - extra, int(extra)
        ),
        out_shape=shapes,
        in_specs=[LOCAL] * (2 + len(ins)) + places,
        out_specs=[LOCAL] * len(shapes),
        scratch_shapes=scratch,
        compiler_params=talk(collective_id, 60),
        cost_estimate=cost(2 * a.shape[0] * a.shape[1] * width, 100 * a.shape[0] * width),
    )(a, w, *ins, *ahead)


def attend_kernel(
    block, group, x_ref, w_ref, params_ref, qkv_bias_ref, live_ref, source, _,
    normed_ref, qkv_ref, mixed_ref, total_ref, target, bias_ref, *refs,
):
    seg_rows, heads = x_ref.shape[0] // 2, mixed_ref.shape[1] // HEAD
    gather = PlaneGather(group, halves(source, False), halves(target, False), *refs)
    greet(gather.core, gather.inner, group)
    gather.start()

    @pl.loop(0, 2 * seg_rows // block)
    def _(at):
        rows = pl.ds(pl.multiple_of(at * block, block), block)
        normed = unit_norm(x_ref[rows, :].astype(f32))[0] * line(params_ref, GAIN_ONE)
        normed = (normed + line(params_ref, SHIFT_ONE)).astype(bf16)
        normed_ref[rows, :] = normed
        qkv_ref[rows, :] = (dot(normed, w_ref[...], 1, 0) + qkv_bias_ref[...]).astype(bf16)

    for seg in range(2):
        attend_segment(block, heads, seg_rows, seg, qkv_ref, live_ref, mixed_ref, total_ref, bias_ref)
        if seg == 0:
            gather.relay()
    gather.finish()


def attend(x, w, params, qkv_bias, live, array, gathered, group, collective_id):
    rows, width = x.shape
    cols = w.shape[1] // 3
    block = 256
    local = pl.BlockSpec(memory_space=pltpu.VMEM)
    anywhere = pl.BlockSpec(memory_space=pl.ANY)
    results = pl.pallas_call(
        functools.partial(attend_kernel, block, group),
        out_shape=[
            jax.ShapeDtypeStruct((rows, width), bf16),
            jax.ShapeDtypeStruct((rows, 3 * cols), bf16),
            jax.ShapeDtypeStruct((rows, cols), bf16),
            jax.ShapeDtypeStruct((2, 8, rows // 2), f32),
            jax.ShapeDtypeStruct((2 * group, *array.shape), array.dtype),
        ],
        in_specs=[local] * 5 + [anywhere] * 2,
        out_specs=[local] * 4 + [anywhere],
        input_output_aliases={6: 4},
        scratch_shapes=[pltpu.VMEM((block, rows // 2), f32), *PlaneGather.scratch(group)],
        compiler_params=pltpu.CompilerParams(
            collective_id=collective_id, has_side_effects=True, vmem_limit_bytes=60 * 2**20
        ),
        cost_estimate=pl.CostEstimate(
            flops=rows * rows * cols + 6 * rows * width * cols, bytes_accessed=10**8, transcendentals=0
        ),
    )(x, w, params, qkv_bias[None], live.astype(f32)[:, None], array, gathered)
    return [*results[:4], results[4].reshape(-1, array.shape[-1])]


def attend_back_kernel(
    block, group, qkv_ref, first_ref, second_ref, live_ref, total_ref, a, w, normed, *refs
):
    out_ref, own_ref, column_ref, grad_w, *refs = refs
    a_ref, w_ref, load_sems, bias_ref, sums_ref, *refs = refs
    grad_ref = first_ref, second_ref
    seg_rows, heads = qkv_ref.shape[0] // 2, first_ref.shape[1] // HEAD
    cols = heads * HEAD
    loads = [
        pltpu.make_async_copy(whole, held, load_sems.at[i])
        for i, (whole, held) in enumerate(((a, a_ref), (w, w_ref)))
    ]
    for load in loads:
        load.start()
    strips = Strips(normed, out_ref, grad_w, *refs[:3])
    strips.start()
    total = PlaneSum(group, row_product(group, own_ref.shape[0], False, a_ref, w_ref), own_ref, *refs[3:])
    greet(total.core, total.inner, group)
    column_ref[...] = jnp.zeros_like(column_ref)
    blocks = seg_rows // block
    parts, relayed = total.order(group), False
    for seg in range(2):
        sums_ref[...] = jnp.zeros_like(sums_ref)
        for at in range(blocks):
            turn = seg * blocks + at
            if turn == 0:
                for load in loads:
                    load.wait()
            for part in parts[:2]:
                total.part(part)
            if not parts and not relayed and turn >= group + 1:
                total.relay()
                relayed = True
            parts = parts[2:]
            attend_back_rows(
                block, heads, seg_rows, seg, at, qkv_ref, grad_ref, live_ref, total_ref, out_ref, bias_ref, sums_ref
            )
        low = sums_ref[...].astype(bf16)
        out_ref[pl.ds(seg * seg_rows, seg_rows), cols:] = low
        column_ref[:, cols:] += jnp.sum(low.astype(f32), axis=0, keepdims=True)
    column_ref[:, :cols] = jnp.sum(out_ref[:, :cols].astype(f32), axis=0, keepdims=True)
    strips.run()
    total.finish()
    strips.finish()


def attend_back(qkv, grads, live, totals, a, w, normed, group, collective_id):
    rows, cols = qkv.shape[0], qkv.shape[1] // 3
    here, width = rows // (2 * group), w.shape[1]
    block = here
    shapes = [
        jax.ShapeDtypeStruct((rows, 3 * cols), bf16),
        jax.ShapeDtypeStruct((here, width), f32),
        jax.ShapeDtypeStruct((1, 3 * cols), f32),
        jax.ShapeDtypeStruct((width, 3 * cols), bf16),
    ]
    scratch = [
        pltpu.VMEM(a.shape, bf16),
        pltpu.VMEM(w.shape, bf16),
        pltpu.SemaphoreType.DMA((2,)),
        pltpu.VMEM((rows // 2, block), f32),
        pltpu.VMEM((rows // 2, 2 * cols), f32),
        *Strips.scratch(rows, 3 * cols, 1024 // group),
        *PlaneSum.scratch(group, here, width),
    ]
    return pl.pallas_call(
        functools.partial(attend_back_kernel, block, group),
        out_shape=shapes,
        in_specs=[LOCAL] * 5 + [ANY] * 3,
        out_specs=[LOCAL] * 3 + [ANY],
        scratch_shapes=scratch,
        compiler_params=talk(collective_id, 63),
        cost_estimate=cost(2 * rows * rows * cols + 2 * rows * a.shape[1] * width, 10**8),
    )(qkv, *grads, live.astype(f32).reshape(rows, 1), totals, a, w, normed)


def gelu_parts(value):
    cdf = 0.5 * (1.0 + lax.erf(value * 0.7071067811865476))
    return value * cdf, cdf + value * jnp.exp(-0.5 * value * value) * 0.3989422804014327


def gather_up_kernel(group, source, up_ref, bias_ref, all_out, act_ref, slope_ref, all_ref, out_sems, *refs):
    gather = PlaneGather(group, source, all_ref, *refs)
    greet(gather.core, gather.inner, group)
    here = source.shape[0]
    tile = math.gcd(1024, up_ref.shape[1])

    def out_copy(core, inner):
        at = core * group + inner
        return pltpu.make_async_copy(all_ref.at[at], all_out.at[at], out_sems.at[at])

    def use(core, inner):
        at = core * group + inner
        out_copy(core, inner).start()
        rows = pl.ds(pl.multiple_of(at * here, here), here)

        @pl.loop(0, up_ref.shape[1] // tile)
        def _(i):
            columns = pl.ds(pl.multiple_of(i * tile, tile), tile)
            value, slope = gelu_parts(dot(all_ref[at], up_ref[:, columns], 1, 0) + bias_ref[:, columns])
            act_ref[rows, columns] = value.astype(bf16)
            slope_ref[rows, columns] = slope.astype(bf16)

    gather.run(use)
    for at in range(2 * group):
        pltpu.make_async_copy(all_ref.at[at], all_out.at[at], out_sems.at[at]).wait()


def gather_up(array, up, bias, group, collective_id):
    here, width = array.shape
    rows, wide = 2 * group * here, up.shape[1]
    local = pl.BlockSpec(memory_space=pltpu.VMEM)
    anywhere = pl.BlockSpec(memory_space=pl.ANY)
    all_rows, act, slope = pl.pallas_call(
        functools.partial(gather_up_kernel, group),
        out_shape=[
            jax.ShapeDtypeStruct((2 * group, here, width), bf16),
            jax.ShapeDtypeStruct((rows, wide), bf16),
            jax.ShapeDtypeStruct((rows, wide), bf16),
        ],
        in_specs=[anywhere, local, local],
        out_specs=[anywhere, local, local],
        scratch_shapes=[
            pltpu.VMEM((2 * group, here, width), bf16),
            pltpu.SemaphoreType.DMA((2 * group,)),
            *PlaneGather.scratch(group),
        ],
        compiler_params=pltpu.CompilerParams(
            collective_id=collective_id, has_side_effects=True, vmem_limit_bytes=60 * 2**20
        ),
        cost_estimate=pl.CostEstimate(
            flops=2 * rows * width * wide, bytes_accessed=50 * rows * width, transcendentals=0
        ),
    )(array, up, bias[None])
    return all_rows.reshape(rows, width), act, slope


def gather_mixed_kernel(group, last, array, w_ref, mixed_ref, *refs):
    sum_in, refs = (refs[0], refs[1:]) if last else (None, refs)
    grad_mixed_ref, grad_w_ref, all_ref, sum_ref = refs[:4]
    source = halves(array, not last)
    gather = PlaneGather(group, source, all_ref, *refs[4:])
    greet(gather.core, gather.inner, group)
    rows_here = source.shape[0]
    sum_ref[...] = sum_in[...] if last else jnp.zeros_like(sum_ref)

    def use(core, inner):
        at = core * group + inner
        rows = pl.ds(pl.multiple_of(at * rows_here, rows_here), rows_here)
        grad_mixed_ref[rows, :] = dot(all_ref[at], w_ref[...], 1, 1).astype(bf16)
        start = at * 2 * rows_here + last * rows_here
        mixed = mixed_ref[pl.ds(pl.multiple_of(start, rows_here), rows_here), :]
        sum_ref[...] += dot(mixed, all_ref[at], 0, 0)

    gather.run(use)
    grad_w_ref[...] = sum_ref[...].astype(grad_w_ref.dtype)


def gather_mixed(array, w, mixed, group, collective_id, before=None):
    here, width = array.shape
    rows, cols = mixed.shape
    extra = [] if before is None else [before]
    return pl.pallas_call(
        functools.partial(gather_mixed_kernel, group, len(extra)),
        out_shape=[
            jax.ShapeDtypeStruct((rows // 2, cols), bf16),
            jax.ShapeDtypeStruct((cols, width), bf16 if extra else f32),
        ],
        in_specs=[ANY] + [LOCAL] * (2 + len(extra)),
        out_specs=[LOCAL] * 2,
        scratch_shapes=[
            pltpu.VMEM((2 * group, here // 2, width), bf16),
            pltpu.VMEM((cols, width), f32),
            *PlaneGather.scratch(group),
        ],
        compiler_params=talk(collective_id, 60),
        cost_estimate=cost(2 * rows * width * cols, 25 * rows * width),
    )(array, w, mixed, *extra)


class Strips:

    @staticmethod
    def scratch(rows, right, depth):
        return [
            pltpu.VMEM((2, rows, depth), bf16),
            pltpu.VMEM((2, depth, right), bf16),
            pltpu.SemaphoreType.DMA((2, 2)),
        ]

    def __init__(self, whole, right_ref, target, held, done, sems):
        self.whole, self.right_ref, self.target = whole, right_ref, target
        self.held, self.done, self.sems = held, done, sems
        self.depth = held.shape[2]
        self.count = whole.shape[1] // self.depth

    def strip(self, at):
        return pl.ds(pl.multiple_of(at * self.depth, self.depth), self.depth)

    def load(self, at):
        slot = lax.rem(at, 2)
        return pltpu.make_async_copy(self.whole.at[:, self.strip(at)], self.held.at[slot], self.sems.at[0, slot])

    def store(self, at):
        slot = lax.rem(at, 2)
        return pltpu.make_async_copy(self.done.at[slot], self.target.at[self.strip(at)], self.sems.at[1, slot])

    def start(self):
        for at in range(2):
            self.load(at).start()

    def run(self):
        @pl.loop(0, self.count)
        def _(at):
            slot = lax.rem(at, 2)
            self.load(at).wait()

            @pl.when(at >= 2)
            def _():
                self.store(at - 2).wait()

            self.done[slot] = dot(self.held[slot], self.right_ref[...], 0, 0).astype(bf16)
            self.store(at).start()

            @pl.when(at + 2 < self.count)
            def _():
                self.load(at + 2).start()

    def finish(self):
        for at in range(self.count - 2, self.count):
            self.store(at).wait()


def back_sum_kernel(
    group, out_live, slope, down, up, second, attended_ref, out_ref, params_ref, bias_ref,
    after_ref, low_ref, sums_ref, grad_up, grad_pre_ref, own_ref, live_v, slope_v, down_v, up_v, sems, *refs,
):
    here = own_ref.shape[0]
    wide = down.shape[0]
    tile = math.gcd(1024, wide)
    order = PlaneSum.order(group, True)

    def rows_of(core, inner):
        return pl.ds(pl.multiple_of((core * group + inner) * here, here), here)

    slots = live_v.shape[0]

    def loads(turn):
        core = total.core if order[turn] % 2 else 1 - total.core
        rows, slot = rows_of(core, total.targets[order[turn] // 2]), turn % slots
        return (
            pltpu.make_async_copy(out_live.at[rows, :], live_v.at[slot], sems.at[0, slot]),
            pltpu.make_async_copy(slope.at[rows, :], slope_v.at[slot], sems.at[1, slot]),
        )

    def start_loads(turn):
        if turn < 2 * group:
            for load in loads(turn):
                load.start()

    down_load = pltpu.make_async_copy(down, down_v, sems.at[0, slots])
    up_load = pltpu.make_async_copy(up, up_v, sems.at[1, slots])

    def prepare(core, inner, at):
        turn = order.index(at)
        slot = turn % slots
        for load in loads(turn):
            load.wait()
        if turn == 0:
            down_load.wait()
        else:
            start_loads(turn + slots - 1)
        rows = rows_of(core, inner)

        @pl.loop(0, wide // tile)
        def _(i):
            columns = pl.ds(pl.multiple_of(i * tile, tile), tile)
            value = dot(live_v[slot], down_v[columns, :], 1, 1) * slope_v[slot, :, columns].astype(f32)
            value = value.astype(bf16)
            grad_pre_ref[rows, columns] = value
            bias_ref[:, columns] += jnp.sum(value.astype(f32), axis=0, keepdims=True)

        if turn == 0:
            up_load.wait()

    strips = Strips(second, grad_pre_ref, grad_up, *refs[:3])
    total = PlaneSum(group, row_product(group, here, True, grad_pre_ref, up_v), own_ref, *refs[3:], prepare=prepare)
    down_load.start()
    for turn in range(slots):
        start_loads(turn)
        if turn == 0:
            up_load.start()
    bias_ref[...] = jnp.zeros_like(bias_ref)
    strips.start()
    greet(total.core, total.inner, group)
    total.run(True, strips.run)
    close_second(total.inner, own_ref, (attended_ref, out_ref, params_ref), (after_ref, low_ref, sums_ref))
    strips.finish()


def back_sum(out_live, slope, down, up, second, attended, out_own, params, group, collective_id):
    rows, width = out_live.shape
    here, wide = rows // (2 * group), down.shape[0]
    local = pl.BlockSpec(memory_space=pltpu.VMEM)
    anywhere = pl.BlockSpec(memory_space=pl.ANY)
    bias, grad_after, low, sums, grad_up = pl.pallas_call(
        functools.partial(back_sum_kernel, group),
        out_shape=[
            jax.ShapeDtypeStruct((1, wide), f32),
            jax.ShapeDtypeStruct((here, width), f32),
            jax.ShapeDtypeStruct((here, width), bf16),
            jax.ShapeDtypeStruct((8, width), f32),
            jax.ShapeDtypeStruct((width, wide), bf16),
        ],
        in_specs=[anywhere] * 5 + [local] * 3,
        out_specs=[local] * 4 + [anywhere],
        scratch_shapes=[
            pltpu.VMEM((rows, wide), bf16),
            pltpu.VMEM((here, width), f32),
            pltpu.VMEM((4, here, width), bf16),
            pltpu.VMEM((4, here, wide), bf16),
            pltpu.VMEM(down.shape, bf16),
            pltpu.VMEM(up.shape, bf16),
            pltpu.SemaphoreType.DMA((2, 5)),
            *Strips.scratch(rows, wide, 1024 // group),
            *PlaneSum.scratch(group, here, width),
        ],
        compiler_params=pltpu.CompilerParams(
            collective_id=collective_id, has_side_effects=True, vmem_limit_bytes=63 * 2**20
        ),
        cost_estimate=pl.CostEstimate(
            flops=4 * rows * width * wide, bytes_accessed=50 * rows * width, transcendentals=0
        ),
    )(out_live, slope, down, up, second, attended, out_own, params)
    return bias[0], grad_after, low, sums, grad_up


def closing_kernel(planes, group, unit, repeats, extra, terms, attn, *refs):
    source, refs = refs[:extra], refs[extra:]
    out_ref, weight_refs, line_ref, refs = refs[0], refs[1:4], refs[4 : 4 + extra], refs[4 + extra :]
    attn_all, from_plane, summed, from_z, plane_sems, z_sems = refs[:6]
    exchange = PlaneExchange(group, attn, attn_all, *refs[6:8])
    sums = [PlanesSum(planes, 1, *source, *line_ref, *refs[8:])] if extra else []
    team = 2 * group
    z_at, core_at, inner_at, mine = lax.axis_index("z"), exchange.core, exchange.inner, exchange.mine
    greet_all(core_at, inner_at, group, planes)
    for one in sums:
        one.start()
    copies = []
    for step in range(1, team):
        core, inner = other_device(core_at, inner_at, group, step)
        copy = send(
            terms.at[core * group + inner],
            from_plane.at[step],
            plane_sems.at[0, step],
            plane_sems.at[1, step],
            core,
            inner,
        )
        copy.start()
        copies.append(copy)
    exchange.start()
    summed[...] = terms[mine]
    for copy in copies:
        copy.wait_recv()
    for step in range(1, team):
        summed[...] += from_plane[step]
    more = []
    for step in range(1, planes):
        to = lax.rem(z_at + step, planes)
        copy = pltpu.make_async_remote_copy(
            src_ref=summed.at[to],
            dst_ref=from_z.at[step],
            send_sem=z_sems.at[0, step],
            recv_sem=z_sems.at[1, step],
            device_id={"z": to},
            device_id_type=MESH,
        )
        copy.start()
        more.append(copy)
    exchange.finish()
    cols = unit * repeats
    for i in range(3):
        place_columns(weight_refs[i], attn_all, i * cols, unit, repeats, team)
    out_ref[...] = summed[z_at]
    for step, copy in enumerate(more, 1):
        copy.wait_recv()
        out_ref[...] += from_z[step]
    for copy in copies + more:
        copy.wait_send()
    for one in sums:
        one.finish()


def closing(terms, attn, planes, group, unit, collective_id, source=None):
    team, _, lines, _ = terms.shape
    rows, cols = attn.shape[1], attn.shape[2] // 3
    weight = jax.ShapeDtypeStruct((rows, cols * team), bf16)
    extra = [] if source is None else [source]
    sums = [(one.shape[0] // planes, one.shape[1] // 2) for one in extra]
    return pl.pallas_call(
        functools.partial(closing_kernel, planes, group, unit, cols // unit, len(extra)),
        out_shape=[
            jax.ShapeDtypeStruct((lines, 128), f32),
            weight,
            weight,
            weight,
            *[jax.ShapeDtypeStruct(shape, f32) for shape in sums],
        ],
        in_specs=[LOCAL, ANY] + [LOCAL] * len(extra),
        out_specs=[LOCAL] * (4 + len(extra)),
        scratch_shapes=[
            pltpu.VMEM(attn.shape, bf16),
            pltpu.VMEM((team, planes, lines, 128), f32),
            pltpu.VMEM((planes, lines, 128), f32),
            pltpu.VMEM((planes, lines, 128), f32),
            pltpu.SemaphoreType.DMA((2, team)),
            pltpu.SemaphoreType.DMA((2, planes)),
            *PlaneExchange.scratch(group),
            *[one for shape in sums for one in PlanesSum.scratch(planes, *shape)],
        ],
        compiler_params=talk(collective_id, 40),
        cost_estimate=cost(0, 10**8),
    )(terms, attn, *extra)


def body(
    layer_input,
    first_gain,
    first_shift,
    query_weight,
    key_weight,
    value_weight,
    output_weight,
    query_bias,
    value_bias,
    output_bias,
    second_gain,
    second_shift,
    up_weight,
    up_bias,
    down_weight,
    down_bias,
    segment_counts,
    out_grad,
):
    here, width = layer_input.shape
    wide = up_weight.shape[1]
    planes = lax.axis_size("z")
    group = lax.axis_size("fsdp")
    team = 2 * group
    z_at, core_at, inner_at = (lax.axis_index(name) for name in ALL)
    plane_at = core_at * group + inner_at
    seg_rows = here * group
    own_rows = query_weight.shape[0]
    own_wide = down_weight.shape[0]
    cols = width // team
    heads_here = cols // HEAD
    whole_heads = own_rows % HEAD == 0

    def to_columns(weight, unit):
        cut = weight.reshape(weight.shape[0], planes, team, unit)
        return cut.transpose(2, 0, 1, 3).reshape(team, weight.shape[0], planes * unit)

    def head_columns(weight):
        if whole_heads:
            return to_columns(weight, own_rows)
        return weight.reshape(own_rows, team, cols).transpose(1, 0, 2)

    attn_blocks = jnp.concatenate([head_columns(w) for w in (query_weight, key_weight, value_weight)], axis=2)
    out_here = z_gather(output_weight) if whole_heads else lax.all_gather(output_weight, ALL, axis=0, tiled=True)
    attn_cols, up_cols = plane_exchange(attn_blocks, up_weight, own_wide, planes, group, 0)
    attn_cols = attn_cols.reshape(team * own_rows, 3 * cols)
    up_cols = up_cols.reshape(team * own_rows, wide // team)
    attn_full = z_gather(after(attn_cols, out_here))
    small = jnp.concatenate(
        [first_gain, first_shift, query_bias, value_bias, output_bias, second_gain, second_shift, down_bias, up_bias]
    )
    length = small.shape[0]
    small = jnp.pad(small.astype(f32), (0, -length % 1024)).reshape(-1, 128)
    segment = 2 * z_at + jnp.arange(2, dtype=jnp.int32)
    place = segment % MAXSEG
    present = place < segment_counts[segment // MAXSEG]
    pos = jnp.arange(seg_rows, dtype=jnp.int32)
    live = present[:, None] & ((pos >= PRE)[None] | (place[:, None] >= PREV - pos[None] // SUMM))
    live_own = lax.dynamic_slice(live, (core_at, inner_at * here), (1, here))[0]
    out_own = jnp.where(live_own[:, None], out_grad, jnp.zeros_like(out_grad))
    all_rows, small_all, out_live = entry(after(layer_input, up_cols), small, out_own, planes, group, 1)
    all_rows = all_rows.reshape(-1, width)
    small_all = small_all.swapaxes(0, 1).reshape(planes * team, -1)
    params = small_all[:, : 8 * own_rows].reshape(planes * team, 8, own_rows).swapaxes(0, 1).reshape(8, width)
    bias_up = small_all[:, 8 * own_rows : length].reshape(planes, team, own_wide)[:, plane_at].reshape(wide // team)

    def own_columns(bias):
        if whole_heads:
            return bias.reshape(planes, team, own_rows)[:, plane_at].reshape(cols)
        return lax.dynamic_slice_in_dim(bias, plane_at * cols, cols)

    bias_q, bias_v = own_columns(params[BIAS_Q]), own_columns(params[BIAS_V])
    out_full = out_here if whole_heads else lax.dynamic_slice_in_dim(out_here, plane_at * cols, cols)
    up_full = z_gather(up_cols)
    down_full = z_gather(after(down_weight, up_cols))
    normed_low, qkv, mixed_low, totals, out_live = attend(
        all_rows,
        attn_full,
        params,
        jnp.concatenate([bias_q, jnp.zeros_like(bias_q), bias_v]),
        live,
        out_own,
        out_live,
        group,
        11,
    )
    out_live = out_live.reshape(-1, width)
    attended, second_own = product_sum(
        mixed_low,
        out_full,
        False,
        close_attention,
        [layer_input, params],
        [(here, f32), (here, bf16)],
        group,
        2,
    )
    second_low, activated, slope = gather_up(second_own, up_full, bias_up, group, 3)
    grad_down = dot(activated, out_live, 0, 0).astype(bf16)
    out_live = after(out_live, grad_down)
    grad_down = z_sum(grad_down)
    grad_up_bias, grad_after, after_low_own, second_sums, grad_up = back_sum(
        out_live, slope, down_full, up_full, second_low, attended, out_own, params, group, 5
    )
    first_mixed, first_output = gather_mixed(after_low_own, out_full, mixed_low, group, 6)
    grad_up = z_sum(after(grad_up, grad_down, first_mixed)).reshape(team, own_rows, wide // team)
    second_mixed, grad_output = gather_mixed(after_low_own, out_full, mixed_low, group, 7, first_output)
    grad_qkv, added, grad_bias, grad_attn = attend_back(
        qkv, (first_mixed, second_mixed), live, totals, activated, down_full, normed_low, group, 4
    )
    grad_bias = grad_bias[0]
    grad_attn = z_sum(after(grad_attn, grad_up)).reshape(team, own_rows, 3 * cols)
    input_grad, first_sums, grad_up, *summed = product_sum(
        grad_qkv,
        attn_full,
        True,
        close_first,
        [layer_input, params, grad_after],
        [(here, f32), (8, f32)],
        group,
        8,
        planes,
        grad_up,
        grad_output if whole_heads else None,
    )
    grad_down, added = after(grad_down, input_grad), after(added, input_grad)
    layer_output = (attended + added + params[BIAS_DOWN]).astype(bf16)
    own_pos = inner_at * here + jnp.arange(here, dtype=jnp.int32)
    input_grad = jnp.where((own_pos >= SUMM)[:, None], input_grad, 0.0)

    def spread_columns(bias):
        if whole_heads:
            full = jnp.zeros((planes, team, own_rows), f32)
            return lax.dynamic_update_slice(full, bias.reshape(planes, 1, own_rows), (0, plane_at, 0)).reshape(width)
        return lax.dynamic_update_slice(jnp.zeros((width,), f32), bias, (plane_at * cols,))

    sums = [
        first_sums[0],
        first_sums[1],
        spread_columns(grad_bias[:cols]),
        spread_columns(grad_bias[2 * cols :]),
        second_sums[2],
        second_sums[0],
        second_sums[1],
        second_sums[3],
    ]
    up_spread = jnp.zeros((planes, team, own_wide), f32)
    up_spread = lax.dynamic_update_slice(up_spread, grad_up_bias.reshape(planes, 1, own_wide), (0, plane_at, 0))
    packed = jnp.concatenate(
        [a.reshape(planes * team, own_rows) for a in sums] + [up_spread.reshape(planes * team, own_wide)], axis=1
    )
    packed = jnp.pad(packed, ((0, 0), (0, -length % 1024))).reshape(planes, team, -1, 128).swapaxes(0, 1)
    if not whole_heads:
        spread = jnp.zeros((width, width), bf16)
        spread = lax.dynamic_update_slice_in_dim(spread, grad_output, plane_at * cols, 0)
        last_sum = lax.psum_scatter(spread, ALL, scatter_dimension=0, tiled=True).astype(f32)
    packed, *grad_weights = closing(
        packed,
        grad_attn,
        planes,
        group,
        own_rows if whole_heads else cols,
        9,
        grad_output if whole_heads else None,
    )
    if whole_heads:
        last_sum = jnp.concatenate([*summed, grad_weights.pop()], axis=1)
    packed = packed.reshape(-1)
    small_grads = [packed[i * own_rows : (i + 1) * own_rows] for i in range(8)]
    return (
        layer_output,
        input_grad,
        small_grads[0],
        small_grads[1],
        *[weight.astype(f32) for weight in grad_weights],
        last_sum,
        small_grads[2],
        small_grads[3],
        small_grads[4],
        small_grads[5],
        small_grads[6],
        grad_up.astype(f32),
        packed[8 * own_rows : length],
        grad_down.astype(f32),
        small_grads[7],
    )


def solution(mesh):
    outer, inner = mesh.devices.shape
    fine = Mesh(mesh.devices.reshape(outer // 2, 2, inner), ALL)
    rows, vector = P(ALL, None), P(ALL)
    return jax.shard_map(
        body,
        mesh=fine,
        in_specs=(
            rows, vector, vector, rows, rows, rows, rows, vector, vector, vector, vector, vector,
            rows, vector, rows, vector, P(), rows,
        ),
        out_specs=(
            rows, rows, vector, vector, rows, rows, rows, rows, vector, vector, vector, vector, vector,
            rows, vector, rows, vector,
        ),
        check_vma=False,
    )
```
